32 devices in a mesh: section: 2 (over core), dp: 16 (over z, y, x).
Axes of the slice: x: 2, y: 2, z: 4, core: 2. Of those that a mesh axis runs over, the one named last changes fastest.
Arguments:
- bytes_in: bfloat16 [16, 1024, 768], P('dp', None, 'section'), may hold values from -6 to 6
- lengths: int32 [16], P('dp'), may hold values from 768 to 1024, as said below
- patch_index: int32 [16, 2, 96], P('dp'), may hold values from 0 to 1023, as said below
- patch_count: int32 [16, 2], P('dp'), may hold values from 1 to 96, as said below
- gain_l1: bfloat16 [768], P('dp'), may hold values from 0.099609375 to 1.8984375
- qkv_l: bfloat16 [768, 2304], P('dp'), may hold values from -0.21875 to 0.21875
- out_l: bfloat16 [768, 768], P('dp'), may hold values from -3.5 to 3.5
- gain_l2: bfloat16 [768], P('dp'), may hold values from 0.099609375 to 1.8984375
- up_l: bfloat16 [768, 3072], P('dp'), may hold values from -0.21875 to 0.21875
- down_l: bfloat16 [3072, 768], P('dp'), may hold values from -0.109375 to 0.109375
- patch_proj: bfloat16 [768, 1536], P('dp'), may hold values from -0.21875 to 0.21875
- gain_g1: bfloat16 [1536], P('dp'), may hold values from 0.099609375 to 1.8984375
- qkv_g: bfloat16 [1536, 4608], P('dp'), may hold values from -0.15625 to 0.15625
- out_g: bfloat16 [1536, 1536], P('dp'), may hold values from -1.25 to 1.25
- gain_g2: bfloat16 [1536], P('dp'), may hold values from 0.099609375 to 1.8984375
- up_g: bfloat16 [1536, 6144], P('dp'), may hold values from -0.15625 to 0.15625
- down_g: bfloat16 [6144, 1536], P('dp'), may hold values from -0.078125 to 0.078125
- out_grad: bfloat16 [16, 1024, 768], P('dp', None, 'section'), may hold values from -6 to 6
Outputs:
- hidden_out: bfloat16 [16, 1024, 768], P('dp', None, 'section')
- input_grad: bfloat16 [16, 1024, 768], P('dp', None, 'section')
- grad_gain_l1: float32 [768], P('dp')
- grad_qkv_l: float32 [768, 2304], P('dp')
- grad_out_l: float32 [768, 768], P('dp')
- grad_gain_l2: float32 [768], P('dp')
- grad_up_l: float32 [768, 3072], P('dp')
- grad_down_l: float32 [3072, 768], P('dp')
- grad_patch_proj: float32 [768, 1536], P('dp')
- grad_gain_g1: float32 [1536], P('dp')
- grad_qkv_g: float32 [1536, 4608], P('dp')
- grad_out_g: float32 [1536, 1536], P('dp')
- grad_gain_g2: float32 [1536], P('dp')
- grad_up_g: float32 [1536, 6144], P('dp')
- grad_down_g: float32 [6144, 1536], P('dp')
The draws below stay inside these ranges and needn't reach their ends.
Inputs may be any that keep to these rules, and one draw needn't show every extreme that they name: `lengths`: each sequence's length; some sequence has exactly 1024. `patch_count`: live patch slots of block m of a sequence; some block of some sequence fills all 96. `patch_index`: in row (s, m) the first patch_count[s, m] entries are increasing byte positions from m * 512 to (m + 1) * 512 - 1 and below the sequence's length, the first of them m * 512; the remaining entries equal m * 512.
All inputs are finite; a program needn't handle non-finite values.
Results may differ from the reference program's by a relative error of at most 0.024.
Values may be sent and summed in bfloat16 or wider, within the bound.
No kernel may reach another device: no remote copies, remote signals or barrier semaphores. Data moves between devices by JAX's collectives and lax.ppermute only.
A program may use at most 576 MiB of HBM per device.

```python
import jax
import jax.numpy as jnp
from jax import lax

D_L = 768
H_L = 12
FF_L = 3072
D_G = 1536
H_G = 24
FF_G = 6144
WINDOW = 1536
MB_TOK = 512
MICRO = 2
SEQ_LEN = 1024
CAP_MB = 96
BATCH = 16


def patch_layout(key):
    key_len, key_pick, key_count, key_fill, key_score, key_run = jax.random.split(key, 6)
    seq_index = jnp.arange(BATCH)
    lengths = jax.random.randint(key_len, (BATCH,), SEQ_LEN - MB_TOK // 2, SEQ_LEN + 1)
    longest = jax.random.randint(key_pick, (), 0, BATCH)
    lengths = jnp.where(seq_index == longest, SEQ_LEN, lengths)
    totals = jax.random.randint(key_count, (BATCH, MICRO), CAP_MB // 3, CAP_MB + 1)
    fullest = jax.random.randint(key_fill, (), 0, BATCH * MICRO)
    flat_index = jnp.arange(BATCH * MICRO).reshape(BATCH, MICRO)
    totals = jnp.where(flat_index == fullest, CAP_MB, totals)
    offset = jnp.arange(MB_TOK)[None, None, :]
    block_start = (jnp.arange(MICRO) * MB_TOK)[None, :, None]
    position = block_start + offset
    raw_score = jax.random.randint(key_score, (BATCH, MICRO, MB_TOK), 0, 4096)
    run_start = jax.random.randint(key_run, (BATCH, 1, 1), 0, SEQ_LEN - SEQ_LEN // 4)
    in_run = (position >= run_start) & (position < run_start + SEQ_LEN // 4)
    raw_score = jnp.where(in_run, raw_score, raw_score + 4096)
    raw_score = jnp.where(position == SEQ_LEN - 1, 16382, raw_score)
    raw_score = jnp.where(offset == 0, 16383, raw_score)
    priority = raw_score * MB_TOK + offset
    priority = jnp.where(position < lengths[:, None, None], priority, -1 - offset)
    chosen = lax.top_k(priority, CAP_MB)[1]
    slot_ids = jnp.arange(CAP_MB)[None, None, :]
    chosen = jnp.where(slot_ids < totals[..., None], chosen, MB_TOK + slot_ids)
    chosen = jnp.sort(chosen, axis=-1)
    chosen = jnp.where(slot_ids < totals[..., None], chosen, 0) + block_start
    return (lengths.astype(jnp.int32), chosen.astype(jnp.int32), totals.astype(jnp.int32))


def draw_lengths(key, part):
    layout = patch_layout(key)
    return layout[0]


def draw_patch_index(key, part):
    layout = patch_layout(key)
    return layout[1]


def draw_patch_count(key, part):
    layout = patch_layout(key)
    return layout[2]


def shard_levels(stream_key, extent, cuts, low, top_value):
    loudness, own = 1.0, jax.random.fold_in(stream_key, 6)
    for dim, blocks in cuts:
        steps = jnp.exp(jax.random.uniform(jax.random.fold_in(own, dim), (blocks,), jnp.float32, low / len(cuts), top_value / len(cuts)))
        loudness = loudness * jnp.repeat(steps, extent[dim] // blocks).reshape([-1 if axis == dim else 1 for axis in range(len(extent))])
    return loudness


def bell_draw(own_key, shape, width, most, shards=(), held_as=jnp.bfloat16):
    drawn = width * jax.random.normal(own_key, shape, jnp.float32)
    if shards:
        drawn = drawn * shard_levels(own_key, shape, shards, -0.22, 0.18)
    return jnp.clip(drawn, -most, most).astype(held_as)


def setup_inputs(seed: int = 0) -> dict:
    keys = jax.random.split(jax.random.key(seed), 19)
    return {
        "bytes_in": bell_draw(keys[0], (BATCH, SEQ_LEN, D_L), 1.0, 6.0, ((0, 16), (2, 2))),
        "lengths": draw_lengths(jax.random.fold_in(keys[18], 71), 0),
        "patch_index": draw_patch_index(jax.random.fold_in(keys[18], 71), 0),
        "patch_count": draw_patch_count(jax.random.fold_in(keys[18], 71), 0),
        "gain_l1": jnp.clip(1.0 + 0.18 * jax.random.normal(keys[4], (D_L,), jnp.float32), 0.099609375, 1.8984375).astype(jnp.bfloat16),
        "qkv_l": bell_draw(keys[5], (D_L, 3 * D_L), D_L ** -0.5, 0.21875, ((0, 16),)),
        "out_l": bell_draw(keys[6], (D_L, D_L), (max(D_L // 256, 1)) ** -0.5, 3.5, ((0, 16),)),
        "gain_l2": jnp.clip(1.0 + 0.18 * jax.random.normal(keys[7], (D_L,), jnp.float32), 0.099609375, 1.8984375).astype(jnp.bfloat16),
        "up_l": bell_draw(keys[8], (D_L, FF_L), D_L ** -0.5, 0.21875, ((0, 16),)),
        "down_l": bell_draw(keys[9], (FF_L, D_L), FF_L ** -0.5, 0.109375, ((0, 16),)),
        "patch_proj": bell_draw(keys[10], (D_L, D_G), D_L ** -0.5, 0.21875, ((0, 16),)),
        "gain_g1": jnp.clip(1.0 + 0.18 * jax.random.normal(keys[11], (D_G,), jnp.float32), 0.099609375, 1.8984375).astype(jnp.bfloat16),
        "qkv_g": bell_draw(keys[12], (D_G, 3 * D_G), D_G ** -0.5, 0.15625, ((0, 16),)),
        "out_g": bell_draw(keys[13], (D_G, D_G), (max(D_G // 64, 1)) ** -0.5, 1.25, ((0, 16),)),
        "gain_g2": jnp.clip(1.0 + 0.18 * jax.random.normal(keys[14], (D_G,), jnp.float32), 0.099609375, 1.8984375).astype(jnp.bfloat16),
        "up_g": bell_draw(keys[15], (D_G, FF_G), D_G ** -0.5, 0.15625, ((0, 16),)),
        "down_g": bell_draw(keys[16], (FF_G, D_G), FF_G ** -0.5, 0.078125, ((0, 16),)),
        "out_grad": bell_draw(keys[17], (BATCH, SEQ_LEN, D_L), 1.0, 6.0, ((0, 16), (2, 2))),
    }


EPSILON = 1e-06

@jax.custom_vjp
def low(v):
    return lax.optimization_barrier(v.astype(jnp.bfloat16)).astype(jnp.float32)

@jax.custom_vjp
def low_back(v):
    return v

def low_keep(v):
    return (low(v), None)

def low_pass(kept, grad):
    return (grad,)

def back_keep(v):
    return (v, None)

def back_low(kept, grad):
    return (low(grad),)
low.defvjp(low_keep, low_pass)
low_back.defvjp(back_keep, back_low)

def norm_scale(values, gain):
    return values * lax.rsqrt(lax.optimization_barrier(jnp.mean(values * values, axis=-1, keepdims=True)) + EPSILON) * gain

def layer_block(inputs, weights, allowed, head_count):
    gain_one, qkv_weight, out_weight, gain_two, up_weight, down_weight = weights
    rows_total, model_width = inputs.shape
    head_dim = model_width // head_count
    normed = low(norm_scale(inputs, gain_one))
    projected = low(low_back(jnp.dot(normed, qkv_weight, precision=lax.Precision.HIGHEST)))
    queries = projected[:, :model_width].reshape(rows_total, head_count, head_dim)
    key_heads = projected[:, model_width:2 * model_width].reshape(rows_total, head_count, head_dim)
    value_heads = projected[:, 2 * model_width:].reshape(rows_total, head_count, head_dim)
    scores = low_back(jnp.einsum('qhd,khd->hqk', queries, key_heads, precision=lax.Precision.HIGHEST) * head_dim ** (-0.5))
    scores = jnp.where(allowed[None], scores, -1e+30)
    attention = low(jax.nn.softmax(scores, axis=-1))
    mixture = jnp.einsum('hqk,khd->qhd', attention, value_heads, precision=lax.Precision.HIGHEST).reshape(rows_total, model_width)
    mixture = low(low_back(mixture))
    hidden = inputs + low_back(jnp.dot(mixture, out_weight, precision=lax.Precision.HIGHEST))
    upward = low_back(jnp.dot(low(norm_scale(hidden, gain_two)), up_weight, precision=lax.Precision.HIGHEST))
    activated = low(jax.nn.gelu(upward))
    return hidden + low_back(jnp.dot(activated, down_weight, precision=lax.Precision.HIGHEST))

def sequence(inputs, length, positions, live_totals, params):
    local_weights = params[0:6]
    proj_weight = params[6]
    global_weights = params[7:13]
    token_pos = jnp.arange(SEQ_LEN, dtype=jnp.int32)
    query_col = token_pos[:, None]
    key_row = token_pos[None, :]
    allowed_local = (key_row <= query_col) & (query_col - key_row < WINDOW) & ((key_row < length) | (key_row == query_col))
    local_out = layer_block(inputs, local_weights, allowed_local, H_L)
    slot_rows = positions.reshape(MICRO * CAP_MB).astype(jnp.int32)
    live = (jnp.arange(CAP_MB, dtype=jnp.int32)[None, :] < live_totals[:, None]).reshape(MICRO * CAP_MB)
    boundary = low(local_out)[slot_rows]
    start_rows = low_back(jnp.dot(boundary, proj_weight, precision=lax.Precision.HIGHEST))
    slot_pos = jnp.arange(MICRO * CAP_MB, dtype=jnp.int32)
    slot_col = slot_pos[:, None]
    slot_row = slot_pos[None, :]
    allowed_global = (slot_row <= slot_col) & (live[None, :] | (slot_row == slot_col))
    global_out = layer_block(start_rows, global_weights, allowed_global, H_G)
    returned = jnp.where(live[:, None], global_out[:, :D_L], jnp.zeros((), jnp.float32))
    return local_out.at[slot_rows].add(returned)

def reference(bytes_in, lengths, patch_index, patch_count, gain_l1, qkv_l, out_l, gain_l2, up_l, down_l, patch_proj, gain_g1, qkv_g, out_g, gain_g2, up_g, down_g, out_grad):
    params = tuple((weight.astype(jnp.float32) for weight in (gain_l1, qkv_l, out_l, gain_l2, up_l, down_l, patch_proj, gain_g1, qkv_g, out_g, gain_g2, up_g, down_g)))

    def forward(inputs, weights):

        def one_sequence(carried, item_set):
            row_inputs, length, positions, live_totals = item_set
            return (carried, jax.checkpoint(sequence)(row_inputs, length, positions, live_totals, weights))
        unused, outputs = lax.scan(one_sequence, jnp.zeros((), jnp.float32), (inputs, lengths, patch_index, patch_count))
        return outputs
    hidden_out, pull_back = jax.vjp(forward, bytes_in.astype(jnp.float32), params)
    input_grad, weight_grads = pull_back(out_grad.astype(jnp.float32))
    return (hidden_out.astype(jnp.bfloat16), input_grad.astype(jnp.bfloat16), weight_grads[0], weight_grads[1], weight_grads[2], weight_grads[3], weight_grads[4], weight_grads[5], weight_grads[6], weight_grads[7], weight_grads[8], weight_grads[9], weight_grads[10], weight_grads[11], weight_grads[12])
```

```python
import functools

import jax
import jax.numpy as jnp
import numpy as np
from jax import lax
from jax.experimental import pallas as pl
from jax.experimental.pallas import tpu as pltpu
from jax.sharding import PartitionSpec as P

H_L = 12
H_G = 24
WINDOW = 1536
EPSILON = 1e-06
LANES = 128
NEG = -1e30
VMEM_LIMIT = 48 * 1024 * 1024
F32 = jnp.float32
BF16 = jnp.bfloat16


def mm(left, right):
    return jnp.dot(left, right, preferred_element_type=F32)


def mm_nt(left, right):
    return lax.dot_general(left, right, (((1,), (1,)), ((), ())), preferred_element_type=F32)


def mm_tn(left, right):
    return lax.dot_general(left, right, (((0,), (0,)), ((), ())), preferred_element_type=F32)


def row_scale(values):
    return lax.rsqrt(jnp.mean(values * values, axis=-1, keepdims=True) + EPSILON)


def norm_backward(grad_normed, values, scale, gain):
    grad_gain = jnp.sum(grad_normed * values * scale, axis=0)
    pulled = grad_normed * gain
    inner = jnp.mean(pulled * values, axis=-1, keepdims=True)
    return scale * pulled - values * (scale * scale * scale * inner), grad_gain


def query_block(rows):
    return 256 if rows % 256 == 0 else rows


def masked_scores(keys, query, bias, start, block, window):
    pos_k = lax.broadcasted_iota(jnp.int32, (block, block), 0)
    pos_q = lax.broadcasted_iota(jnp.int32, (block, block), 1)
    parts = []
    if start:
        before = mm_nt(keys[:start], query) + bias[:start]
        if window is not None:
            far = lax.broadcasted_iota(jnp.int32, (start, block), 0)
            own = lax.broadcasted_iota(jnp.int32, (start, block), 1) + start
            before = jnp.where(own - far < window, before, NEG)
        parts.append(before)
    diagonal = mm_nt(keys[start : start + block], query)
    diagonal = jnp.where(
        pos_k == pos_q,
        diagonal,
        jnp.where(pos_k < pos_q, diagonal + bias[start : start + block], NEG),
    )
    parts.append(diagonal)
    return parts


def attention_forward_kernel(rows, head_dim, window, q_ref, k_ref, v_ref, bias_ref, o_ref, lse_ref):
    block = query_block(rows)
    lane = lax.broadcasted_iota(jnp.int32, (block, LANES), 1)
    score_scale = head_dim ** (-0.5)
    for index in range(rows // block):
        start = index * block
        queries = q_ref[start : start + block, :] * score_scale
        out = jnp.zeros((block, LANES), F32)
        for head in range(LANES // head_dim):
            mine = (lane >= head * head_dim) & (lane < (head + 1) * head_dim)
            query = jnp.where(mine, queries, jnp.zeros_like(queries)).astype(BF16)
            parts = masked_scores(k_ref, query, bias_ref, start, block, window)
            top = functools.reduce(jnp.maximum, [jnp.max(p, axis=0, keepdims=True) for p in parts])
            parts = [jnp.exp(p - top) for p in parts]
            total = functools.reduce(jnp.add, [jnp.sum(p, axis=0, keepdims=True) for p in parts])
            inverse = 1.0 / total
            mixed = jnp.zeros((block, LANES), F32)
            low = 0
            for part in parts:
                high = low + part.shape[0]
                mixed += mm_tn((part * inverse).astype(BF16), v_ref[low:high, :])
                low = high
            out = jnp.where(mine, mixed, out)
            lse_ref[0, head : head + 1, start : start + block] = top + jnp.log(total)
        o_ref[start : start + block, :] = out.astype(BF16)


def attention_backward_kernel(
    rows, head_dim, window, q_ref, k_ref, v_ref, bias_ref, lse_ref, do_ref, dq_ref, dk_ref, dv_ref, dk_acc, dv_acc
):
    block = query_block(rows)
    lane = lax.broadcasted_iota(jnp.int32, (block, LANES), 1)
    score_scale = head_dim ** (-0.5)
    dk_acc[...] = jnp.zeros((rows, LANES), F32)
    dv_acc[...] = jnp.zeros((rows, LANES), F32)
    for index in range(rows // block):
        start = index * block
        queries = q_ref[start : start + block, :] * score_scale
        grads = do_ref[start : start + block, :]
        dq = jnp.zeros((block, LANES), F32)
        for head in range(LANES // head_dim):
            mine = (lane >= head * head_dim) & (lane < (head + 1) * head_dim)
            query = jnp.where(mine, queries, jnp.zeros_like(queries)).astype(BF16)
            grad = jnp.where(mine, grads, jnp.zeros_like(grads))
            lse = lse_ref[0, head : head + 1, start : start + block]
            parts = masked_scores(k_ref, query, bias_ref, start, block, window)
            parts = [jnp.exp(p - lse) for p in parts]
            grad_parts = []
            low = 0
            for part in parts:
                high = low + part.shape[0]
                grad_parts.append(mm_nt(v_ref[low:high, :], grad))
                low = high
            delta = functools.reduce(
                jnp.add,
                [jnp.sum(p * g, axis=0, keepdims=True) for p, g in zip(parts, grad_parts)],
            )
            mixed = jnp.zeros((block, LANES), F32)
            low = 0
            for part, grad_part in zip(parts, grad_parts):
                high = low + part.shape[0]
                grad_score = (part * (grad_part - delta)).astype(BF16)
                dv_acc[low:high, :] += mm(part.astype(BF16), grad)
                dk_acc[low:high, :] += mm(grad_score, query)
                mixed += mm_tn(grad_score, k_ref[low:high, :])
                low = high
            dq = jnp.where(mine, mixed, dq)
        dq_ref[start : start + block, :] = (dq * score_scale).astype(BF16)
    dk_ref[...] = dk_acc[...].astype(BF16)
    dv_ref[...] = dv_acc[...].astype(BF16)


def attention_specs(rows, width):
    pairs = width // LANES
    wide = lambda part: pl.BlockSpec((rows, LANES), lambda i, part=part: (0, part * pairs + i))
    bias = pl.BlockSpec((rows, 1), lambda i: (0, 0))
    return pairs, wide, bias


def attention_forward(projected, bias, head_dim):
    rows, width = projected.shape[0], projected.shape[1] // 3
    pairs, wide, bias_spec = attention_specs(rows, width)
    per = LANES // head_dim
    window = WINDOW if rows > WINDOW else None
    return pl.pallas_call(
        functools.partial(attention_forward_kernel, rows, head_dim, window),
        grid=(pairs,),
        in_specs=[wide(0), wide(1), wide(2), bias_spec],
        out_specs=[wide(0), pl.BlockSpec((1, per, rows), lambda i: (i, 0, 0))],
        out_shape=[
            jax.ShapeDtypeStruct((rows, width), BF16),
            jax.ShapeDtypeStruct((pairs, per, rows), F32),
        ],
        compiler_params=pltpu.CompilerParams(vmem_limit_bytes=VMEM_LIMIT),
        cost_estimate=pl.CostEstimate(
            flops=8 * rows * rows * width,
            bytes_accessed=8 * rows * width,
            transcendentals=rows * rows * width // head_dim,
        ),
    )(projected, projected, projected, bias)


def attention_backward(projected, bias, lse, grad_mixture, head_dim):
    rows, width = grad_mixture.shape
    pairs, wide, bias_spec = attention_specs(rows, width)
    per = LANES // head_dim
    window = WINDOW if rows > WINDOW else None
    shape = jax.ShapeDtypeStruct((rows, width), BF16)
    grads = pl.pallas_call(
        functools.partial(attention_backward_kernel, rows, head_dim, window),
        grid=(pairs,),
        in_specs=[
            wide(0),
            wide(1),
            wide(2),
            bias_spec,
            pl.BlockSpec((1, per, rows), lambda i: (i, 0, 0)),
            wide(0),
        ],
        out_specs=[wide(0), wide(0), wide(0)],
        out_shape=[shape, shape, shape],
        scratch_shapes=[pltpu.VMEM((rows, LANES), F32), pltpu.VMEM((rows, LANES), F32)],
        compiler_params=pltpu.CompilerParams(vmem_limit_bytes=VMEM_LIMIT),
        cost_estimate=pl.CostEstimate(
            flops=20 * rows * rows * width,
            bytes_accessed=16 * rows * width,
            transcendentals=rows * rows * width // head_dim,
        ),
    )(projected, projected, projected, bias, lse, grad_mixture)
    return jnp.concatenate(grads, axis=1)


def swap(array):
    return lax.ppermute(array, "section", [(0, 1), (1, 0)])


def exchange(array, bits, size, sends=None):
    pairs = [
        (core * size + i, core * size + (i ^ (1 << bit)))
        for core, bit in enumerate(bits)
        for i in range(size)
        if sends is None or sends(core, i)
    ]
    return lax.ppermute(array, ("section", "dp"), pairs)


def bit_count(size):
    return size.bit_length() - 1


def orders(size, middle):
    bits = bit_count(size)
    others = tuple(reversed(range(2, bits - 1)))
    result = []
    for core in range(2):
        lowest = (0, 1) if core == 0 else (1, 0)
        order = ()
        for entry in middle:
            order += others if entry is None else (lowest[0] if entry == -1 else lowest[1],)
        result.append(order)
    return result


def mask_of(index, order, places):
    return sum(((index >> t) & 1) << places.index(bit) for t, bit in enumerate(order))


def placement(order_pair, places):
    position = lax.axis_index("dp")
    own = sum(((position >> bit) & 1) << p for p, bit in enumerate(places))
    count = 1 << len(places)
    masks = [jnp.asarray([mask_of(j, order, places) for j in range(count)], jnp.int32) for order in order_pair]
    return (own ^ jnp.where(lax.axis_index("section") == 0, masks[0], masks[1])).astype(jnp.int32)


def aligned(rows, cuts=()):
    return rows % 16 == 0 and all(c % LANES == 0 and r % 16 == 0 for r0, r1, c0, c1 in cuts for r, c in ((r0, c0), (r1, c1)))


def assembly_kernel(half, cuts, table, low, high, *outs):
    step = pl.program_id(0)

    def store(ref):
        for (r0, r1, c0, c1), out in zip(cuts, outs):
            out[...] = ref[0, r0:r1, c0:c1]

    pl.when(step < half)(lambda: store(low))
    pl.when(step >= half)(lambda: store(high))


def assembled(low, high, table, cuts):
    half, rows, width = low.shape
    shapes = [(2 * half * (r1 - r0), c1 - c0) for r0, r1, c0, c1 in cuts]
    if not aligned(rows, cuts):
        stack = jnp.concatenate([low, high], axis=0)[jnp.argsort(table)]
        return [stack[:, r0:r1, c0:c1].reshape(s) for (r0, r1, c0, c1), s in zip(cuts, shapes)]
    return pl.pallas_call(
        functools.partial(assembly_kernel, half, cuts),
        grid_spec=pltpu.PrefetchScalarGridSpec(
            num_scalar_prefetch=1,
            grid=(2 * half,),
            in_specs=[
                pl.BlockSpec((1, rows, width), lambda j, t: (jnp.minimum(j, half - 1), 0, 0)),
                pl.BlockSpec((1, rows, width), lambda j, t: (jnp.maximum(j - half, 0), 0, 0)),
            ],
            out_specs=[pl.BlockSpec((r1 - r0, c1 - c0), lambda j, t: (t[j], 0)) for r0, r1, c0, c1 in cuts],
        ),
        out_shape=[jax.ShapeDtypeStruct(s, low.dtype) for s in shapes],
        compiler_params=pltpu.CompilerParams(vmem_limit_bytes=VMEM_LIMIT),
        cost_estimate=pl.CostEstimate(flops=0, bytes_accessed=8 * half * rows * width, transcendentals=0),
    )(table, low, high)


def split_kernel(half, table, *refs):
    step = pl.program_id(0)
    send, keep = refs[-2:]

    def store(out):
        base = 0
        for ref in refs[:-2]:
            width = ref.shape[1]
            out[0, :, base : base + width] = ref[...]
            base += width

    pl.when(step < half)(lambda: store(send))
    pl.when(step >= half)(lambda: store(keep))


def split_stack(grads, table, count):
    half, rows = count // 2, grads[0].shape[0] // count
    width = sum(grad.shape[1] for grad in grads)
    if not (aligned(rows) and all(grad.shape[1] % LANES == 0 for grad in grads)):
        stack = jnp.concatenate([grad.reshape(count, rows, grad.shape[1]) for grad in grads], axis=2)[table]
        return stack[half:], stack[:half]
    shape = jax.ShapeDtypeStruct((half, rows, width), BF16)
    return pl.pallas_call(
        functools.partial(split_kernel, half),
        grid_spec=pltpu.PrefetchScalarGridSpec(
            num_scalar_prefetch=1,
            grid=(count,),
            in_specs=[
                pl.BlockSpec((rows, grad.shape[1]), lambda j, t: (t[jnp.where(j < half, j + half, j - half)], 0))
                for grad in grads
            ],
            out_specs=[
                pl.BlockSpec((1, rows, width), lambda j, t: (jnp.minimum(j, half - 1), 0, 0)),
                pl.BlockSpec((1, rows, width), lambda j, t: (jnp.maximum(j - half, 0), 0, 0)),
            ],
        ),
        out_shape=[shape, shape],
        compiler_params=pltpu.CompilerParams(vmem_limit_bytes=VMEM_LIMIT),
        cost_estimate=pl.CostEstimate(flops=0, bytes_accessed=4 * count * rows * width, transcendentals=0),
    )(table, *grads)


class Stream:
    def __init__(self, size, steps):
        self.size, self.steps = size, steps
        self.arriving = None
        self.value = None
        self.done = False
        self.pending = None

    def begin(self, arrived=None):
        try:
            self.pending = self.steps.send(arrived)
        except StopIteration as stop:
            self.pending, self.value, self.done = None, stop.value, True

    def launch(self):
        outgoing, bits, sends = self.pending
        self.arriving, self.pending = exchange(outgoing, bits, self.size, sends), None

    def result(self):
        if self.arriving is None and self.pending is None and not self.done:
            self.begin()
        while not self.done:
            if self.arriving is None:
                self.launch()
            arrived, self.arriving = self.arriving, None
            self.begin(arrived)
        return self.value


def advance(streams, tied):
    for stream in streams:
        if stream.arriving is None and stream.pending is None and not stream.done:
            stream.begin()
    moving = [stream for stream in streams if not stream.done]
    ending = [stream for stream in moving if stream.arriving is not None]
    fresh = [stream for stream in moving if stream.arriving is None]
    arrived, outgoing, tied = lax.optimization_barrier(
        ([s.arriving for s in ending], [s.pending[0] for s in fresh], tied)
    )
    for stream, array in zip(fresh, outgoing):
        stream.pending = (array,) + stream.pending[1:]
    for stream, array in zip(ending, arrived):
        stream.arriving = None
        stream.begin(array)
    for stream in moving:
        if not stream.done:
            stream.launch()
    return tied


def top_sends(size):
    top = bit_count(size) - 1
    return lambda core, i: (i >> top) == core


def doubling(held, order_pair, first=0):
    steps = list(zip(*order_pair))[first:]
    for bits in steps[:-1]:
        arrived = yield held, bits, None
        held = jnp.concatenate([held, arrived], axis=0)
    arrived = yield held, steps[-1], None
    return held, arrived


def gather_all(packed, order_pair, places, cuts):
    low, high = yield from doubling(packed[None], order_pair)
    return assembled(low, high, placement(order_pair, places), cuts)


def gather_core(piece, order_pair, places, cuts, size):
    top = bit_count(size) - 1
    arrived = yield piece, (top, top), top_sends(size)
    mine = (lax.axis_index("dp") >> top) == lax.axis_index("section")
    low, high = yield from doubling(jnp.where(mine, piece, arrived)[None], order_pair)
    return assembled(low, high, placement(order_pair, places), cuts)


def own_bit(pair):
    position = lax.axis_index("dp")
    return (position >> jnp.where(lax.axis_index("section") == 0, pair[0], pair[1])) & 1


def gather_square(blocks, order_pair, places, cuts):
    first, second = list(zip(*order_pair))[:2]
    a, b = own_bit(first), own_bit(second)
    kept = lax.dynamic_index_in_dim(blocks, a, 0, keepdims=False)
    arrived = yield lax.dynamic_index_in_dim(blocks, 1 - a, 0, keepdims=False), first, None
    held = jnp.stack([kept, arrived])
    kept = lax.dynamic_index_in_dim(held, b, 1, keepdims=False)
    arrived = yield lax.dynamic_index_in_dim(held, 1 - b, 1, keepdims=False), second, None
    low, high = yield from doubling(jnp.concatenate([kept, arrived], axis=0), order_pair, 2)
    return assembled(low, high, placement(order_pair, places), cuts)


def total_of(terms):
    return sum(term.astype(F32) for term in terms)


def halving(grads, order_pair, places, last=0):
    steps = list(zip(*order_pair))
    count = 1 << len(steps)
    outgoing, kept = split_stack([grad.astype(BF16) for grad in grads], placement(order_pair, places), count)
    terms = [kept]
    for bits in reversed(steps[last:]):
        half = terms[0].shape[0]
        if outgoing is None:
            half //= 2
            outgoing = total_of([term[half:] for term in terms]).astype(BF16)
            terms = [term[:half] for term in terms]
        arrived = yield outgoing, bits, None
        terms, outgoing = terms + [arrived], None
    return terms


def scatter_all(grads, order_pair, places):
    terms = yield from halving(grads, order_pair, places)
    return total_of(terms)[0].astype(BF16)


def scatter_core(grads, order_pair, places, size):
    terms = yield from halving(grads, order_pair, places)
    top = bit_count(size) - 1
    sends = top_sends(size)
    arrived = yield total_of(terms)[0].astype(BF16), (top, top), lambda core, i: not sends(core, i)
    return (total_of(terms)[0] + arrived.astype(F32)).astype(BF16)


def scatter_square(grads, order_pair, places):
    terms = yield from halving(grads, order_pair, places, 2)
    held = total_of(terms).astype(BF16)
    first, second = list(zip(*order_pair))[:2]
    arrived = yield held[2:], second, None
    held = jnp.stack([held[:2], arrived])
    arrived = yield held[:, 1], first, None
    return jnp.stack([held[:, 0], arrived])


def scatter_small(vector, size):
    position = lax.axis_index("dp")
    held = vector
    for bit in reversed(range(bit_count(size))):
        half = held.shape[0] // 2
        own = (position >> bit) & 1
        arrived = yield lax.dynamic_slice_in_dim(held, (1 - own) * half, half, 0), (bit, bit), None
        held = lax.dynamic_slice_in_dim(held, own * half, half, 0) + arrived
    return held[0, 0]


def in_square(blocks):
    is_first = lax.axis_index("section") == 0
    middle = jnp.where(is_first, blocks[1:3], jnp.stack([blocks[2], blocks[1]]))
    return jnp.concatenate([blocks[:1], middle, blocks[3:]], axis=0)


SQUARE = ((0, 1), (1, 0))


def square_gather(rows, size):
    held = rows[None]
    for bits in SQUARE:
        held = jnp.concatenate([held, exchange(held, bits, size)], axis=0)
    return in_square(held)


def square_scatter(blocks, size):
    held = in_square(blocks)
    for bits in reversed(SQUARE):
        half = held.shape[0] // 2
        arrived = exchange(held[half:].astype(BF16), bits, size)
        held = held[:half] + arrived.astype(F32)
    return held[0]


def local(
    size,
    bytes_in,
    lengths,
    patch_index,
    patch_count,
    gain_l1,
    qkv_l,
    out_l,
    gain_l2,
    up_l,
    down_l,
    patch_proj,
    gain_g1,
    qkv_g,
    out_g,
    gain_g2,
    up_g,
    down_g,
    out_grad,
):
    core = lax.axis_index("section")
    position = lax.axis_index("dp")
    is_first = core == 0
    seq_rows, half_l = bytes_in.shape[1:]
    width_l, width_g = 2 * half_l, out_g.shape[1]
    half_g = width_g // 2
    rows_l, rows_g = out_l.shape[0], out_g.shape[0]
    units_l, units_g = down_l.shape[0], down_g.shape[0]
    head_l, head_g = width_l // H_L, width_g // H_G
    micro_total, slot_total = patch_index.shape[1:]
    slots = micro_total * slot_total
    bits = bit_count(size)
    every = tuple(range(bits))

    def joined(mine, theirs, axis=1):
        low = jnp.where(is_first, mine, theirs)
        high = jnp.where(is_first, theirs, mine)
        return jnp.concatenate([low, high], axis=axis)

    def shared(mine, axis=1):
        return joined(mine, swap(mine), axis)

    def half_of(array, which, axis=1):
        length = array.shape[axis] // 2
        return lax.dynamic_slice_in_dim(array, which * length, length, axis)

    def own_heads(weight):
        rows, width = weight.shape
        thirds = weight.reshape(rows, 3, 2, width // 6)
        return lax.dynamic_index_in_dim(thirds, core, 2, keepdims=False).reshape(rows, width // 2)

    def gain_block(one, two):
        return jnp.pad(jnp.stack([one, two], axis=1), ((0, 0), (0, LANES - 2)))

    top_first = [(bits - 1,) + o for o in orders(size, (None, -1, -2))]
    mixed = orders(size, (-1, None, -2))
    plane = [o[:2] + (bits - 1,) + o[2:] for o in orders(size, (-1, -2, None))]
    line = orders(size, (None,))
    below, beyond = tuple(range(bits - 1)), tuple(range(2, bits - 1))

    fresh = functools.partial(Stream, size)
    up_width, qkv_width = up_l.shape[1] // 2, 3 * half_g
    square_units = units_g * (size // 8)
    stream_qkv_l = fresh(
        gather_all(
            jnp.concatenate([own_heads(qkv_l), gain_block(gain_l1, gain_l2)], axis=1),
            top_first,
            every,
            [(0, rows_l, 0, 3 * half_l), (0, rows_l, 3 * half_l, 3 * half_l + LANES)],
        )
    )
    stream_up_l = fresh(
        gather_all(
            jnp.concatenate([half_of(up_l, core), half_of(out_l, core), half_of(patch_proj, core)], axis=1),
            top_first,
            every,
            [
                (0, rows_l, 0, up_width),
                (0, rows_l, up_width, up_width + half_l),
                (0, rows_l, up_width + half_l, up_width + half_l + half_g),
            ],
        )
    )
    stream_down_l = fresh(gather_core(down_l, mixed, below, [(0, units_l, 0, width_l)], size))
    stream_qkv_g = fresh(
        gather_all(
            jnp.concatenate([own_heads(qkv_g), half_of(out_g, core), gain_block(gain_g1, gain_g2)], axis=1),
            top_first,
            every,
            [
                (0, rows_g, 0, qkv_width),
                (0, rows_g, qkv_width, qkv_width + half_g),
                (0, rows_g, qkv_width + half_g, qkv_width + half_g + LANES),
            ],
        )
    )
    blocks = half_of(up_g, core).reshape(rows_g, size // 8, 2, 2, units_g)
    blocks = jnp.where(is_first, blocks.transpose(3, 2, 0, 1, 4), blocks.transpose(2, 3, 0, 1, 4))
    stream_up_g = fresh(
        gather_square(
            blocks.reshape(2, 2, rows_g, square_units), plane, every, [(0, rows_g, 0, square_units)]
        )
    )
    stream_down_g = fresh(
        gather_core(down_g[:, :width_l], line, beyond, [(0, units_g, 0, width_l)], size)
    )

    bias_l = jnp.where(jnp.arange(seq_rows) < lengths[0], 0.0, NEG).astype(F32)[:, None]
    live = (jnp.arange(slot_total)[None, :] < patch_count[0][:, None]).reshape(slots)
    bias_g = jnp.where(live, 0.0, NEG).astype(F32)[:, None]
    positions = patch_index[0].reshape(slots)
    picks = positions[:, None] == jnp.arange(seq_rows)[None, :]
    picks_live = (picks & live[:, None]).astype(BF16)
    picks = picks.astype(BF16)

    advance([stream_qkv_l, stream_up_g], ())
    seq_inputs = shared(bytes_in[0])
    inputs = seq_inputs.astype(F32)
    scale_l1 = row_scale(inputs)
    scale_l1 = advance([stream_qkv_l, stream_up_l, stream_up_g], scale_l1)
    seq_grads = shared(out_grad[0])
    grad_top_b = mm(picks_live, seq_grads).astype(BF16)
    grad_top_b = advance([stream_qkv_l, stream_up_l, stream_down_l, stream_up_g], grad_top_b)
    square_top = square_gather(half_of(grad_top_b, core), size).reshape(4 * slots, half_l)
    square_top = shared(square_top)
    square_top = advance([stream_qkv_l, stream_up_l, stream_down_l, stream_qkv_g], square_top)

    advance([stream_qkv_l, stream_up_l, stream_down_l, stream_qkv_g], ())
    qkv_wl, gains_l = stream_qkv_l.result()
    gain_one_l, gain_two_l = gains_l[:, 0].astype(F32), gains_l[:, 1].astype(F32)
    normed_l = (inputs * scale_l1 * gain_one_l).astype(BF16)
    projected_l = mm(normed_l, qkv_wl).astype(BF16)
    mixture_l, lse_l = attention_forward(projected_l, bias_l, head_l)
    mixture_l = shared(mixture_l)
    mixture_l = advance([stream_up_l, stream_down_l, stream_qkv_g], mixture_l)
    up_wl, out_wl, proj_w = stream_up_l.result()
    out_wl, proj_w = shared(out_wl), shared(proj_w)
    out_own_l = half_of(out_wl, core, 0)
    hidden_l = inputs + mm(mixture_l, out_wl)
    scale_l2 = row_scale(hidden_l)
    normed_l2 = (hidden_l * scale_l2 * gain_two_l).astype(BF16)
    upward_l = mm(normed_l2, up_wl)
    activated_l = jax.nn.gelu(upward_l).astype(BF16)
    activated_l = advance([stream_down_l, stream_qkv_g, stream_up_g, stream_down_g], activated_l)
    (down_wl,) = stream_down_l.result()
    partial_l = mm(activated_l, down_wl)
    local_out = half_of(hidden_l, core) + half_of(partial_l, core) + swap(half_of(partial_l, 1 - core))

    boundary = shared(mm(picks, local_out.astype(BF16)).astype(BF16))
    start_rows = mm(boundary, proj_w)
    scale_g1 = row_scale(start_rows)
    scale_g1 = advance([stream_qkv_g, stream_up_g, stream_down_g], scale_g1)
    qkv_wg, out_wg, gains_g = stream_qkv_g.result()
    gain_one_g, gain_two_g = gains_g[:, 0].astype(F32), gains_g[:, 1].astype(F32)
    normed_g = (start_rows * scale_g1 * gain_one_g).astype(BF16)
    out_theirs_g = swap(out_wg)
    projected_g = mm(normed_g, qkv_wg).astype(BF16)
    mixture_g, lse_g = attention_forward(projected_g, bias_g, head_g)
    mixture_g = shared(mixture_g)
    hidden_g = start_rows + joined(mm(mixture_g, out_wg), mm(mixture_g, out_theirs_g))
    scale_g2 = row_scale(hidden_g)
    normed_g2 = (hidden_g * scale_g2 * gain_two_g).astype(BF16)
    square_normed = square_gather(half_of(normed_g2, core), size).reshape(4 * slots, half_g)
    square_normed = shared(square_normed)
    square_normed = advance([stream_up_g, stream_down_g], square_normed)
    (up_wg,) = stream_up_g.result()
    (down_wg,) = stream_down_g.result()
    upward_g = mm(square_normed, up_wg)
    activated_g = jax.nn.gelu(upward_g).astype(BF16)

    def scattered(grads, order_pair, places):
        return fresh(scatter_all(grads, order_pair, places))

    grad_down_g = mm_tn(activated_g, square_top).astype(BF16)
    stream_down_g = fresh(scatter_core([grad_down_g], line, beyond, size))
    grad_act_g = mm_nt(square_top, down_wg)
    grad_up_g_rows = jax.vjp(jax.nn.gelu, upward_g)[1](grad_act_g)[0].astype(BF16)
    grad_up_g = mm_tn(square_normed, grad_up_g_rows).astype(BF16)
    stream_up_g = fresh(scatter_square([grad_up_g], plane, every))
    part = mm_nt(grad_up_g_rows, up_wg)
    part = half_of(part, core) + swap(half_of(part, 1 - core).astype(BF16)).astype(F32)
    part = advance([stream_down_g, stream_up_g], part)
    part = shared(square_scatter(part.reshape(4, slots, half_g), size))
    pulled, grad_gain_g2 = norm_backward(part, hidden_g, scale_g2, gain_two_g)
    grad_hidden_g = jnp.pad(grad_top_b.astype(F32), ((0, 0), (0, width_g - width_l))) + pulled
    grad_hidden_gb = grad_hidden_g.astype(BF16)
    mine_gb, theirs_gb = half_of(grad_hidden_gb, core), half_of(grad_hidden_gb, 1 - core)
    grad_out_g = mm_tn(mixture_g, mine_gb).astype(BF16)
    grad_mixture_g = (
        mm_nt(mine_gb, half_of(out_wg, core, 0)) + mm_nt(theirs_gb, half_of(out_theirs_g, core, 0))
    ).astype(BF16)
    grad_projected_g = attention_backward(projected_g, bias_g, lse_g, grad_mixture_g, head_g)
    grad_qkv_g = mm_tn(normed_g, grad_projected_g).astype(BF16)
    stream_qkv_g = scattered([grad_qkv_g, grad_out_g], top_first, every)
    grad_projected_g = advance([stream_down_g, stream_up_g, stream_qkv_g], grad_projected_g)
    part = mm_nt(grad_projected_g, qkv_wg)
    pulled, grad_gain_g1 = norm_backward(part + swap(part), start_rows, scale_g1, gain_one_g)
    grad_start = (grad_hidden_g + pulled).astype(BF16)
    grad_proj = mm_tn(boundary, half_of(grad_start, core)).astype(BF16)

    grad_rows = mm_nt(grad_start, proj_w).astype(BF16)
    grad_local = seq_grads.astype(F32) + mm_tn(picks, grad_rows)
    grad_local_b = grad_local.astype(BF16)
    grad_down_l = mm_tn(activated_l, grad_local_b).astype(BF16)
    stream_down_l = fresh(scatter_core([grad_down_l], mixed, below, size))
    grad_act_l = mm_nt(grad_local_b, down_wl)
    grad_up_l_rows = jax.vjp(jax.nn.gelu, upward_l)[1](grad_act_l)[0].astype(BF16)
    grad_up_l_rows = advance([stream_down_g, stream_up_g, stream_qkv_g, stream_down_l], grad_up_l_rows)
    grad_up_l = mm_tn(normed_l2, grad_up_l_rows).astype(BF16)
    part = mm_nt(grad_up_l_rows, up_wl)
    pulled, grad_gain_l2 = norm_backward(part + swap(part), hidden_l, scale_l2, gain_two_l)
    grad_hidden_l = grad_local + pulled
    grad_hidden_lb = grad_hidden_l.astype(BF16)
    grad_out_l = mm_tn(mixture_l, half_of(grad_hidden_lb, core)).astype(BF16)
    stream_up_l = scattered([grad_up_l, grad_out_l, grad_proj], top_first, every)
    grad_mixture_l = mm_nt(grad_hidden_lb, out_own_l).astype(BF16)
    grad_mixture_l = advance([stream_up_g, stream_qkv_g, stream_down_l, stream_up_l], grad_mixture_l)
    grad_projected_l = attention_backward(projected_l, bias_l, lse_l, grad_mixture_l, head_l)
    grad_qkv_l = mm_tn(normed_l, grad_projected_l).astype(BF16)
    stream_qkv_l = scattered([grad_qkv_l], top_first, every)
    grad_projected_l = advance(
        [stream_up_g, stream_qkv_g, stream_down_l, stream_up_l, stream_qkv_l], grad_projected_l
    )
    part = mm_nt(grad_projected_l, qkv_wl)
    pulled, grad_gain_l1 = norm_backward(part + swap(part), inputs, scale_l1, gain_one_l)
    input_grad = half_of(grad_hidden_l + pulled, core).astype(BF16)[None]
    gains = jnp.concatenate(
        [
            grad.reshape(size, 1, grad.shape[0] // size)
            for grad in (grad_gain_l1, grad_gain_l2, grad_gain_g1, grad_gain_g2)
        ],
        axis=2,
    )
    stream_gains = fresh(scatter_small(gains, size))

    partial_g = mm(activated_g, down_wg)
    partial_g = half_of(partial_g, core) + swap(half_of(partial_g, 1 - core).astype(BF16)).astype(F32)
    returned = half_of(hidden_g[:, :width_l], core) + square_scatter(partial_g.reshape(4, slots, half_l), size)
    hidden_out = (local_out + mm_tn(picks_live, returned.astype(BF16))).astype(BF16)[None]
    input_grad, hidden_out = advance(
        [stream_qkv_g, stream_down_l, stream_up_l, stream_qkv_l, stream_gains], (input_grad, hidden_out)
    )
    advance([stream_up_l, stream_qkv_l, stream_gains], ())
    advance([stream_up_l, stream_qkv_l, stream_gains], ())

    def joined_columns(mine, theirs):
        return joined(mine, theirs).astype(F32)

    def joined_heads(mine, theirs):
        rows, width = mine.shape
        thirds = [part.reshape(rows, 3, width // 3) for part in (mine, theirs)]
        return joined(*thirds, axis=2).reshape(rows, 2 * width).astype(F32)

    def from_owner(mine, theirs):
        return jnp.where((position >> (bits - 1)) == core, mine, theirs).astype(F32)

    def in_order(blocks):
        low = own_bit((0, 0)), own_bit((1, 1))
        rows, width = blocks.shape[2:]
        placed = []
        for y in range(2):
            for x in range(2):
                dx, dy = x ^ low[0], y ^ low[1]
                index = jnp.where(is_first, 2 * dx + dy, 2 * dy + dx)
                placed.append(lax.dynamic_index_in_dim(blocks.reshape(4, rows, width), index, 0, keepdims=False))
        stack = jnp.stack(placed).reshape(4, rows, size // 8, units_g)
        return stack.transpose(1, 2, 0, 3).reshape(rows, 4 * width)

    down_g_mine = stream_down_g.result()
    total_down_g = from_owner(down_g_mine, swap(down_g_mine))
    total_down_g = jnp.pad(total_down_g, ((0, 0), (0, width_g - width_l)))
    up_g_mine = in_order(stream_up_g.result())
    total_up_g = joined_columns(up_g_mine, swap(up_g_mine))
    g_mine = stream_qkv_g.result()
    g_theirs = swap(g_mine)
    total_qkv_g = joined_heads(g_mine[:, :qkv_width], g_theirs[:, :qkv_width])
    total_out_g = joined_columns(g_mine[:, qkv_width:], g_theirs[:, qkv_width:])
    down_l_mine = stream_down_l.result()
    total_down_l = from_owner(down_l_mine, swap(down_l_mine))
    l_mine = stream_up_l.result()
    l_theirs = swap(l_mine)
    cuts = [0, up_width, up_width + half_l, up_width + half_l + half_g]
    total_up_l, total_out_l, total_proj = (
        joined_columns(l_mine[:, low:high], l_theirs[:, low:high]) for low, high in zip(cuts, cuts[1:])
    )
    q_mine = stream_qkv_l.result()
    total_qkv_l = joined_heads(q_mine, swap(q_mine))
    gains = stream_gains.result()
    gains = jnp.where(is_first, gains, lax.ppermute(gains, "section", [(0, 1)]))
    total_gain_l1 = gains[:rows_l]
    total_gain_l2 = gains[rows_l : 2 * rows_l]
    total_gain_g1 = gains[2 * rows_l : 2 * rows_l + rows_g]
    total_gain_g2 = gains[2 * rows_l + rows_g :]
    return (
        hidden_out,
        input_grad,
        total_gain_l1,
        total_qkv_l,
        total_out_l,
        total_gain_l2,
        total_up_l,
        total_down_l,
        total_proj,
        total_gain_g1,
        total_qkv_g,
        total_out_g,
        total_gain_g2,
        total_up_g,
        total_down_g,
    )


def solution(mesh):
    rows, vector = P("dp", None), P("dp")
    features = P("dp", None, "section")
    in_specs = (
        features,
        vector,
        P("dp", None, None),
        rows,
        vector,
        rows,
        rows,
        vector,
        rows,
        rows,
        rows,
        vector,
        rows,
        rows,
        vector,
        rows,
        rows,
        features,
    )
    out_specs = (
        features,
        features,
        vector,
        rows,
        rows,
        vector,
        rows,
        rows,
        rows,
        vector,
        rows,
        rows,
        vector,
        rows,
        rows,
    )
    return jax.shard_map(
        functools.partial(local, mesh.shape["dp"]),
        mesh=mesh,
        in_specs=in_specs,
        out_specs=out_specs,
        check_vma=False,
    )
```

```python
import functools

import jax
import jax.numpy as jnp
import numpy as np
from jax import lax
from jax.experimental import pallas as pl
from jax.experimental.pallas import tpu as pltpu
from jax.sharding import PartitionSpec as P

H_L = 12
H_G = 24
WINDOW = 1536
EPSILON = 1e-06
LANES = 128
GELU_SCALE = (2.0 / np.pi) ** 0.5
GELU_CUBE = 0.044715
NEG = -1e30
VMEM_LIMIT = 48 * 1024 * 1024
FREE = pl.CostEstimate(flops=0, bytes_accessed=0, transcendentals=0)
LONG = pl.CostEstimate(flops=10**11, bytes_accessed=0, transcendentals=0)
F32 = jnp.float32
BF16 = jnp.bfloat16


def mm(left, right):
    return jnp.dot(left, right, preferred_element_type=F32)


def mm_nt(left, right):
    return lax.dot_general(left, right, (((1,), (1,)), ((), ())), preferred_element_type=F32)


def mm_tn(left, right):
    return lax.dot_general(left, right, (((0,), (0,)), ((), ())), preferred_element_type=F32)


def row_scale(values):
    return lax.rsqrt(jnp.mean(values * values, axis=-1, keepdims=True) + EPSILON)


def norm_backward(grad_normed, values, scale, gain):
    grad_gain = jnp.sum(grad_normed * values * scale, axis=0)
    pulled = grad_normed * gain
    inner = jnp.mean(pulled * values, axis=-1, keepdims=True)
    return scale * pulled - values * (scale * scale * scale * inner), grad_gain


def query_block(rows):
    return 256 if rows % 256 == 0 else rows


def masked_scores(keys, query, bias, start, block, window):
    pos_k = lax.broadcasted_iota(jnp.int32, (block, block), 0)
    pos_q = lax.broadcasted_iota(jnp.int32, (block, block), 1)
    parts = []
    if start:
        before = mm_nt(keys[:start], query) + bias[:start]
        if window is not None:
            far = lax.broadcasted_iota(jnp.int32, (start, block), 0)
            own = lax.broadcasted_iota(jnp.int32, (start, block), 1) + start
            before = jnp.where(own - far < window, before, NEG)
        parts.append(before)
    diagonal = mm_nt(keys[start : start + block], query)
    diagonal = jnp.where(
        pos_k == pos_q,
        diagonal,
        jnp.where(pos_k < pos_q, diagonal + bias[start : start + block], NEG),
    )
    parts.append(diagonal)
    return parts


def attention_forward_kernel(rows, head_dim, window, q_ref, k_ref, v_ref, bias_ref, o_ref, lse_ref):
    block = query_block(rows)
    lane = lax.broadcasted_iota(jnp.int32, (block, LANES), 1)
    score_scale = head_dim ** (-0.5)
    for index in range(rows // block):
        start = index * block
        queries = q_ref[start : start + block, :] * score_scale
        out = jnp.zeros((block, LANES), F32)
        for head in range(LANES // head_dim):
            mine = (lane >= head * head_dim) & (lane < (head + 1) * head_dim)
            query = jnp.where(mine, queries, jnp.zeros_like(queries)).astype(BF16)
            parts = masked_scores(k_ref, query, bias_ref, start, block, window)
            top = functools.reduce(jnp.maximum, [jnp.max(p, axis=0, keepdims=True) for p in parts])
            parts = [jnp.exp(p - top) for p in parts]
            total = functools.reduce(jnp.add, [jnp.sum(p, axis=0, keepdims=True) for p in parts])
            inverse = 1.0 / total
            mixed = jnp.zeros((block, LANES), F32)
            low = 0
            for part in parts:
                high = low + part.shape[0]
                mixed += mm_tn((part * inverse).astype(BF16), v_ref[low:high, :])
                low = high
            out = jnp.where(mine, mixed, out)
            lse_ref[0, head : head + 1, start : start + block] = top + jnp.log(total)
        o_ref[start : start + block, :] = out.astype(BF16)


def attention_backward_kernel(
    rows, head_dim, window, q_ref, k_ref, v_ref, bias_ref, lse_ref, do_ref, dq_ref, dk_ref, dv_ref, dk_acc, dv_acc
):
    block = query_block(rows)
    lane = lax.broadcasted_iota(jnp.int32, (block, LANES), 1)
    score_scale = head_dim ** (-0.5)
    dk_acc[...] = jnp.zeros((rows, LANES), F32)
    dv_acc[...] = jnp.zeros((rows, LANES), F32)
    for index in range(rows // block):
        start = index * block
        queries = q_ref[start : start + block, :] * score_scale
        grads = do_ref[start : start + block, :]
        dq = jnp.zeros((block, LANES), F32)
        for head in range(LANES // head_dim):
            mine = (lane >= head * head_dim) & (lane < (head + 1) * head_dim)
            query = jnp.where(mine, queries, jnp.zeros_like(queries)).astype(BF16)
            grad = jnp.where(mine, grads, jnp.zeros_like(grads))
            lse = lse_ref[0, head : head + 1, start : start + block]
            parts = masked_scores(k_ref, query, bias_ref, start, block, window)
            parts = [jnp.exp(p - lse) for p in parts]
            grad_parts = []
            low = 0
            for part in parts:
                high = low + part.shape[0]
                grad_parts.append(mm_nt(v_ref[low:high, :], grad))
                low = high
            delta = functools.reduce(
                jnp.add,
                [jnp.sum(p * g, axis=0, keepdims=True) for p, g in zip(parts, grad_parts)],
            )
            mixed = jnp.zeros((block, LANES), F32)
            low = 0
            for part, grad_part in zip(parts, grad_parts):
                high = low + part.shape[0]
                grad_score = (part * (grad_part - delta)).astype(BF16)
                dv_acc[low:high, :] += mm(part.astype(BF16), grad)
                dk_acc[low:high, :] += mm(grad_score, query)
                mixed += mm_tn(grad_score, k_ref[low:high, :])
                low = high
            dq = jnp.where(mine, mixed, dq)
        dq_ref[start : start + block, :] = (dq * score_scale).astype(BF16)
    dk_ref[...] = dk_acc[...].astype(BF16)
    dv_ref[...] = dv_acc[...].astype(BF16)


def attention_specs(rows, width):
    pairs = width // LANES
    wide = lambda part: pl.BlockSpec((rows, LANES), lambda i, part=part: (0, part * pairs + i))
    bias = pl.BlockSpec((rows, 1), lambda i: (0, 0))
    return pairs, wide, bias


def attention_forward(projected, bias, head_dim):
    rows, width = projected.shape[0], projected.shape[1] // 3
    pairs, wide, bias_spec = attention_specs(rows, width)
    per = LANES // head_dim
    window = WINDOW if rows > WINDOW else None
    return pl.pallas_call(
        functools.partial(attention_forward_kernel, rows, head_dim, window),
        grid=(pairs,),
        in_specs=[wide(0), wide(1), wide(2), bias_spec],
        out_specs=[wide(0), pl.BlockSpec((1, per, rows), lambda i: (i, 0, 0))],
        out_shape=[
            jax.ShapeDtypeStruct((rows, width), BF16),
            jax.ShapeDtypeStruct((pairs, per, rows), F32),
        ],
        compiler_params=pltpu.CompilerParams(vmem_limit_bytes=VMEM_LIMIT),
        cost_estimate=FREE,
    )(projected, projected, projected, bias)


def attention_backward(projected, bias, lse, grad_mixture, head_dim):
    rows, width = grad_mixture.shape
    pairs, wide, bias_spec = attention_specs(rows, width)
    per = LANES // head_dim
    window = WINDOW if rows > WINDOW else None
    shape = jax.ShapeDtypeStruct((rows, width), BF16)
    grads = pl.pallas_call(
        functools.partial(attention_backward_kernel, rows, head_dim, window),
        grid=(pairs,),
        in_specs=[
            wide(0),
            wide(1),
            wide(2),
            bias_spec,
            pl.BlockSpec((1, per, rows), lambda i: (i, 0, 0)),
            wide(0),
        ],
        out_specs=[wide(0), wide(0), wide(0)],
        out_shape=[shape, shape, shape],
        scratch_shapes=[pltpu.VMEM((rows, LANES), F32), pltpu.VMEM((rows, LANES), F32)],
        compiler_params=pltpu.CompilerParams(vmem_limit_bytes=VMEM_LIMIT),
        cost_estimate=LONG,
    )(projected, projected, projected, bias, lse, grad_mixture)
    return grads


def swap(array):
    return lax.ppermute(array, "section", [(0, 1), (1, 0)])


def exchange(array, bits, size, sends=None):
    if sends == "flips":
        return tuple(
            lax.ppermute(part, "dp", [(i, i ^ flip) for i in range(size)]) for part, flip in zip(array, bits)
        )
    pairs = [
        (core * size + i, core * size + (i ^ (1 << bit)))
        for core, bit in enumerate(bits)
        for i in range(size)
        if sends is None or sends(core, i)
    ]
    return jax.tree.map(lambda part: lax.ppermute(part, ("section", "dp"), pairs), array)


def bit_count(size):
    return size.bit_length() - 1


def orders(size, middle):
    bits = bit_count(size)
    others = tuple(reversed(range(2, bits - 1)))
    result = []
    for core in range(2):
        lowest = (0, 1) if core == 0 else (1, 0)
        order = ()
        for entry in middle:
            order += others if entry is None else (lowest[0] if entry == -1 else lowest[1],)
        result.append(order)
    return result


def mask_of(index, order, places):
    return sum(((index >> t) & 1) << places.index(bit) for t, bit in enumerate(order))


def placement(order_pair, places):
    position = lax.axis_index("dp")
    own = sum(((position >> bit) & 1) << p for p, bit in enumerate(places))
    count = 1 << len(places)
    masks = [jnp.asarray([mask_of(j, order, places) for j in range(count)], jnp.int32) for order in order_pair]
    return (own ^ jnp.where(lax.axis_index("section") == 0, masks[0], masks[1])).astype(jnp.int32)


def aligned(rows, cuts=()):
    return rows % 16 == 0 and all(c % LANES == 0 and r % 16 == 0 for r0, r1, c0, c1 in cuts for r, c in ((r0, c0), (r1, c1)))


def assembly_kernel(bounds, cuts, table, *refs):
    step = pl.program_id(0)
    parts, outs = refs[: len(bounds)], refs[len(bounds) :]

    def store(ref):
        for (r0, r1, c0, c1), out in zip(cuts, outs):
            out[...] = ref[0, r0:r1, c0:c1]

    for (low, high), ref in zip(bounds, parts):
        pl.when((step >= low) & (step < high))(functools.partial(store, ref))


def assembled(parts, table, cuts, offset=0, width=None):
    rows = parts[0].shape[1]
    width = width or parts[0].shape[2]
    ends = np.cumsum([part.shape[0] for part in parts])
    count = int(ends[-1])
    bounds = [(int(end) - part.shape[0], int(end)) for end, part in zip(ends, parts)]
    shapes = [(count * (r1 - r0), c1 - c0) for r0, r1, c0, c1 in cuts]
    if not aligned(rows, cuts):
        stack = jnp.concatenate(parts, axis=0)[jnp.argsort(table)][..., offset : offset + width]
        return [stack[:, r0:r1, c0:c1].reshape(s) for (r0, r1, c0, c1), s in zip(cuts, shapes)]
    return pl.pallas_call(
        functools.partial(assembly_kernel, bounds, cuts),
        grid_spec=pltpu.PrefetchScalarGridSpec(
            num_scalar_prefetch=1,
            grid=(count,),
            in_specs=[
                pl.BlockSpec(
                    (1, rows, width),
                    lambda j, t, low=low, high=high: (jnp.clip(j, low, high - 1) - low, 0, offset // width),
                )
                for low, high in bounds
            ],
            out_specs=[pl.BlockSpec((r1 - r0, c1 - c0), lambda j, t: (t[j], 0)) for r0, r1, c0, c1 in cuts],
        ),
        out_shape=[jax.ShapeDtypeStruct(s, parts[0].dtype) for s in shapes],
        compiler_params=pltpu.CompilerParams(vmem_limit_bytes=VMEM_LIMIT),
        cost_estimate=FREE,
    )(table, *parts)


def quarters(parts):
    if len(parts) == 4:
        return [(part, 0) for part in parts]
    return [(part, k) for part in parts for k in range(2)]


def grouped_kernel(cuts, table, *refs):
    step = pl.program_id(0)
    for index, part in enumerate(refs[:4]):
        place = table[step + index * pl.num_programs(0)] % 4
        for (r0, r1, c0, c1), out in zip(cuts, refs[4:]):
            rows = r1 - r0
            out[pl.ds(pl.multiple_of(place * rows, 16), rows), :] = part[0, r0:r1, c0:c1]


def assembled_fours(parts, table, cuts, width=None, cost=FREE):
    rows = parts[0].shape[1]
    width = width or parts[0].shape[2]
    count = sum(part.shape[0] for part in parts)
    shapes = [(count * (r1 - r0), c1 - c0) for r0, r1, c0, c1 in cuts]
    if not aligned(rows, cuts):
        stack = jnp.concatenate(parts, axis=0)[jnp.argsort(table)]
        return [stack[:, r0:r1, c0:c1].reshape(s) for (r0, r1, c0, c1), s in zip(cuts, shapes)]
    steps = count // 4
    return pl.pallas_call(
        functools.partial(grouped_kernel, cuts),
        grid_spec=pltpu.PrefetchScalarGridSpec(
            num_scalar_prefetch=1,
            grid=(steps,),
            in_specs=[
                pl.BlockSpec((1, rows, width), lambda j, t, k=k: (k * steps + j, 0, 0)) for _, k in quarters(parts)
            ],
            out_specs=[
                pl.BlockSpec((4 * (r1 - r0), c1 - c0), lambda j, t: (t[j] // 4, 0)) for r0, r1, c0, c1 in cuts
            ],
        ),
        out_shape=[jax.ShapeDtypeStruct(s, parts[0].dtype) for s in shapes],
        compiler_params=pltpu.CompilerParams(vmem_limit_bytes=VMEM_LIMIT),
        cost_estimate=cost,
    )(table, *[part for part, _ in quarters(parts)])


def split_kernel(half, count, table, *refs):
    step = pl.program_id(0)
    send, keep = refs[-2:]

    def store(out):
        base = 0
        for ref in refs[:count]:
            width = ref.shape[1]
            out[0, :, base : base + width] = ref[...]
            base += width

    pl.when(step < half)(lambda: store(send))
    pl.when(step >= half)(lambda: store(keep))


def split_stack(grads, table, count, into=None):
    half, rows = count // 2, grads[0].shape[0] // count
    width = sum(grad.shape[1] for grad in grads)
    if not (aligned(rows) and all(grad.shape[1] % LANES == 0 for grad in grads)):
        stack = jnp.concatenate([grad.reshape(count, rows, grad.shape[1]) for grad in grads], axis=2)[table]
        halves = [stack[half:], stack[:half]]
        if into is not None:
            halves = [jnp.concatenate([part, old[..., width:]], axis=2) for part, old in zip(halves, into)]
        return halves
    full = width if into is None else into[0].shape[2]
    shape = jax.ShapeDtypeStruct((half, rows, full), BF16)
    into = [] if into is None else list(into)
    return pl.pallas_call(
        functools.partial(split_kernel, half, len(grads)),
        grid_spec=pltpu.PrefetchScalarGridSpec(
            num_scalar_prefetch=1,
            grid=(count,),
            in_specs=[
                pl.BlockSpec((rows, grad.shape[1]), lambda j, t: (t[jnp.where(j < half, j + half, j - half)], 0))
                for grad in grads
            ]
            + [pl.BlockSpec(memory_space=pl.ANY) for _ in into],
            out_specs=[
                pl.BlockSpec((1, rows, width), lambda j, t: (jnp.minimum(j, half - 1), 0, 0)),
                pl.BlockSpec((1, rows, width), lambda j, t: (jnp.maximum(j - half, 0), 0, 0)),
            ],
        ),
        out_shape=[shape, shape],
        input_output_aliases={1 + len(grads) + k: k for k in range(len(into))},
        compiler_params=pltpu.CompilerParams(vmem_limit_bytes=VMEM_LIMIT),
        cost_estimate=FREE,
    )(table, *grads, *into)


def write_rows(target, parts, table, rows):
    index = 0
    for part in parts:
        for k in range(part.shape[0]):
            target[pl.ds(pl.multiple_of(table[index] * rows, 16), rows), :] = part[k]
            index += 1


def product_kernel(rows, count, gelu, table, x_ref, *refs):
    parts, outs, weight = refs[:count], refs[count:-1], refs[-1]
    write_rows(weight, parts, table, rows)
    result = jnp.dot(x_ref[...], weight[...], preferred_element_type=F32)
    if not gelu:
        outs[0][...] = result.astype(outs[0].dtype)
        return
    square = result * result
    bend = jnp.tanh(GELU_SCALE * (result + GELU_CUBE * (result * square)))
    outs[0][...] = (0.5 * result * (1.0 + bend)).astype(outs[0].dtype)
    slope = 0.5 * (1.0 + bend)
    slope += (0.5 * GELU_SCALE) * result * (1.0 - bend * bend) * (1.0 + (3.0 * GELU_CUBE) * square)
    outs[1][...] = slope.astype(outs[1].dtype)


def pullback_kernel(rows, count, bounds, table, places, x_ref, *refs):
    parts, grads = refs[:count], refs[count : count + len(bounds)]
    dx_ref, send, keep, weight, turned, total = refs[count + len(bounds) :]
    step = pl.program_id(0)

    @pl.when(step == 0)
    def _():
        turned[...] = x_ref[...].T
        total[...] = jnp.zeros_like(total)

    write_rows(weight, parts, table, rows)
    grad = grads[-1][...]
    for (low, high), ref in list(zip(bounds, grads))[:-1]:
        grad = jnp.where((step >= low) & (step < high), ref[...], grad)
    total[...] += lax.dot_general(grad, weight[...], (((1,), (1,)), ((), ())), preferred_element_type=F32)
    weight[...] = jnp.dot(turned[...], grad, preferred_element_type=F32).astype(BF16)
    half = keep.shape[0]
    for index in range(2 * half):
        block = weight[pl.ds(pl.multiple_of(places[index] * rows, 16), rows), :]
        (keep if index < half else send)[index % half] = block

    @pl.when(step == pl.num_programs(0) - 1)
    def _():
        dx_ref[...] = total[...].astype(BF16)


TILE = 384


class Weight:
    def __init__(self, parts, table, offset, width):
        self.parts, self.table, self.offset, self.width = parts, table, offset, width
        self.rows = parts[0].shape[1]
        self.count = sum(part.shape[0] for part in parts)
        self.aligned = aligned(self.rows) and offset % TILE == 0 and width % TILE == 0

    def whole(self):
        cut = (0, self.rows, 0, self.width)
        stack = jnp.concatenate(self.parts, axis=0)[jnp.argsort(self.table)]
        return stack[..., self.offset : self.offset + self.width].reshape(-1, self.width)

    def part_specs(self):
        first = self.offset // TILE
        return [
            pl.BlockSpec((self.count // 4, self.rows, TILE), lambda i, *tables, k=k: (k, 0, first + i))
            for _, k in quarters(self.parts)
        ]

    def product(self, x, gelu=False):
        if not self.aligned:
            result = mm(x, self.whole())
            if not gelu:
                return result.astype(BF16)
            slope = jax.vjp(jax.nn.gelu, result)[1](jnp.ones_like(result))[0]
            return jax.nn.gelu(result).astype(BF16), slope.astype(BF16)
        tokens, depth = x.shape
        outs = 2 if gelu else 1
        shape = jax.ShapeDtypeStruct((tokens, self.width), BF16)
        results = pl.pallas_call(
            functools.partial(product_kernel, self.rows, 4, gelu),
            grid_spec=pltpu.PrefetchScalarGridSpec(
                num_scalar_prefetch=1,
                grid=(self.width // TILE,),
                in_specs=[pl.BlockSpec((tokens, depth), lambda i, t: (0, 0))] + self.part_specs(),
                out_specs=[pl.BlockSpec((tokens, TILE), lambda i, t: (0, i))] * outs,
                scratch_shapes=[pltpu.VMEM((depth, TILE), BF16)],
            ),
            out_shape=[shape] * outs,
            compiler_params=pltpu.CompilerParams(vmem_limit_bytes=VMEM_LIMIT),
            cost_estimate=LONG if gelu else FREE,
        )(self.table, x, *[part for part, _ in quarters(self.parts)])
        return results if gelu else results[0]

    def pullback(self, x, grads, places, lead=0):
        if not self.aligned:
            grad = jnp.concatenate(grads, axis=1)
            halves = split_stack([mm_tn(x, grad).astype(BF16)], places, self.count)
            return mm_nt(grad, self.whole()).astype(BF16), [jnp.pad(h, ((0, 0), (0, 0), (lead, 0))) for h in halves]
        tokens, depth = x.shape
        ends = np.cumsum([grad.shape[1] // TILE for grad in grads])
        bounds = [(int(end) - grad.shape[1] // TILE, int(end)) for end, grad in zip(ends, grads)]
        half = jax.ShapeDtypeStruct((self.count // 2, self.rows, lead + self.width), BF16)
        half_spec = pl.BlockSpec((self.count // 2, self.rows, TILE), lambda i, t, p: (0, 0, lead // TILE + i))
        result = pl.pallas_call(
            functools.partial(pullback_kernel, self.rows, 4, bounds),
            grid_spec=pltpu.PrefetchScalarGridSpec(
                num_scalar_prefetch=2,
                grid=(self.width // TILE,),
                in_specs=[pl.BlockSpec((tokens, depth), lambda i, t, p: (0, 0))]
                + self.part_specs()
                + [
                    pl.BlockSpec((tokens, TILE), lambda i, t, p, low=low, high=high: (0, jnp.clip(i, low, high - 1) - low))
                    for low, high in bounds
                ],
                out_specs=[pl.BlockSpec((tokens, depth), lambda i, t, p: (0, 0)), half_spec, half_spec],
                scratch_shapes=[
                    pltpu.VMEM((depth, TILE), BF16),
                    pltpu.VMEM((depth, tokens), BF16),
                    pltpu.VMEM((tokens, depth), F32),
                ],
            ),
            out_shape=[jax.ShapeDtypeStruct((tokens, depth), BF16), half, half],
            compiler_params=pltpu.CompilerParams(vmem_limit_bytes=VMEM_LIMIT),
            cost_estimate=FREE,
        )(self.table, places, x, *[part for part, _ in quarters(self.parts)], *grads)
        return result[0], result[1:]


class Stream:
    def __init__(self, size, steps):
        self.size, self.steps = size, steps
        self.arriving = None
        self.value = None
        self.done = False
        self.pending = None

    def begin(self, arrived=None):
        try:
            self.pending = self.steps.send(arrived)
        except StopIteration as stop:
            self.pending, self.value, self.done = None, stop.value, True

    def launch(self):
        outgoing, bits, sends = self.pending
        self.arriving, self.pending = exchange(outgoing, bits, self.size, sends), None

    def result(self):
        if self.arriving is None and self.pending is None and not self.done:
            self.begin()
        while not self.done:
            if self.arriving is None:
                self.launch()
            arrived, self.arriving = self.arriving, None
            self.begin(arrived)
        return self.value


def advance(streams, tied, hold=()):
    for stream in streams:
        if stream.arriving is None and stream.pending is None and not stream.done:
            stream.begin()
    moving = [stream for stream in streams if not stream.done]
    ending = [stream for stream in moving if stream.arriving is not None]
    fresh = [stream for stream in moving if stream.arriving is None]
    arrived, outgoing, tied = lax.optimization_barrier(
        ([s.arriving for s in ending], [s.pending[0] for s in fresh], tied)
    )
    for stream, array in zip(fresh, outgoing):
        stream.pending = (array,) + stream.pending[1:]
    for stream, array in zip(ending, arrived):
        stream.arriving = None
        stream.begin(array)
    for stream in moving:
        if not stream.done and stream not in hold:
            stream.launch()
    return tied


def top_sends(size):
    top = bit_count(size) - 1
    return lambda core, i: (i >> top) == core


def doubling(held, order_pair, first=0, twice=False):
    parts = (held,)
    steps = list(zip(*order_pair))[first:]
    for index, bits in enumerate(steps):
        if len(parts) > 1 and not (twice and index == len(steps) - 1):
            parts = (jnp.concatenate(parts, axis=0),)
        arrived = yield lax.optimization_barrier(parts), bits, None
        parts = parts + arrived
    return parts


def gather_all(packed, order_pair, twice):
    return (yield from doubling(packed[None], order_pair, 0, twice))


def gather_core(piece, order_pair, places):
    size = lax.axis_size("dp")
    top = bit_count(size) - 1
    arrived = yield piece, (top, top), top_sends(size)
    mine = (lax.axis_index("dp") >> top) == lax.axis_index("section")
    parts = yield from doubling(jnp.where(mine, piece, arrived)[None], order_pair)
    table, cuts = placement(order_pair, places), [(0, piece.shape[0], 0, piece.shape[1])]
    return assembled_fours(parts, table, cuts) if len(places) > 1 else assembled(parts, table, cuts)


def own_bit(pair):
    position = lax.axis_index("dp")
    return (position >> jnp.where(lax.axis_index("section") == 0, pair[0], pair[1])) & 1


def gather_square(blocks, order_pair, places, cuts):
    first, second = list(zip(*order_pair))[:2]
    a, b = own_bit(first), own_bit(second)
    kept = lax.dynamic_index_in_dim(blocks, a, 0, keepdims=False)
    arrived = yield lax.dynamic_index_in_dim(blocks, 1 - a, 0, keepdims=False), first, None
    held = jnp.stack([kept, arrived])
    kept = lax.dynamic_index_in_dim(held, b, 1, keepdims=False)
    arrived = yield lax.dynamic_index_in_dim(held, 1 - b, 1, keepdims=False), second, None
    parts = yield from doubling(jnp.concatenate([kept, arrived], axis=0), order_pair, 2)
    return assembled(parts, placement(order_pair, places), cuts)


def total_of(terms):
    return sum(term.astype(F32) for term in terms)


def halving(send, kept, order_pair, last=0):
    terms, outgoing = [kept], send
    for bits in reversed(list(zip(*order_pair))[last:]):
        if outgoing is None:
            half = terms[0].shape[0] // 2
            outgoing = total_of([term[half:] for term in terms]).astype(BF16)
            terms = [term[:half] for term in terms]
        arrived = yield outgoing, bits, None
        terms, outgoing = terms + [arrived], None
    return terms


def scatter_all(halves, order_pair):
    terms = yield from halving(*halves, order_pair)
    return total_of(terms)[0].astype(BF16)


def scatter_core(grad, order_pair, places, size):
    halves = split_stack([grad], placement(order_pair, places), 1 << len(places))
    terms = yield from halving(*halves, order_pair)
    top = bit_count(size) - 1
    sends = top_sends(size)
    arrived = yield total_of(terms)[0].astype(BF16), (top, top), lambda core, i: not sends(core, i)
    return (total_of(terms)[0] + arrived.astype(F32)).astype(BF16)


def scatter_square(grad, order_pair, places):
    halves = split_stack([grad], placement(order_pair, places), 1 << len(places))
    terms = yield from halving(*halves, order_pair, 2)
    held = total_of(terms).astype(BF16)
    first, second = list(zip(*order_pair))[:2]
    arrived = yield held[2:], second, None
    held = jnp.stack([held[:2], arrived])
    arrived = yield held[:, 1], first, None
    return jnp.stack([held[:, 0], arrived])


def scatter_small(vector, size):
    position = lax.axis_index("dp")
    held = vector.reshape(size // 4, 4, vector.shape[2])
    for count, low in ((4, 0), (size // 4, 2)):
        own = (position >> low) & (count - 1)

        def part(index):
            return lax.dynamic_index_in_dim(held, index, 1 if low == 0 else 0, keepdims=False)

        outgoing = tuple(part(own ^ other) for other in range(1, count))
        arrived = yield outgoing, tuple(other << low for other in range(1, count)), "flips"
        held = part(own) + sum(arrived)
    return held


def in_square(blocks):
    is_first = lax.axis_index("section") == 0
    middle = jnp.where(is_first, blocks[1:3], jnp.stack([blocks[2], blocks[1]]))
    return jnp.concatenate([blocks[:1], middle, blocks[3:]], axis=0)


SQUARE = ((0, 1), (1, 0))


def gather_in_square(rows):
    held = rows[None]
    for bits in SQUARE:
        arrived = yield held, bits, None
        held = jnp.concatenate([held, arrived], axis=0)
    return in_square(held)


def scatter_in_square(blocks):
    held = in_square(blocks)
    for bits in reversed(SQUARE):
        half = held.shape[0] // 2
        arrived = yield held[half:].astype(BF16), bits, None
        held = held[:half] + arrived.astype(F32)
    return held[0]


def local(
    size,
    bytes_in,
    lengths,
    patch_index,
    patch_count,
    gain_l1,
    qkv_l,
    out_l,
    gain_l2,
    up_l,
    down_l,
    patch_proj,
    gain_g1,
    qkv_g,
    out_g,
    gain_g2,
    up_g,
    down_g,
    out_grad,
):
    core = lax.axis_index("section")
    position = lax.axis_index("dp")
    is_first = core == 0
    seq_rows, half_l = bytes_in.shape[1:]
    width_l, width_g = 2 * half_l, out_g.shape[1]
    half_g = width_g // 2
    rows_l, rows_g = out_l.shape[0], out_g.shape[0]
    units_l, units_g = down_l.shape[0], down_g.shape[0]
    head_l, head_g = width_l // H_L, width_g // H_G
    micro_total, slot_total = patch_index.shape[1:]
    slots = micro_total * slot_total
    bits = bit_count(size)
    every = tuple(range(bits))

    def joined(mine, theirs, axis=1):
        low = jnp.where(is_first, mine, theirs)
        high = jnp.where(is_first, theirs, mine)
        return jnp.concatenate([low, high], axis=axis)

    def shared(mine, axis=1):
        return joined(mine, swap(mine), axis)

    def half_of(array, which, axis=1):
        length = array.shape[axis] // 2
        return lax.dynamic_slice_in_dim(array, which * length, length, axis)

    def slope_of(upward):
        return jax.vjp(jax.nn.gelu, upward)[1](jnp.ones_like(upward))[0]

    def summed_cores(part):
        part = part.astype(BF16)
        return part.astype(F32) + swap(part).astype(F32)

    def own_heads(weight):
        return jnp.concatenate([half_of(third, core) for third in jnp.split(weight, 3, axis=1)], axis=1)

    def square_columns(weight):
        pieces = jnp.split(weight, size // 2, axis=1)
        return [jnp.concatenate(pieces[k::4], axis=1) for k in range(4)]

    def gain_block():
        columns = [gain.reshape(rows_l, -1) for gain in (gain_l1, gain_l2, gain_g1, gain_g2)]
        block = jnp.concatenate(columns, axis=1)
        return jnp.pad(block, ((0, 0), (0, TILE - block.shape[1])))

    top_first = [(bits - 1,) + o for o in orders(size, (None, -1, -2))]
    mixed = orders(size, (-1, None, -2))
    lows_last = orders(size, (None, -1, -2))
    plane = [o[:2] + (bits - 1,) + o[2:] for o in orders(size, (-1, -2, None))]
    line = orders(size, (None,))
    below, beyond = tuple(range(bits - 1)), tuple(range(2, bits - 1))

    fresh = functools.partial(Stream, size)
    up_width, qkv_width = up_l.shape[1] // 2, 3 * half_g
    square_units = units_g * (size // 8)
    table = placement(top_first, every)
    between = [
        (bits - 1,) + orders(size, middle)[which] for which, middle in enumerate(((None, -1, -2), (-1, None, -2)))
    ]
    places_g = placement(between, every)
    side_l = half_l + half_g
    stream_l = fresh(
        gather_all(
            jnp.concatenate(
                [half_of(out_l, core), half_of(patch_proj, core), gain_block(), own_heads(qkv_l), half_of(up_l, core)],
                axis=1,
            ),
            top_first,
            True,
        )
    )
    stream_down_l = fresh(gather_core(down_l, lows_last, below))
    stream_g = fresh(gather_all(own_heads(qkv_g), top_first, False))
    stream_out_g = fresh(gather_all(half_of(out_g, core), top_first, False))
    square = square_columns(half_of(up_g, core))
    one_two = jnp.where(is_first, square[2], square[1])
    two_one = jnp.where(is_first, square[1], square[2])
    blocks = jnp.stack([square[0], one_two, two_one, square[3]]).reshape(2, 2, rows_g, square_units)
    stream_up_g = fresh(gather_square(blocks, plane, every, [(0, rows_g, 0, square_units)]))
    stream_down_g = fresh(
        gather_core(down_g[:, :width_l], line, beyond)
    )

    bias_l = jnp.where(jnp.arange(seq_rows) < lengths[0], 0.0, NEG).astype(F32)[:, None]
    live = (jnp.arange(slot_total)[None, :] < patch_count[0][:, None]).reshape(slots)
    bias_g = jnp.where(live, 0.0, NEG).astype(F32)[:, None]
    positions = patch_index[0].reshape(slots)
    picks = positions[:, None] == jnp.arange(seq_rows)[None, :]
    picks_live = (picks & live[:, None]).astype(BF16)
    picks = picks.astype(BF16)

    advance([stream_l], ())
    seq_inputs = shared(bytes_in[0])
    inputs = seq_inputs.astype(F32)
    scale_l1 = row_scale(inputs)
    seq_grads = shared(out_grad[0])
    grad_top_b = mm(picks_live, seq_grads).astype(BF16)
    scale_l1 = advance([stream_l, stream_up_g, stream_down_l, stream_g], scale_l1)
    stream_top = fresh(gather_in_square(half_of(grad_top_b, core)))
    grad_top_b = advance([stream_l, stream_up_g, stream_down_l, stream_top], grad_top_b)
    advance([stream_l, stream_g, stream_top, stream_out_g], ())

    advance([stream_l, stream_g, stream_down_l, stream_up_g, stream_down_g, stream_top, stream_out_g], ())
    parts = stream_l.result()
    front = side_l + TILE
    out_wl, proj_w, gains = assembled_fours(
        parts,
        table,
        [(0, rows_l, 0, half_l), (0, rows_l, half_l, side_l), (0, rows_l, side_l, side_l + LANES)],
        front,
        LONG,
    )
    qkv_wl = Weight(parts, table, front, 3 * half_l)
    up_wl = Weight(parts, table, front + 3 * half_l, up_width)
    gain_one_l, gain_two_l = gains[:, 0].astype(F32), gains[:, 1].astype(F32)
    per = width_g // width_l
    gain_one_g, gain_two_g = (
        gains[:, low : low + per].reshape(width_g).astype(F32) for low in (2, 2 + per)
    )
    normed_l = (inputs * scale_l1 * gain_one_l).astype(BF16)
    projected_l = qkv_wl.product(normed_l)
    mixture_l, lse_l = attention_forward(projected_l, bias_l, head_l)
    mixture_l, out_wl, proj_w = advance(
        [stream_down_l, stream_up_g, stream_down_g, stream_out_g], (mixture_l, out_wl, proj_w), [stream_up_g]
    )
    mixture_l = advance([stream_g], mixture_l)
    mixture_l, out_wl = shared(mixture_l), shared(out_wl)
    out_own_l = half_of(out_wl, core, 0)
    hidden_l = inputs + mm(mixture_l, out_wl)
    scale_l2 = row_scale(hidden_l)
    normed_l2 = (hidden_l * scale_l2 * gain_two_l).astype(BF16)
    activated_l, slope_l = up_wl.product(normed_l2, gelu=True)
    activated_l, proj_w = advance(
        [stream_down_l, stream_down_g, stream_out_g, stream_up_g], (activated_l, proj_w), [stream_out_g]
    )
    proj_w = shared(proj_w)
    (down_wl,) = stream_down_l.result()
    partial_l = mm(activated_l, down_wl)
    local_out = half_of(hidden_l, core) + half_of(partial_l, core) + swap(half_of(partial_l, 1 - core))

    boundary = shared(mm(picks, local_out.astype(BF16)).astype(BF16))
    start_rows = mm(boundary, proj_w)
    scale_g1 = row_scale(start_rows)
    square_top = shared(stream_top.result().reshape(4 * slots, half_l))
    scale_g1, square_top = advance([stream_g, stream_out_g, stream_up_g], (scale_g1, square_top))
    qkv_wg = Weight(stream_g.result(), table, 0, qkv_width)
    normed_g = (start_rows * scale_g1 * gain_one_g).astype(BF16)
    projected_g = qkv_wg.product(normed_g)
    mixture_g, lse_g = attention_forward(projected_g, bias_g, head_g)
    mixture_g = advance([stream_out_g], mixture_g)
    (out_wg,) = assembled_fours(stream_out_g.result(), table, [(0, rows_g, 0, half_g)])
    out_theirs_g = swap(out_wg)
    mixture_g = shared(mixture_g)
    hidden_g = start_rows + joined(mm(mixture_g, out_wg), mm(mixture_g, out_theirs_g))
    scale_g2 = row_scale(hidden_g)
    normed_g2 = (hidden_g * scale_g2 * gain_two_g).astype(BF16)
    square_normed = fresh(gather_in_square(half_of(normed_g2, core))).result()
    square_normed = shared(square_normed.reshape(4 * slots, half_g))
    (up_wg,) = stream_up_g.result()
    (down_wg,) = stream_down_g.result()
    upward_g = mm(square_normed, up_wg)
    activated_g = jax.nn.gelu(upward_g).astype(BF16)

    grad_down_g = mm_tn(activated_g, square_top).astype(BF16)
    stream_down_g = fresh(scatter_core(grad_down_g, line, beyond, size))
    grad_act_g = mm_nt(square_top, down_wg)
    grad_up_g_rows = jax.vjp(jax.nn.gelu, upward_g)[1](grad_act_g)[0].astype(BF16)
    grad_up_g = mm_tn(square_normed, grad_up_g_rows).astype(BF16)
    stream_up_g = fresh(scatter_square(grad_up_g, plane, every))
    part = mm_nt(grad_up_g_rows, up_wg)
    part = half_of(part, core) + swap(half_of(part, 1 - core).astype(BF16)).astype(F32)
    part = advance([stream_down_g, stream_up_g], part)
    part = shared(fresh(scatter_in_square(part.reshape(4, slots, half_g))).result())
    pulled, grad_gain_g2 = norm_backward(part, hidden_g, scale_g2, gain_two_g)
    grad_hidden_g = jnp.pad(grad_top_b.astype(F32), ((0, 0), (0, width_g - width_l))) + pulled
    grad_hidden_gb = grad_hidden_g.astype(BF16)
    mine_gb, theirs_gb = half_of(grad_hidden_gb, core), half_of(grad_hidden_gb, 1 - core)
    grad_out_g = mm_tn(mixture_g, mine_gb).astype(BF16)
    stream_out_g = fresh(scatter_all(split_stack([grad_out_g], table, size), top_first))
    grad_mixture_g = (
        mm_nt(mine_gb, half_of(out_wg, core, 0)) + mm_nt(theirs_gb, half_of(out_theirs_g, core, 0))
    ).astype(BF16)
    partial_g = mm(activated_g, down_wg)
    partial_g = half_of(partial_g, core) + swap(half_of(partial_g, 1 - core).astype(BF16)).astype(F32)
    stream_out = fresh(scatter_in_square(partial_g.reshape(4, slots, half_l)))
    grad_mixture_g = advance([stream_down_g, stream_out_g, stream_out], grad_mixture_g)
    grad_projected_g = attention_backward(projected_g, bias_g, lse_g, grad_mixture_g, head_g)
    part, halves = qkv_wg.pullback(normed_g, grad_projected_g, places_g)
    stream_g = fresh(scatter_all(halves, between))
    part = advance([stream_g, stream_out, stream_out_g, stream_up_g], part)
    part = summed_cores(part)
    pulled, grad_gain_g1 = norm_backward(part, start_rows, scale_g1, gain_one_g)
    grad_start = (grad_hidden_g + pulled).astype(BF16)
    grad_proj = mm_tn(boundary, half_of(grad_start, core)).astype(BF16)

    grad_rows = mm_nt(grad_start, proj_w).astype(BF16)
    grad_local = seq_grads.astype(F32) + mm_tn(picks, grad_rows)
    grad_local_b = grad_local.astype(BF16)
    grad_down_l = mm_tn(activated_l, grad_local_b).astype(BF16)
    stream_down_l = fresh(scatter_core(grad_down_l, mixed, below, size))
    grad_act_l = mm_nt(grad_local_b, down_wl)
    grad_up_l_rows = (slope_l.astype(F32) * grad_act_l).astype(BF16)
    part, up_halves = up_wl.pullback(normed_l2, [grad_up_l_rows], table, side_l)
    part, up_halves = advance([stream_down_g, stream_up_g, stream_g, stream_out_g], (part, up_halves))
    part = summed_cores(part)
    pulled, grad_gain_l2 = norm_backward(part, hidden_l, scale_l2, gain_two_l)
    grad_hidden_l = grad_local + pulled
    grad_hidden_lb = grad_hidden_l.astype(BF16)
    grad_out_l = mm_tn(mixture_l, half_of(grad_hidden_lb, core)).astype(BF16)
    stream_up_l = fresh(scatter_all(split_stack([grad_out_l, grad_proj], table, size, up_halves), top_first))
    grad_mixture_l = mm_nt(grad_hidden_lb, out_own_l).astype(BF16)
    grad_mixture_l = advance([stream_g, stream_down_l, stream_up_l], grad_mixture_l)
    grad_projected_l = attention_backward(projected_l, bias_l, lse_l, grad_mixture_l, head_l)
    grad_projected_l = advance([stream_g, stream_out_g, stream_up_g], grad_projected_l)
    part, halves = qkv_wl.pullback(normed_l, grad_projected_l, table)
    stream_qkv_l = fresh(scatter_all(halves, top_first))
    part = advance([stream_up_l, stream_down_l, stream_qkv_l], part)
    part = summed_cores(part)
    pulled, grad_gain_l1 = norm_backward(part, inputs, scale_l1, gain_one_l)
    input_grad = half_of(grad_hidden_l + pulled, core).astype(BF16)[None]
    gains = jnp.concatenate(
        [
            grad.reshape(size, 1, grad.shape[0] // size)
            for grad in (grad_gain_l1, grad_gain_l2, grad_gain_g1, grad_gain_g2)
        ],
        axis=2,
    )
    returned = half_of(hidden_g[:, :width_l], core) + stream_out.result()
    hidden_out = (local_out + mm_tn(picks_live, returned.astype(BF16))).astype(BF16)[None]
    input_grad, gains = advance(
        [stream_qkv_l, stream_up_l, stream_down_l, stream_up_g, stream_out_g, stream_g], (input_grad, gains)
    )
    stream_gains = fresh(scatter_small(gains, size))
    advance([stream_qkv_l, stream_gains], ())
    advance([stream_up_l, stream_down_l, stream_gains], ())
    advance([stream_qkv_l, stream_gains], ())
    advance([stream_up_l, stream_qkv_l, stream_down_l], ())

    def joined_columns(mine, theirs):
        return joined(mine, theirs).astype(F32)

    def joined_heads(mine, theirs):
        low, high = jnp.where(is_first, mine, theirs), jnp.where(is_first, theirs, mine)
        thirds = [jnp.split(part, 3, axis=1) for part in (low, high)]
        return jnp.concatenate([part for pair in zip(*thirds) for part in pair], axis=1).astype(F32)

    def from_owner(mine, theirs):
        return jnp.where((position >> (bits - 1)) == core, mine, theirs).astype(F32)

    def in_order(blocks):
        low = own_bit((0, 0)), own_bit((1, 1))
        rows, width = blocks.shape[2:]
        placed = []
        for y in range(2):
            for x in range(2):
                dx, dy = x ^ low[0], y ^ low[1]
                index = jnp.where(is_first, 2 * dx + dy, 2 * dy + dx)
                placed.append(lax.dynamic_index_in_dim(blocks.reshape(4, rows, width), index, 0, keepdims=False))
        pieces = [jnp.split(part, size // 8, axis=1) for part in placed]
        return jnp.concatenate([piece for group in zip(*pieces) for piece in group], axis=1)

    down_g_mine = stream_down_g.result()
    total_down_g = from_owner(down_g_mine, swap(down_g_mine))
    total_down_g = jnp.pad(total_down_g, ((0, 0), (0, width_g - width_l)))
    up_g_mine = in_order(stream_up_g.result())
    total_up_g = joined_columns(up_g_mine, swap(up_g_mine))
    g_mine = stream_g.result()
    total_qkv_g = joined_heads(g_mine, swap(g_mine))
    out_g_mine = stream_out_g.result()
    total_out_g = joined_columns(out_g_mine, swap(out_g_mine))
    down_l_mine = stream_down_l.result()
    total_down_l = from_owner(down_l_mine, swap(down_l_mine))
    l_mine = stream_up_l.result()
    l_theirs = swap(l_mine)
    cuts = [0, half_l, side_l, side_l + up_width]
    total_out_l, total_proj, total_up_l = (
        joined_columns(l_mine[:, low:high], l_theirs[:, low:high]) for low, high in zip(cuts, cuts[1:])
    )
    q_mine = stream_qkv_l.result()
    total_qkv_l = joined_heads(q_mine, swap(q_mine))
    gains = stream_gains.result()
    gains = jnp.where(is_first, gains, lax.ppermute(gains, "section", [(0, 1)]))
    total_gain_l1 = gains[:rows_l]
    total_gain_l2 = gains[rows_l : 2 * rows_l]
    total_gain_g1 = gains[2 * rows_l : 2 * rows_l + rows_g]
    total_gain_g2 = gains[2 * rows_l + rows_g :]
    return (
        hidden_out,
        input_grad,
        total_gain_l1,
        total_qkv_l,
        total_out_l,
        total_gain_l2,
        total_up_l,
        total_down_l,
        total_proj,
        total_gain_g1,
        total_qkv_g,
        total_out_g,
        total_gain_g2,
        total_up_g,
        total_down_g,
    )


def solution(mesh):
    rows, vector = P("dp", None), P("dp")
    features = P("dp", None, "section")
    in_specs = (
        features,
        vector,
        P("dp", None, None),
        rows,
        vector,
        rows,
        rows,
        vector,
        rows,
        rows,
        rows,
        vector,
        rows,
        rows,
        vector,
        rows,
        rows,
        features,
    )
    out_specs = (
        features,
        features,
        vector,
        rows,
        rows,
        vector,
        rows,
        rows,
        rows,
        vector,
        rows,
        rows,
        vector,
        rows,
        rows,
    )
    return jax.shard_map(
        functools.partial(local, mesh.shape["dp"]),
        mesh=mesh,
        in_specs=in_specs,
        out_specs=out_specs,
        check_vma=False,
    )
```

```python
import functools

import jax
import jax.numpy as jnp
import numpy as np
from jax import lax
from jax.experimental import pallas as pl
from jax.experimental.pallas import tpu as pltpu
from jax.sharding import PartitionSpec as P

WINDOW = 1536
EPSILON = 1e-06
LANES = 128
GELU_SCALE = (2.0 / np.pi) ** 0.5
GELU_CUBE = 0.044715
NEG = -1e30
VMEM_LIMIT = 48 * 1024 * 1024
FREE = pl.CostEstimate(flops=0, bytes_accessed=0, transcendentals=0)
LONG = pl.CostEstimate(flops=10**11, bytes_accessed=0, transcendentals=0)
F32 = jnp.float32
BF16 = jnp.bfloat16


def mm(left, right):
    return jnp.dot(left, right, preferred_element_type=F32)


def mm_nt(left, right):
    return lax.dot_general(left, right, (((1,), (1,)), ((), ())), preferred_element_type=F32)


def mm_tn(left, right):
    return lax.dot_general(left, right, (((0,), (0,)), ((), ())), preferred_element_type=F32)


def row_scale(values):
    return lax.rsqrt(jnp.mean(values * values, axis=-1, keepdims=True) + EPSILON)


def norm_backward(grad_normed, values, scale, gain):
    grad_gain = jnp.sum(grad_normed * values * scale, axis=0)
    pulled = grad_normed * gain
    inner = jnp.mean(pulled * values, axis=-1, keepdims=True)
    return scale * pulled - values * (scale * scale * scale * inner), grad_gain


def query_block(rows):
    return 256 if rows % 256 == 0 else rows


def head_masks(block):
    lane = lax.broadcasted_iota(jnp.int32, (block, LANES), 1)
    return [lane < LANES // 2, lane >= LANES // 2]


def stacked(values, masks):
    return jnp.concatenate([jnp.where(mask, values, jnp.zeros_like(values)) for mask in masks], axis=0)


def first_lanes(values):
    lane = lax.broadcasted_iota(jnp.int32, (values[0].shape[0], LANES), 1)
    result = jnp.zeros(lane.shape, F32)
    for index, value in enumerate(values):
        result = jnp.where(lane == index, value, result)
    return result.astype(BF16)


def masked_scores(keys, biased, query, extended, bias, start, block, window):
    key_at = lax.broadcasted_iota(jnp.int32, (block, 2 * block), 0)
    query_at = lax.broadcasted_iota(jnp.int32, (block, 2 * block), 1)
    query_at = jnp.where(query_at < block, query_at, query_at - block)
    parts = []
    if start:
        before = mm_nt(biased[:start], extended)
        if window is not None:
            far = lax.broadcasted_iota(jnp.int32, (start, 2 * block), 0)
            own = lax.broadcasted_iota(jnp.int32, (start, 2 * block), 1)
            own = jnp.where(own < block, own, own - block) + start
            before = jnp.where(own - far < window, before, NEG)
        parts.append(before)
    diagonal = mm_nt(keys[start : start + block], query)
    masked = jnp.where(key_at < query_at, diagonal + bias[start : start + block], NEG)
    parts.append(jnp.where(key_at == query_at, diagonal, masked))
    return parts


def ranges(parts):
    low = 0
    for part in parts:
        yield low, low + part.shape[0], part
        low += part.shape[0]


def extend_keys(biased, k_ref, bias_ref):
    biased[:, :LANES] = k_ref[...]
    biased[:, LANES:] = first_lanes([bias_ref[...]])


def attention_forward_kernel(rows, window, q_ref, k_ref, v_ref, bias_ref, o_ref, lse_ref, biased, counted):
    block = query_block(rows)
    masks = head_masks(block)
    score_scale = (LANES // 2) ** (-0.5)
    lane = lax.broadcasted_iota(jnp.int32, (block, LANES), 1)
    extend_keys(biased, k_ref, bias_ref)
    for head, mask in enumerate(head_masks(rows)):
        counted[head] = jnp.where(mask, v_ref[...], jnp.ones_like(v_ref))
    one = first_lanes([jnp.ones((2 * block, 1), F32)])
    query_at = lax.broadcasted_iota(jnp.int32, (2 * block, block), 0)
    query_at = jnp.where(query_at < block, query_at, query_at - block)
    key_at = lax.broadcasted_iota(jnp.int32, (2 * block, block), 1)
    for index in range(rows // block):
        start = index * block
        query = stacked((q_ref[start : start + block, :] * score_scale).astype(BF16), masks)
        extended = jnp.concatenate([query, one], axis=1)
        parts = []
        if start:
            before = mm_nt(extended, biased[:start, :])
            if window is not None:
                far = lax.broadcasted_iota(jnp.int32, (2 * block, start), 1)
                own = lax.broadcasted_iota(jnp.int32, (2 * block, start), 0)
                own = jnp.where(own < block, own, own - block) + start
                before = jnp.where(own - far < window, before, NEG)
            parts.append(before)
        masked = jnp.where(key_at < query_at, mm_nt(extended, biased[start : start + block, :]), NEG)
        parts.append(jnp.where(key_at == query_at, mm_nt(query, k_ref[start : start + block, :]), masked))
        top = functools.reduce(jnp.maximum, [jnp.max(p, axis=1, keepdims=True) for p in parts])
        parts = [jnp.exp(p - top).astype(BF16) for p in parts]
        out, logs = jnp.zeros((block, LANES), F32), jnp.zeros((block, LANES), F32)
        for head, mask in enumerate(masks):
            span = slice(head * block, (head + 1) * block)
            mixed, low = jnp.zeros((block, LANES), F32), 0
            for part in parts:
                high = low + part.shape[1]
                mixed += mm(part[span], counted[head, low:high, :])
                low = high
            other = LANES // 2 if head == 0 else 0
            total = mixed[:, other : other + 1]
            out = jnp.where(mask, mixed * (1.0 / total), out)
            logs = jnp.where(lane == head, top[span] + jnp.log(total), logs)
        o_ref[start : start + block, :] = out.astype(BF16)
        lse_ref[0, :, start : start + block] = logs.T[:2]


def attention_backward_kernel(
    rows,
    window,
    q_ref,
    k_ref,
    v_ref,
    bias_ref,
    lse_ref,
    o_ref,
    do_ref,
    dq_ref,
    dk_ref,
    dv_ref,
    dk_acc,
    dv_acc,
    biased,
    reduced,
):
    block = query_block(rows)
    masks = head_masks(block)
    score_scale = (LANES // 2) ** (-0.5)
    extend_keys(biased, k_ref, bias_ref)
    reduced[:, :LANES] = v_ref[...]
    reduced[:, LANES:] = first_lanes([jnp.full((rows, 1), -1.0, F32)] * 2)
    one = first_lanes([jnp.ones((2 * block, 1), F32)])
    for index in reversed(range(rows // block)):
        start = index * block
        query = stacked((q_ref[start : start + block, :] * score_scale).astype(BF16), masks)
        extended = jnp.concatenate([query, one], axis=1)
        grad = stacked(do_ref[start : start + block, :], masks)
        mixed = o_ref[start : start + block, :].astype(F32)
        delta = jnp.sum(grad.astype(F32) * jnp.concatenate([mixed, mixed], axis=0), axis=1, keepdims=True)
        near = delta.astype(BF16).astype(F32)
        grad_extended = jnp.concatenate([grad, first_lanes([near, delta - near])], axis=1)
        lse = jnp.concatenate([lse_ref[0, head : head + 1, start : start + block] for head in range(2)], axis=1)
        parts = masked_scores(k_ref, biased, query, extended, bias_ref, start, block, window)
        turned = jnp.zeros((2 * block, LANES), F32)
        for low, high, part in ranges(parts):
            weights = jnp.exp(part - lse)
            change = (weights * mm_nt(reduced[low:high, :], grad_extended)).astype(BF16)
            dv = mm(weights.astype(BF16), grad)
            dk = mm(change, query)
            if index == rows // block - 1:
                dv_acc[low:high, :] = dv
                dk_acc[low:high, :] = dk
            else:
                dv_acc[low:high, :] += dv
                dk_acc[low:high, :] += dk
            turned += mm_tn(change, k_ref[low:high, :])
        dq = jnp.where(masks[0], turned[:block], turned[block:]) * score_scale
        dq_ref[start : start + block, :] = dq.astype(BF16)
    dk_ref[...] = dk_acc[...].astype(BF16)
    dv_ref[...] = dv_acc[...].astype(BF16)


def attention_specs(rows, width):
    pairs = width // LANES
    wide = lambda part: pl.BlockSpec((rows, LANES), lambda i, part=part: (0, part * pairs + i))
    bias = pl.BlockSpec((rows, 1), lambda i: (0, 0))
    return pairs, wide, bias


def attention_forward(projected, bias):
    rows, width = projected.shape[0], projected.shape[1] // 3
    pairs, wide, bias_spec = attention_specs(rows, width)
    window = WINDOW if rows > WINDOW else None
    return pl.pallas_call(
        functools.partial(attention_forward_kernel, rows, window),
        grid=(pairs,),
        in_specs=[wide(0), wide(1), wide(2), bias_spec],
        out_specs=[wide(0), pl.BlockSpec((1, 2, rows), lambda i: (i, 0, 0))],
        out_shape=[
            jax.ShapeDtypeStruct((rows, width), BF16),
            jax.ShapeDtypeStruct((pairs, 2, rows), F32),
        ],
        scratch_shapes=[pltpu.VMEM((rows, 2 * LANES), BF16), pltpu.VMEM((2, rows, LANES), BF16)],
        compiler_params=pltpu.CompilerParams(vmem_limit_bytes=VMEM_LIMIT),
        cost_estimate=FREE,
    )(projected, projected, projected, bias)


def attention_backward(projected, bias, lse, mixture, grad_mixture):
    rows, width = grad_mixture.shape
    pairs, wide, bias_spec = attention_specs(rows, width)
    window = WINDOW if rows > WINDOW else None
    shape = jax.ShapeDtypeStruct((rows, width), BF16)
    return pl.pallas_call(
        functools.partial(attention_backward_kernel, rows, window),
        grid=(pairs,),
        in_specs=[
            wide(0),
            wide(1),
            wide(2),
            bias_spec,
            pl.BlockSpec((1, 2, rows), lambda i: (i, 0, 0)),
            wide(0),
            wide(0),
        ],
        out_specs=[wide(0), wide(0), wide(0)],
        out_shape=[shape, shape, shape],
        scratch_shapes=[
            pltpu.VMEM((rows, LANES), F32),
            pltpu.VMEM((rows, LANES), F32),
            pltpu.VMEM((rows, 2 * LANES), BF16),
            pltpu.VMEM((rows, 2 * LANES), BF16),
        ],
        compiler_params=pltpu.CompilerParams(vmem_limit_bytes=VMEM_LIMIT),
        cost_estimate=LONG,
    )(projected, projected, projected, bias, lse, mixture, grad_mixture)


def swap(array):
    return lax.ppermute(array, "section", [(0, 1), (1, 0)])


def exchange(array, bits, size, sends=None):
    if sends == "flips":
        return tuple(
            lax.ppermute(part, "dp", [(i, i ^ flip) for i in range(size)]) for part, flip in zip(array, bits)
        )
    pairs = [
        (core * size + i, core * size + (i ^ (1 << bit)))
        for core, bit in enumerate(bits)
        for i in range(size)
        if sends is None or sends(core, i)
    ]
    return jax.tree.map(lambda part: lax.ppermute(part, ("section", "dp"), pairs), array)


def bit_count(size):
    return size.bit_length() - 1


def orders(size, middle):
    bits = bit_count(size)
    others = tuple(reversed(range(2, bits - 1)))
    result = []
    for core in range(2):
        lowest = (0, 1) if core == 0 else (1, 0)
        order = ()
        for entry in middle:
            order += others if entry is None else (lowest[0] if entry == -1 else lowest[1],)
        result.append(order)
    return result


def mask_of(index, order, places):
    return sum(((index >> t) & 1) << places.index(bit) for t, bit in enumerate(order))


def placement(order_pair, places):
    position = lax.axis_index("dp")
    own = sum(((position >> bit) & 1) << p for p, bit in enumerate(places))
    count = 1 << len(places)
    masks = [jnp.asarray([mask_of(j, order, places) for j in range(count)], jnp.int32) for order in order_pair]
    return (own ^ jnp.where(lax.axis_index("section") == 0, masks[0], masks[1])).astype(jnp.int32)


def aligned(rows, cuts=()):
    return rows % 16 == 0 and all(c % LANES == 0 and r % 16 == 0 for r0, r1, c0, c1 in cuts for r, c in ((r0, c0), (r1, c1)))


def assembly_kernel(bounds, cuts, table, *refs):
    step = pl.program_id(0)
    parts, outs = refs[: len(bounds)], refs[len(bounds) :]

    def store(ref):
        for (r0, r1, c0, c1), out in zip(cuts, outs):
            out[...] = ref[0, r0:r1, c0:c1]

    for (low, high), ref in zip(bounds, parts):
        pl.when((step >= low) & (step < high))(functools.partial(store, ref))


def assembled(parts, table, cuts, offset=0, width=None):
    rows = parts[0].shape[1]
    width = width or parts[0].shape[2]
    ends = np.cumsum([part.shape[0] for part in parts])
    count = int(ends[-1])
    bounds = [(int(end) - part.shape[0], int(end)) for end, part in zip(ends, parts)]
    shapes = [(count * (r1 - r0), c1 - c0) for r0, r1, c0, c1 in cuts]
    if not aligned(rows, cuts):
        stack = jnp.concatenate(parts, axis=0)[jnp.argsort(table)][..., offset : offset + width]
        return [stack[:, r0:r1, c0:c1].reshape(s) for (r0, r1, c0, c1), s in zip(cuts, shapes)]
    return pl.pallas_call(
        functools.partial(assembly_kernel, bounds, cuts),
        grid_spec=pltpu.PrefetchScalarGridSpec(
            num_scalar_prefetch=1,
            grid=(count,),
            in_specs=[
                pl.BlockSpec(
                    (1, rows, width),
                    lambda j, t, low=low, high=high: (jnp.clip(j, low, high - 1) - low, 0, offset // width),
                )
                for low, high in bounds
            ],
            out_specs=[pl.BlockSpec((r1 - r0, c1 - c0), lambda j, t: (t[j], 0)) for r0, r1, c0, c1 in cuts],
        ),
        out_shape=[jax.ShapeDtypeStruct(s, parts[0].dtype) for s in shapes],
        compiler_params=pltpu.CompilerParams(vmem_limit_bytes=VMEM_LIMIT),
        cost_estimate=FREE,
    )(table, *parts)


def quarters(parts):
    if len(parts) == 4:
        return [(part, 0) for part in parts]
    return [(part, k) for part in parts for k in range(2)]


def whole_kernel(cuts, table, *refs):
    quarter = refs[0].shape[0]
    for index in range(4 * quarter):
        part, place = refs[index // quarter], table[index]
        for (r0, r1, c0, c1), out in zip(cuts, refs[4:]):
            rows = r1 - r0
            out[pl.ds(pl.multiple_of(place * rows, 16), rows), :] = part[index % quarter, r0:r1, c0:c1]


def assembled_fours(parts, table, cuts, width=None, cost=FREE):
    rows = parts[0].shape[1]
    width = width or parts[0].shape[2]
    count = sum(part.shape[0] for part in parts)
    shapes = [(count * (r1 - r0), c1 - c0) for r0, r1, c0, c1 in cuts]
    if not aligned(rows, cuts):
        stack = jnp.concatenate(parts, axis=0)[jnp.argsort(table)]
        return [stack[:, r0:r1, c0:c1].reshape(s) for (r0, r1, c0, c1), s in zip(cuts, shapes)]
    return pl.pallas_call(
        functools.partial(whole_kernel, cuts),
        grid_spec=pltpu.PrefetchScalarGridSpec(
            num_scalar_prefetch=1,
            grid=(1,),
            in_specs=[pl.BlockSpec((count // 4, rows, width), lambda j, t, k=k: (k, 0, 0)) for _, k in quarters(parts)],
            out_specs=[pl.BlockSpec(shape, lambda j, t: (0, 0)) for shape in shapes],
        ),
        out_shape=[jax.ShapeDtypeStruct(s, parts[0].dtype) for s in shapes],
        compiler_params=pltpu.CompilerParams(vmem_limit_bytes=VMEM_LIMIT),
        cost_estimate=cost,
    )(table, *[part for part, _ in quarters(parts)])


def split_kernel(half, count, table, *refs):
    step = pl.program_id(0)
    send, keep = refs[-2:]

    def store(out):
        base = 0
        for ref in refs[:count]:
            width = ref.shape[1]
            out[0, :, base : base + width] = ref[...]
            base += width

    pl.when(step < half)(lambda: store(send))
    pl.when(step >= half)(lambda: store(keep))


def split_stack(grads, table, count, into=None):
    half, rows = count // 2, grads[0].shape[0] // count
    width = sum(grad.shape[1] for grad in grads)
    if not (aligned(rows) and all(grad.shape[1] % LANES == 0 for grad in grads)):
        stack = jnp.concatenate([grad.reshape(count, rows, grad.shape[1]) for grad in grads], axis=2)[table]
        halves = [stack[half:], stack[:half]]
        if into is not None:
            halves = [jnp.concatenate([part, old[..., width:]], axis=2) for part, old in zip(halves, into)]
        return halves
    full = width if into is None else into[0].shape[2]
    shape = jax.ShapeDtypeStruct((half, rows, full), BF16)
    into = [] if into is None else list(into)
    return pl.pallas_call(
        functools.partial(split_kernel, half, len(grads)),
        grid_spec=pltpu.PrefetchScalarGridSpec(
            num_scalar_prefetch=1,
            grid=(count,),
            in_specs=[
                pl.BlockSpec((rows, grad.shape[1]), lambda j, t: (t[jnp.where(j < half, j + half, j - half)], 0))
                for grad in grads
            ]
            + [pl.BlockSpec(memory_space=pl.ANY) for _ in into],
            out_specs=[
                pl.BlockSpec((1, rows, width), lambda j, t: (jnp.minimum(j, half - 1), 0, 0)),
                pl.BlockSpec((1, rows, width), lambda j, t: (jnp.maximum(j - half, 0), 0, 0)),
            ],
        ),
        out_shape=[shape, shape],
        input_output_aliases={1 + len(grads) + k: k for k in range(len(into))},
        compiler_params=pltpu.CompilerParams(vmem_limit_bytes=VMEM_LIMIT),
        cost_estimate=FREE,
    )(table, *grads, *into)


def write_rows(target, parts, table, rows):
    index = 0
    for part in parts:
        for k in range(part.shape[0]):
            target[pl.ds(pl.multiple_of(table[index] * rows, 16), rows), :] = part[k]
            index += 1


def product_kernel(rows, count, gelu, table, x_ref, *refs):
    parts, outs, weight = refs[:count], refs[count:-1], refs[-1]
    write_rows(weight, parts, table, rows)
    result = jnp.dot(x_ref[...], weight[...], preferred_element_type=F32)
    if not gelu:
        outs[0][...] = result.astype(outs[0].dtype)
        return
    square = result * result
    bend = jnp.tanh(GELU_SCALE * (result + GELU_CUBE * (result * square)))
    outs[0][...] = (0.5 * result * (1.0 + bend)).astype(outs[0].dtype)
    slope = 0.5 * (1.0 + bend)
    slope += (0.5 * GELU_SCALE) * result * (1.0 - bend * bend) * (1.0 + (3.0 * GELU_CUBE) * square)
    outs[1][...] = slope.astype(outs[1].dtype)


def outer_kernel(rows, bounds, places, x_ref, *refs):
    grads, (send, keep, weight, turned) = refs[: len(bounds)], refs[len(bounds) :]
    step = pl.program_id(0)

    @pl.when(step == 0)
    def _():
        turned[...] = x_ref[...].T

    grad = grads[-1][...]
    for (low, high), ref in list(zip(bounds, grads))[:-1]:
        grad = jnp.where((step >= low) & (step < high), ref[...], grad)
    weight[...] = mm(turned[...], grad).astype(BF16)
    half = keep.shape[0]
    for index in range(2 * half):
        block = weight[pl.ds(pl.multiple_of(places[index] * rows, 16), rows), :]
        (keep if index < half else send)[index % half] = block


def inner_kernel(rows, bounds, table, *refs):
    parts, grads, (dx_ref, weight, total) = refs[:4], refs[4 : 4 + len(bounds)], refs[4 + len(bounds) :]
    step = pl.program_id(0)

    @pl.when(step == 0)
    def _():
        total[...] = jnp.zeros_like(total)

    write_rows(weight, parts, table, rows)
    grad = grads[-1][...]
    for (low, high), ref in list(zip(bounds, grads))[:-1]:
        grad = jnp.where((step >= low) & (step < high), ref[...], grad)
    total[...] += mm_nt(grad, weight[...])

    @pl.when(step == pl.num_programs(0) - 1)
    def _():
        dx_ref[...] = total[...].astype(BF16)


def pullback_kernel(rows, count, bounds, table, places, x_ref, *refs):
    parts, grads = refs[:count], refs[count : count + len(bounds)]
    dx_ref, send, keep, weight, turned, total = refs[count + len(bounds) :]
    step = pl.program_id(0)

    @pl.when(step == 0)
    def _():
        turned[...] = x_ref[...].T
        total[...] = jnp.zeros_like(total)

    write_rows(weight, parts, table, rows)
    grad = grads[-1][...]
    for (low, high), ref in list(zip(bounds, grads))[:-1]:
        grad = jnp.where((step >= low) & (step < high), ref[...], grad)
    total[...] += lax.dot_general(grad, weight[...], (((1,), (1,)), ((), ())), preferred_element_type=F32)
    weight[...] = jnp.dot(turned[...], grad, preferred_element_type=F32).astype(BF16)
    half = keep.shape[0]
    for index in range(2 * half):
        block = weight[pl.ds(pl.multiple_of(places[index] * rows, 16), rows), :]
        (keep if index < half else send)[index % half] = block

    @pl.when(step == pl.num_programs(0) - 1)
    def _():
        dx_ref[...] = total[...].astype(BF16)


def feed_forward_kernel(rows, table, places, x_ref, grad_ref, down_ref, slope_ref, act_ref, *refs):
    parts, (dx_ref, down_out, send, keep, weight, turned, total) = refs[:4], refs[4:]
    step = pl.program_id(0)

    @pl.when(step == 0)
    def _():
        turned[...] = x_ref[...].T
        total[...] = jnp.zeros_like(total)

    grad = grad_ref[...]
    change = (mm_nt(grad, down_ref[...]) * slope_ref[...].astype(F32)).astype(BF16)
    down_out[...] = mm_tn(act_ref[...], grad).astype(BF16)
    write_rows(weight, parts, table, rows)
    total[...] += mm_nt(change, weight[...])
    weight[...] = mm(turned[...], change).astype(BF16)
    half = keep.shape[0]
    for index in range(2 * half):
        block = weight[pl.ds(pl.multiple_of(places[index] * rows, 16), rows), :]
        (keep if index < half else send)[index % half] = block

    @pl.when(step == pl.num_programs(0) - 1)
    def _():
        dx_ref[...] = total[...].astype(BF16)


TILE = 384


class Weight:
    def __init__(self, parts, table, offset, width):
        self.parts, self.table, self.offset, self.width = parts, table, offset, width
        self.rows = parts[0].shape[1]
        self.count = sum(part.shape[0] for part in parts)
        self.aligned = aligned(self.rows) and offset % TILE == 0 and width % TILE == 0

    def whole(self):
        cut = (0, self.rows, 0, self.width)
        stack = jnp.concatenate(self.parts, axis=0)[jnp.argsort(self.table)]
        return stack[..., self.offset : self.offset + self.width].reshape(-1, self.width)

    def part_specs(self):
        first = self.offset // TILE
        return [
            pl.BlockSpec((self.count // 4, self.rows, TILE), lambda i, *tables, k=k: (k, 0, first + i))
            for _, k in quarters(self.parts)
        ]

    def product(self, x, gelu=False):
        if not self.aligned:
            result = mm(x, self.whole())
            if not gelu:
                return result.astype(BF16)
            slope = jax.vjp(jax.nn.gelu, result)[1](jnp.ones_like(result))[0]
            return jax.nn.gelu(result).astype(BF16), slope.astype(BF16)
        tokens, depth = x.shape
        outs = 2 if gelu else 1
        shape = jax.ShapeDtypeStruct((tokens, self.width), BF16)
        results = pl.pallas_call(
            functools.partial(product_kernel, self.rows, 4, gelu),
            grid_spec=pltpu.PrefetchScalarGridSpec(
                num_scalar_prefetch=1,
                grid=(self.width // TILE,),
                in_specs=[pl.BlockSpec((tokens, depth), lambda i, t: (0, 0))] + self.part_specs(),
                out_specs=[pl.BlockSpec((tokens, TILE), lambda i, t: (0, i))] * outs,
                scratch_shapes=[pltpu.VMEM((depth, TILE), BF16)],
            ),
            out_shape=[shape] * outs,
            compiler_params=pltpu.CompilerParams(vmem_limit_bytes=VMEM_LIMIT),
            cost_estimate=LONG if gelu else FREE,
        )(self.table, x, *[part for part, _ in quarters(self.parts)])
        return results if gelu else results[0]

    def feed_forward_pullback(self, x, grad, down, slope, activated, places, lead):
        if not self.aligned or down.shape[0] != self.width:
            change = (slope.astype(F32) * mm_nt(grad, down)).astype(BF16)
            dx, halves = self.pullback(x, [change], places, lead)
            return dx, mm_tn(activated, grad).astype(BF16), halves
        tokens, depth = x.shape
        half = jax.ShapeDtypeStruct((self.count // 2, self.rows, lead + self.width), BF16)
        half_spec = pl.BlockSpec((self.count // 2, self.rows, TILE), lambda i, t, p: (0, 0, lead // TILE + i))
        full = pl.BlockSpec((tokens, depth), lambda i, t, p: (0, 0))
        units = pl.BlockSpec((tokens, TILE), lambda i, t, p: (0, i))
        unit_rows = pl.BlockSpec((TILE, depth), lambda i, t, p: (i, 0))
        result = pl.pallas_call(
            functools.partial(feed_forward_kernel, self.rows),
            grid_spec=pltpu.PrefetchScalarGridSpec(
                num_scalar_prefetch=2,
                grid=(self.width // TILE,),
                in_specs=[full, full, unit_rows, units, units] + self.part_specs(),
                out_specs=[full, unit_rows, half_spec, half_spec],
                scratch_shapes=[
                    pltpu.VMEM((depth, TILE), BF16),
                    pltpu.VMEM((depth, tokens), BF16),
                    pltpu.VMEM((tokens, depth), F32),
                ],
            ),
            out_shape=[jax.ShapeDtypeStruct((tokens, depth), BF16), jax.ShapeDtypeStruct(down.shape, BF16), half, half],
            compiler_params=pltpu.CompilerParams(vmem_limit_bytes=VMEM_LIMIT),
            cost_estimate=FREE,
        )(self.table, places, x, grad, down, slope, activated, *[part for part, _ in quarters(self.parts)])
        return result[0], result[1], result[2:]

    def grad_specs(self, tokens, grads):
        ends = np.cumsum([grad.shape[1] // TILE for grad in grads])
        bounds = [(int(end) - grad.shape[1] // TILE, int(end)) for end, grad in zip(ends, grads)]
        specs = [
            pl.BlockSpec((tokens, TILE), lambda i, t, low=low, high=high: (0, jnp.clip(i, low, high - 1) - low))
            for low, high in bounds
        ]
        return bounds, specs

    def outer(self, x, grads, places):
        if not self.aligned:
            return split_stack([mm_tn(x, jnp.concatenate(grads, axis=1)).astype(BF16)], places, self.count)
        tokens, depth = x.shape
        bounds, specs = self.grad_specs(tokens, grads)
        half = jax.ShapeDtypeStruct((self.count // 2, self.rows, self.width), BF16)
        half_spec = pl.BlockSpec((self.count // 2, self.rows, TILE), lambda i, t: (0, 0, i))
        return pl.pallas_call(
            functools.partial(outer_kernel, self.rows, bounds),
            grid_spec=pltpu.PrefetchScalarGridSpec(
                num_scalar_prefetch=1,
                grid=(self.width // TILE,),
                in_specs=[pl.BlockSpec((tokens, depth), lambda i, t: (0, 0))] + specs,
                out_specs=[half_spec, half_spec],
                scratch_shapes=[pltpu.VMEM((depth, TILE), BF16), pltpu.VMEM((depth, tokens), BF16)],
            ),
            out_shape=[half, half],
            compiler_params=pltpu.CompilerParams(vmem_limit_bytes=VMEM_LIMIT),
            cost_estimate=FREE,
        )(places, x, *grads)

    def inner(self, grads):
        if not self.aligned:
            return mm_nt(jnp.concatenate(grads, axis=1), self.whole()).astype(BF16)
        tokens, depth = grads[0].shape[0], self.rows * self.count
        bounds, specs = self.grad_specs(tokens, grads)
        return pl.pallas_call(
            functools.partial(inner_kernel, self.rows, bounds),
            grid_spec=pltpu.PrefetchScalarGridSpec(
                num_scalar_prefetch=1,
                grid=(self.width // TILE,),
                in_specs=self.part_specs() + specs,
                out_specs=pl.BlockSpec((tokens, depth), lambda i, t: (0, 0)),
                scratch_shapes=[pltpu.VMEM((depth, TILE), BF16), pltpu.VMEM((tokens, depth), F32)],
            ),
            out_shape=jax.ShapeDtypeStruct((tokens, depth), BF16),
            compiler_params=pltpu.CompilerParams(vmem_limit_bytes=VMEM_LIMIT),
            cost_estimate=FREE,
        )(self.table, *[part for part, _ in quarters(self.parts)], *grads)

    def pullback(self, x, grads, places, lead=0):
        if not self.aligned:
            grad = jnp.concatenate(grads, axis=1)
            halves = split_stack([mm_tn(x, grad).astype(BF16)], places, self.count)
            return mm_nt(grad, self.whole()).astype(BF16), [jnp.pad(h, ((0, 0), (0, 0), (lead, 0))) for h in halves]
        tokens, depth = x.shape
        ends = np.cumsum([grad.shape[1] // TILE for grad in grads])
        bounds = [(int(end) - grad.shape[1] // TILE, int(end)) for end, grad in zip(ends, grads)]
        half = jax.ShapeDtypeStruct((self.count // 2, self.rows, lead + self.width), BF16)
        half_spec = pl.BlockSpec((self.count // 2, self.rows, TILE), lambda i, t, p: (0, 0, lead // TILE + i))
        result = pl.pallas_call(
            functools.partial(pullback_kernel, self.rows, 4, bounds),
            grid_spec=pltpu.PrefetchScalarGridSpec(
                num_scalar_prefetch=2,
                grid=(self.width // TILE,),
                in_specs=[pl.BlockSpec((tokens, depth), lambda i, t, p: (0, 0))]
                + self.part_specs()
                + [
                    pl.BlockSpec((tokens, TILE), lambda i, t, p, low=low, high=high: (0, jnp.clip(i, low, high - 1) - low))
                    for low, high in bounds
                ],
                out_specs=[pl.BlockSpec((tokens, depth), lambda i, t, p: (0, 0)), half_spec, half_spec],
                scratch_shapes=[
                    pltpu.VMEM((depth, TILE), BF16),
                    pltpu.VMEM((depth, tokens), BF16),
                    pltpu.VMEM((tokens, depth), F32),
                ],
            ),
            out_shape=[jax.ShapeDtypeStruct((tokens, depth), BF16), half, half],
            compiler_params=pltpu.CompilerParams(vmem_limit_bytes=VMEM_LIMIT),
            cost_estimate=FREE,
        )(self.table, places, x, *[part for part, _ in quarters(self.parts)], *grads)
        return result[0], result[1:]


class Stream:
    def __init__(self, size, steps):
        self.size, self.steps = size, steps
        self.arriving = None
        self.value = None
        self.done = False
        self.pending = None

    def begin(self, arrived=None):
        try:
            self.pending = self.steps.send(arrived)
        except StopIteration as stop:
            self.pending, self.value, self.done = None, stop.value, True

    def launch(self):
        outgoing, bits, sends = self.pending
        self.arriving, self.pending = exchange(outgoing, bits, self.size, sends), None

    def result(self):
        if self.arriving is None and self.pending is None and not self.done:
            self.begin()
        while not self.done:
            if self.arriving is None:
                self.launch()
            arrived, self.arriving = self.arriving, None
            self.begin(arrived)
        return self.value


def advance(streams, tied, hold=()):
    for stream in streams:
        if stream.arriving is None and stream.pending is None and not stream.done:
            stream.begin()
    moving = [stream for stream in streams if not stream.done]
    ending = [stream for stream in moving if stream.arriving is not None]
    fresh = [stream for stream in moving if stream.arriving is None]
    arrived, outgoing, tied = lax.optimization_barrier(
        ([s.arriving for s in ending], [s.pending[0] for s in fresh], tied)
    )
    for stream, array in zip(fresh, outgoing):
        stream.pending = (array,) + stream.pending[1:]
    for stream, array in zip(ending, arrived):
        stream.arriving = None
        stream.begin(array)
    for stream in moving:
        if not stream.done and stream not in hold:
            stream.launch()
    return tied


def top_sends(size):
    top = bit_count(size) - 1
    return lambda core, i: (i >> top) == core


def doubling(held, order_pair, first=0, twice=False):
    parts = (held,)
    steps = list(zip(*order_pair))[first:]
    for index, bits in enumerate(steps):
        if len(parts) > 1 and not (twice and index == len(steps) - 1):
            parts = (jnp.concatenate(parts, axis=0),)
        arrived = yield lax.optimization_barrier(parts), bits, None
        parts = parts + arrived
    return parts


def gather_all(packed, order_pair, twice):
    return (yield from doubling(packed[None], order_pair, 0, twice))


def gather_core(piece, order_pair, places):
    size = lax.axis_size("dp")
    top = bit_count(size) - 1
    arrived = yield piece, (top, top), top_sends(size)
    mine = (lax.axis_index("dp") >> top) == lax.axis_index("section")
    parts = yield from doubling(jnp.where(mine, piece, arrived)[None], order_pair)
    table, cuts = placement(order_pair, places), [(0, piece.shape[0], 0, piece.shape[1])]
    return assembled_fours(parts, table, cuts) if len(places) > 1 else assembled(parts, table, cuts)


def own_bit(pair):
    position = lax.axis_index("dp")
    return (position >> jnp.where(lax.axis_index("section") == 0, pair[0], pair[1])) & 1


def gather_square(blocks, order_pair, places, cuts):
    first, second = list(zip(*order_pair))[:2]
    a, b = own_bit(first), own_bit(second)
    kept = lax.dynamic_index_in_dim(blocks, a, 0, keepdims=False)
    arrived = yield lax.dynamic_index_in_dim(blocks, 1 - a, 0, keepdims=False), first, None
    held = jnp.stack([kept, arrived])
    kept = lax.dynamic_index_in_dim(held, b, 1, keepdims=False)
    arrived = yield lax.dynamic_index_in_dim(held, 1 - b, 1, keepdims=False), second, None
    parts = yield from doubling(jnp.concatenate([kept, arrived], axis=0), order_pair, 2)
    return assembled(parts, placement(order_pair, places), cuts)


def total_of(terms):
    return sum(term.astype(F32) for term in terms)


def halving(send, kept, order_pair, last=0):
    terms, outgoing = [kept], send
    for bits in reversed(list(zip(*order_pair))[last:]):
        if outgoing is None:
            half = terms[0].shape[0] // 2
            outgoing = total_of([term[half:] for term in terms]).astype(BF16)
            terms = [term[:half] for term in terms]
        arrived = yield outgoing, bits, None
        terms, outgoing = terms + [arrived], None
    return terms


def scatter_all(halves, order_pair):
    terms = yield from halving(*halves, order_pair)
    return total_of(terms)[0].astype(BF16)


def scatter_core(grad, order_pair, places, size):
    halves = split_stack([grad], placement(order_pair, places), 1 << len(places))
    terms = yield from halving(*halves, order_pair)
    top = bit_count(size) - 1
    sends = top_sends(size)
    arrived = yield total_of(terms)[0].astype(BF16), (top, top), lambda core, i: not sends(core, i)
    return (total_of(terms)[0] + arrived.astype(F32)).astype(BF16)


def scatter_square(grad, order_pair, places):
    halves = split_stack([grad], placement(order_pair, places), 1 << len(places))
    terms = yield from halving(*halves, order_pair, 2)
    held = total_of(terms).astype(BF16)
    first, second = list(zip(*order_pair))[:2]
    arrived = yield held[2:], second, None
    held = jnp.stack([held[:2], arrived])
    arrived = yield held[:, 1], first, None
    return jnp.stack([held[:, 0], arrived])


def scatter_small(vector, size):
    position = lax.axis_index("dp")
    held = vector.reshape(size // 4, 4, vector.shape[2])
    for count, low in ((4, 0), (size // 4, 2)):
        own = (position >> low) & (count - 1)

        def part(index):
            return lax.dynamic_index_in_dim(held, index, 1 if low == 0 else 0, keepdims=False)

        outgoing = tuple(part(own ^ other) for other in range(1, count))
        arrived = yield outgoing, tuple(other << low for other in range(1, count)), "flips"
        held = part(own) + sum(arrived)
    return held


def in_square(blocks):
    is_first = lax.axis_index("section") == 0
    middle = jnp.where(is_first, blocks[1:3], jnp.stack([blocks[2], blocks[1]]))
    return jnp.concatenate([blocks[:1], middle, blocks[3:]], axis=0)


SQUARE = ((0, 1), (1, 0))


def gather_in_square(rows):
    held = rows[None]
    for bits in SQUARE:
        arrived = yield held, bits, None
        held = jnp.concatenate([held, arrived], axis=0)
    return in_square(held)


def scatter_in_square(blocks):
    held = in_square(blocks)
    for bits in reversed(SQUARE):
        half = held.shape[0] // 2
        arrived = yield held[half:].astype(BF16), bits, None
        held = held[:half] + arrived.astype(F32)
    return held[0]


def local(
    size,
    bytes_in,
    lengths,
    patch_index,
    patch_count,
    gain_l1,
    qkv_l,
    out_l,
    gain_l2,
    up_l,
    down_l,
    patch_proj,
    gain_g1,
    qkv_g,
    out_g,
    gain_g2,
    up_g,
    down_g,
    out_grad,
):
    core = lax.axis_index("section")
    position = lax.axis_index("dp")
    is_first = core == 0
    seq_rows, half_l = bytes_in.shape[1:]
    width_l, width_g = 2 * half_l, out_g.shape[1]
    half_g = width_g // 2
    rows_l, rows_g = out_l.shape[0], out_g.shape[0]
    units_l, units_g = down_l.shape[0], down_g.shape[0]
    micro_total, slot_total = patch_index.shape[1:]
    slots = micro_total * slot_total
    bits = bit_count(size)
    every = tuple(range(bits))

    def joined(mine, theirs, axis=1):
        low = jnp.where(is_first, mine, theirs)
        high = jnp.where(is_first, theirs, mine)
        return jnp.concatenate([low, high], axis=axis)

    def shared(mine, axis=1):
        return joined(mine, swap(mine), axis)

    def half_of(array, which, axis=1):
        length = array.shape[axis] // 2
        return lax.dynamic_slice_in_dim(array, which * length, length, axis)

    def slope_of(upward):
        return jax.vjp(jax.nn.gelu, upward)[1](jnp.ones_like(upward))[0]

    def summed_cores(part):
        part = part.astype(BF16)
        return part.astype(F32) + swap(part).astype(F32)

    def own_heads(weight):
        return jnp.concatenate([half_of(third, core) for third in jnp.split(weight, 3, axis=1)], axis=1)

    def square_columns(weight):
        pieces = jnp.split(weight, size // 2, axis=1)
        return [jnp.concatenate(pieces[k::4], axis=1) for k in range(4)]

    def gain_block():
        columns = [gain.reshape(rows_l, -1) for gain in (gain_l1, gain_l2, gain_g1, gain_g2)]
        block = jnp.concatenate(columns, axis=1)
        return jnp.pad(block, ((0, 0), (0, TILE - block.shape[1])))

    lows_first = orders(size, (-1, -2, None))
    lows_last = orders(size, (None, -1, -2))
    plane = [o[:2] + (bits - 1,) + o[2:] for o in orders(size, (-1, -2, None))]
    line = orders(size, (None,))
    below, beyond = tuple(range(bits - 1)), tuple(range(2, bits - 1))

    fresh = functools.partial(Stream, size)
    up_width, qkv_width = up_l.shape[1] // 2, 3 * half_g
    square_units = units_g * (size // 8)
    rises, falls = (None, -1, -2), (-1, None, -2)
    order_l = [(bits - 1,) + orders(size, middle)[which] for which, middle in enumerate((falls, rises))]
    order_g = [(bits - 1,) + orders(size, middle)[which] for which, middle in enumerate((rises, falls))]
    table, table_g = placement(order_l, every), placement(order_g, every)
    side_l = half_l + half_g
    stream_l = fresh(
        gather_all(
            jnp.concatenate(
                [half_of(out_l, core), half_of(patch_proj, core), gain_block(), own_heads(qkv_l), half_of(up_l, core)],
                axis=1,
            ),
            order_l,
            True,
        )
    )
    stream_down_l = fresh(gather_core(down_l, lows_last, below))
    stream_g = fresh(gather_all(own_heads(qkv_g), order_g, False))
    stream_out_g = fresh(gather_all(half_of(out_g, core), order_g, False))
    square = square_columns(half_of(up_g, core))
    one_two = jnp.where(is_first, square[2], square[1])
    two_one = jnp.where(is_first, square[1], square[2])
    blocks = jnp.stack([square[0], one_two, two_one, square[3]]).reshape(2, 2, rows_g, square_units)
    stream_up_g = fresh(gather_square(blocks, plane, every, [(0, rows_g, 0, square_units)]))
    stream_down_g = fresh(
        gather_core(down_g[:, :width_l], line, beyond)
    )

    bias_l = jnp.where(jnp.arange(seq_rows) < lengths[0], 0.0, NEG).astype(F32)[:, None]
    live = (jnp.arange(slot_total)[None, :] < patch_count[0][:, None]).reshape(slots)
    bias_g = jnp.where(live, 0.0, NEG).astype(F32)[:, None]
    positions = patch_index[0].reshape(slots)
    picks = positions[:, None] == jnp.arange(seq_rows)[None, :]
    picks_live = (picks & live[:, None]).astype(BF16)
    picks = picks.astype(BF16)

    advance([stream_l], ())
    seq_inputs = shared(bytes_in[0])
    inputs = seq_inputs.astype(F32)
    scale_l1 = row_scale(inputs)
    seq_grads = shared(out_grad[0])
    grad_top_b = mm(picks_live, seq_grads).astype(BF16)
    scale_l1 = advance([stream_l, stream_up_g, stream_down_l, stream_g], scale_l1)
    stream_top = fresh(gather_in_square(half_of(grad_top_b, core)))
    grad_top_b = advance([stream_l, stream_up_g, stream_down_l, stream_top], grad_top_b)
    advance([stream_l, stream_g, stream_top, stream_up_g], (), [stream_up_g])

    advance([stream_l, stream_g, stream_down_l, stream_up_g, stream_down_g, stream_top, stream_out_g], ())
    parts = stream_l.result()
    front = side_l + TILE
    out_wl, proj_w, gains = assembled_fours(
        parts,
        table,
        [(0, rows_l, 0, half_l), (0, rows_l, half_l, side_l), (0, rows_l, side_l, side_l + LANES)],
        front,
        LONG,
    )
    qkv_wl = Weight(parts, table, front, 3 * half_l)
    up_wl = Weight(parts, table, front + 3 * half_l, up_width)
    gain_one_l, gain_two_l = gains[:, 0].astype(F32), gains[:, 1].astype(F32)
    per = width_g // width_l
    gain_one_g, gain_two_g = (
        gains[:, low : low + per].reshape(width_g).astype(F32) for low in (2, 2 + per)
    )
    normed_l = (inputs * scale_l1 * gain_one_l).astype(BF16)
    projected_l = qkv_wl.product(normed_l)
    own_mixture_l, lse_l = attention_forward(projected_l, bias_l)
    mixture_l = own_mixture_l
    mixture_l, out_wl, proj_w = advance(
        [stream_down_l, stream_up_g, stream_down_g, stream_out_g], (mixture_l, out_wl, proj_w), [stream_up_g]
    )
    mixture_l = advance([stream_g], mixture_l)
    mixture_l, out_wl = shared(mixture_l), shared(out_wl)
    out_own_l = half_of(out_wl, core, 0)
    hidden_l = inputs + mm(mixture_l, out_wl)
    scale_l2 = row_scale(hidden_l)
    normed_l2 = (hidden_l * scale_l2 * gain_two_l).astype(BF16)
    activated_l, slope_l = up_wl.product(normed_l2, gelu=True)
    activated_l, proj_w = advance(
        [stream_down_l, stream_down_g, stream_out_g, stream_up_g], (activated_l, proj_w)
    )
    proj_w = shared(proj_w)
    (down_wl,) = stream_down_l.result()
    partial_l = mm(activated_l, down_wl)
    local_out = half_of(hidden_l, core) + half_of(partial_l, core) + swap(half_of(partial_l, 1 - core))

    boundary = shared(mm(picks, local_out.astype(BF16)).astype(BF16))
    start_rows = mm(boundary, proj_w)
    scale_g1 = row_scale(start_rows)
    square_top = shared(stream_top.result().reshape(4 * slots, half_l))
    scale_g1, square_top = advance([stream_g, stream_out_g, stream_up_g], (scale_g1, square_top))
    qkv_wg = Weight(stream_g.result(), table_g, 0, qkv_width)
    normed_g = (start_rows * scale_g1 * gain_one_g).astype(BF16)
    projected_g = qkv_wg.product(normed_g)
    own_mixture_g, lse_g = attention_forward(projected_g, bias_g)
    mixture_g = own_mixture_g
    mixture_g = advance([stream_out_g], mixture_g)
    (out_wg,) = assembled_fours(stream_out_g.result(), table_g, [(0, rows_g, 0, half_g)])
    out_theirs_g = swap(out_wg)
    mixture_g = shared(mixture_g)
    hidden_g = start_rows + joined(mm(mixture_g, out_wg), mm(mixture_g, out_theirs_g))
    scale_g2 = row_scale(hidden_g)
    normed_g2 = (hidden_g * scale_g2 * gain_two_g).astype(BF16)
    square_normed = fresh(gather_in_square(half_of(normed_g2, core))).result()
    square_normed = shared(square_normed.reshape(4 * slots, half_g))
    (up_wg,) = stream_up_g.result()
    (down_wg,) = stream_down_g.result()
    upward_g = mm(square_normed, up_wg)
    activated_g = jax.nn.gelu(upward_g).astype(BF16)

    grad_down_g = mm_tn(activated_g, square_top).astype(BF16)
    stream_down_g = fresh(scatter_core(grad_down_g, line, beyond, size))
    grad_act_g = mm_nt(square_top, down_wg)
    grad_up_g_rows = jax.vjp(jax.nn.gelu, upward_g)[1](grad_act_g)[0].astype(BF16)
    grad_up_g = mm_tn(square_normed, grad_up_g_rows).astype(BF16)
    stream_up_g = fresh(scatter_square(grad_up_g, plane, every))
    part = mm_nt(grad_up_g_rows, up_wg)
    part = half_of(part, core) + swap(half_of(part, 1 - core).astype(BF16)).astype(F32)
    part = advance([stream_down_g, stream_up_g], part)
    part = shared(fresh(scatter_in_square(part.reshape(4, slots, half_g))).result())
    pulled, grad_gain_g2 = norm_backward(part, hidden_g, scale_g2, gain_two_g)
    grad_hidden_g = jnp.pad(grad_top_b.astype(F32), ((0, 0), (0, width_g - width_l))) + pulled
    grad_hidden_gb = grad_hidden_g.astype(BF16)
    mine_gb, theirs_gb = half_of(grad_hidden_gb, core), half_of(grad_hidden_gb, 1 - core)
    grad_out_g = mm_tn(mixture_g, mine_gb).astype(BF16)
    stream_out_g = fresh(scatter_all(split_stack([grad_out_g], table_g, size), order_g))
    grad_mixture_g = (
        mm_nt(mine_gb, half_of(out_wg, core, 0)) + mm_nt(theirs_gb, half_of(out_theirs_g, core, 0))
    ).astype(BF16)
    partial_g = mm(activated_g, down_wg)
    partial_g = half_of(partial_g, core) + swap(half_of(partial_g, 1 - core).astype(BF16)).astype(F32)
    stream_out = fresh(scatter_in_square(partial_g.reshape(4, slots, half_l)))
    grad_mixture_g = advance([stream_out_g, stream_out], grad_mixture_g)
    grad_projected_g = attention_backward(projected_g, bias_g, lse_g, own_mixture_g, grad_mixture_g)
    part, halves = qkv_wg.pullback(normed_g, grad_projected_g, table_g)
    stream_g = fresh(scatter_all(halves, order_g))
    part = advance([stream_g, stream_out, stream_out_g, stream_down_g], part)
    part = summed_cores(part)
    part = advance([stream_up_g], part)
    pulled, grad_gain_g1 = norm_backward(part, start_rows, scale_g1, gain_one_g)
    grad_start = (grad_hidden_g + pulled).astype(BF16)
    grad_proj = mm_tn(boundary, half_of(grad_start, core)).astype(BF16)

    grad_rows = mm_nt(grad_start, proj_w).astype(BF16)
    grad_local = seq_grads.astype(F32) + mm_tn(picks, grad_rows)
    grad_local_b = grad_local.astype(BF16)
    part, grad_down_l, up_halves = up_wl.feed_forward_pullback(
        normed_l2, grad_local_b, down_wl, slope_l, activated_l, table, side_l
    )
    stream_down_l = fresh(scatter_core(grad_down_l, lows_first, below, size))
    part, up_halves = advance([stream_g, stream_down_g, stream_up_g, stream_out_g], (part, up_halves))
    part = summed_cores(part)
    pulled, grad_gain_l2 = norm_backward(part, hidden_l, scale_l2, gain_two_l)
    grad_hidden_l = grad_local + pulled
    grad_hidden_lb = grad_hidden_l.astype(BF16)
    grad_out_l = mm_tn(mixture_l, half_of(grad_hidden_lb, core)).astype(BF16)
    stream_up_l = fresh(scatter_all(split_stack([grad_out_l, grad_proj], table, size, up_halves), order_l))
    grad_mixture_l = mm_nt(grad_hidden_lb, out_own_l).astype(BF16)
    grad_mixture_l = advance([stream_g, stream_down_l, stream_up_l], grad_mixture_l)
    grad_projected_l = attention_backward(projected_l, bias_l, lse_l, own_mixture_l, grad_mixture_l)
    grad_projected_l = advance([stream_out_g, stream_up_g], grad_projected_l)
    stream_qkv_l = fresh(scatter_all(qkv_wl.outer(normed_l, grad_projected_l, table), order_l))
    grad_projected_l = advance([stream_qkv_l], grad_projected_l)
    part = advance([stream_up_l, stream_up_g, stream_g, stream_down_l], qkv_wl.inner(grad_projected_l))
    part = summed_cores(part)
    pulled, grad_gain_l1 = norm_backward(part, inputs, scale_l1, gain_one_l)
    input_grad = half_of(grad_hidden_l + pulled, core).astype(BF16)[None]
    gains = jnp.concatenate(
        [
            grad.reshape(size, 1, grad.shape[0] // size)
            for grad in (grad_gain_l1, grad_gain_l2, grad_gain_g1, grad_gain_g2)
        ],
        axis=2,
    )
    returned = half_of(hidden_g[:, :width_l], core) + stream_out.result()
    hidden_out = (local_out + mm_tn(picks_live, returned.astype(BF16))).astype(BF16)[None]
    stream_gains = fresh(scatter_small(gains, size))
    input_grad = advance([stream_qkv_l, stream_up_l, stream_down_l, stream_gains], input_grad)
    advance([stream_qkv_l, stream_gains, stream_down_l, stream_out_g, stream_g], ())
    advance([stream_up_l, stream_gains], ())
    advance([stream_qkv_l], ())
    advance([stream_up_l, stream_qkv_l, stream_down_l], ())

    def joined_columns(mine, theirs):
        return joined(mine, theirs).astype(F32)

    def joined_heads(mine, theirs):
        low, high = jnp.where(is_first, mine, theirs), jnp.where(is_first, theirs, mine)
        thirds = [jnp.split(part, 3, axis=1) for part in (low, high)]
        return jnp.concatenate([part for pair in zip(*thirds) for part in pair], axis=1).astype(F32)

    def from_owner(mine, theirs):
        return jnp.where((position >> (bits - 1)) == core, mine, theirs).astype(F32)

    def in_order(blocks):
        low = own_bit((0, 0)), own_bit((1, 1))
        rows, width = blocks.shape[2:]
        placed = []
        for y in range(2):
            for x in range(2):
                dx, dy = x ^ low[0], y ^ low[1]
                index = jnp.where(is_first, 2 * dx + dy, 2 * dy + dx)
                placed.append(lax.dynamic_index_in_dim(blocks.reshape(4, rows, width), index, 0, keepdims=False))
        pieces = [jnp.split(part, size // 8, axis=1) for part in placed]
        return jnp.concatenate([piece for group in zip(*pieces) for piece in group], axis=1)

    down_g_mine = stream_down_g.result()
    total_down_g = from_owner(down_g_mine, swap(down_g_mine))
    total_down_g = jnp.pad(total_down_g, ((0, 0), (0, width_g - width_l)))
    up_g_mine = in_order(stream_up_g.result())
    total_up_g = joined_columns(up_g_mine, swap(up_g_mine))
    g_mine = stream_g.result()
    total_qkv_g = joined_heads(g_mine, swap(g_mine))
    out_g_mine = stream_out_g.result()
    total_out_g = joined_columns(out_g_mine, swap(out_g_mine))
    down_l_mine = stream_down_l.result()
    total_down_l = from_owner(down_l_mine, swap(down_l_mine))
    l_mine = stream_up_l.result()
    l_theirs = swap(l_mine)
    cuts = [0, half_l, side_l, side_l + up_width]
    total_out_l, total_proj, total_up_l = (
        joined_columns(l_mine[:, low:high], l_theirs[:, low:high]) for low, high in zip(cuts, cuts[1:])
    )
    q_mine = stream_qkv_l.result()
    total_qkv_l = joined_heads(q_mine, swap(q_mine))
    gains = stream_gains.result()
    gains = jnp.where(is_first, gains, lax.ppermute(gains, "section", [(0, 1)]))
    total_gain_l1 = gains[:rows_l]
    total_gain_l2 = gains[rows_l : 2 * rows_l]
    total_gain_g1 = gains[2 * rows_l : 2 * rows_l + rows_g]
    total_gain_g2 = gains[2 * rows_l + rows_g :]
    return (
        hidden_out,
        input_grad,
        total_gain_l1,
        total_qkv_l,
        total_out_l,
        total_gain_l2,
        total_up_l,
        total_down_l,
        total_proj,
        total_gain_g1,
        total_qkv_g,
        total_out_g,
        total_gain_g2,
        total_up_g,
        total_down_g,
    )


def solution(mesh):
    rows, vector = P("dp", None), P("dp")
    features = P("dp", None, "section")
    in_specs = (
        features,
        vector,
        P("dp", None, None),
        rows,
        vector,
        rows,
        rows,
        vector,
        rows,
        rows,
        rows,
        vector,
        rows,
        rows,
        vector,
        rows,
        rows,
        features,
    )
    out_specs = (
        features,
        features,
        vector,
        rows,
        rows,
        vector,
        rows,
        rows,
        rows,
        vector,
        rows,
        rows,
        vector,
        rows,
        rows,
    )
    return jax.shard_map(
        functools.partial(local, mesh.shape["dp"]),
        mesh=mesh,
        in_specs=in_specs,
        out_specs=out_specs,
        check_vma=False,
    )
```

```python
import functools

import jax
import jax.numpy as jnp
import numpy as np
from jax import lax
from jax.experimental import pallas as pl
from jax.experimental.pallas import tpu as pltpu
from jax.sharding import PartitionSpec as P

WINDOW = 1536
EPSILON = 1e-06
LANES = 128
GELU_SCALE = (2.0 / np.pi) ** 0.5
GELU_CUBE = 0.044715
NEG = -1e30
VMEM_LIMIT = 48 * 1024 * 1024
FREE = pl.CostEstimate(flops=0, bytes_accessed=0, transcendentals=0)
LONG = pl.CostEstimate(flops=10**11, bytes_accessed=0, transcendentals=0)
F32 = jnp.float32
BF16 = jnp.bfloat16


def mm(left, right):
    return jnp.dot(left, right, preferred_element_type=F32)


def mm_nt(left, right):
    return lax.dot_general(left, right, (((1,), (1,)), ((), ())), preferred_element_type=F32)


def mm_tn(left, right):
    return lax.dot_general(left, right, (((0,), (0,)), ((), ())), preferred_element_type=F32)


def row_scale(values):
    return lax.rsqrt(jnp.mean(values * values, axis=-1, keepdims=True) + EPSILON)


def norm_backward(grad_normed, values, scale, gain):
    grad_gain = jnp.sum(grad_normed * values * scale, axis=0)
    pulled = grad_normed * gain
    inner = jnp.mean(pulled * values, axis=-1, keepdims=True)
    return scale * pulled - values * (scale * scale * scale * inner), grad_gain


def query_block(rows):
    return 256 if rows % 256 == 0 else rows


def head_masks(block):
    lane = lax.broadcasted_iota(jnp.int32, (block, LANES), 1)
    return [lane < LANES // 2, lane >= LANES // 2]


def stacked(values, masks):
    return jnp.concatenate([jnp.where(mask, values, jnp.zeros_like(values)) for mask in masks], axis=0)


def first_lanes(values):
    lane = lax.broadcasted_iota(jnp.int32, (values[0].shape[0], LANES), 1)
    result = jnp.zeros(lane.shape, F32)
    for index, value in enumerate(values):
        result = jnp.where(lane == index, value, result)
    return result.astype(BF16)


def masked_scores(keys, biased, query, extended, bias, start, block, window):
    key_at = lax.broadcasted_iota(jnp.int32, (block, 2 * block), 0)
    query_at = lax.broadcasted_iota(jnp.int32, (block, 2 * block), 1)
    query_at = jnp.where(query_at < block, query_at, query_at - block)
    parts = []
    if start:
        before = mm_nt(biased[:start], extended)
        if window is not None:
            far = lax.broadcasted_iota(jnp.int32, (start, 2 * block), 0)
            own = lax.broadcasted_iota(jnp.int32, (start, 2 * block), 1)
            own = jnp.where(own < block, own, own - block) + start
            before = jnp.where(own - far < window, before, NEG)
        parts.append(before)
    diagonal = mm_nt(keys[start : start + block], query)
    masked = jnp.where(key_at < query_at, diagonal + bias[start : start + block], NEG)
    parts.append(jnp.where(key_at == query_at, diagonal, masked))
    return parts


def ranges(parts):
    low = 0
    for part in parts:
        yield low, low + part.shape[0], part
        low += part.shape[0]


def extend_keys(biased, k_ref, bias_ref):
    biased[:, :LANES] = k_ref[...]
    biased[:, LANES:] = first_lanes([bias_ref[...]])


def attention_forward_kernel(rows, window, q_ref, k_ref, v_ref, bias_ref, o_ref, lse_ref, biased, counted):
    block = query_block(rows)
    masks = head_masks(block)
    score_scale = (LANES // 2) ** (-0.5)
    lane = lax.broadcasted_iota(jnp.int32, (block, LANES), 1)
    extend_keys(biased, k_ref, bias_ref)
    for head, mask in enumerate(head_masks(rows)):
        counted[head] = jnp.where(mask, v_ref[...], jnp.ones_like(v_ref))
    one = first_lanes([jnp.ones((2 * block, 1), F32)])
    query_at = lax.broadcasted_iota(jnp.int32, (2 * block, block), 0)
    query_at = jnp.where(query_at < block, query_at, query_at - block)
    key_at = lax.broadcasted_iota(jnp.int32, (2 * block, block), 1)
    for index in range(rows // block):
        start = index * block
        query = stacked((q_ref[start : start + block, :] * score_scale).astype(BF16), masks)
        extended = jnp.concatenate([query, one], axis=1)
        parts = []
        if start:
            before = mm_nt(extended, biased[:start, :])
            if window is not None:
                far = lax.broadcasted_iota(jnp.int32, (2 * block, start), 1)
                own = lax.broadcasted_iota(jnp.int32, (2 * block, start), 0)
                own = jnp.where(own < block, own, own - block) + start
                before = jnp.where(own - far < window, before, NEG)
            parts.append(before)
        masked = jnp.where(key_at < query_at, mm_nt(extended, biased[start : start + block, :]), NEG)
        parts.append(jnp.where(key_at == query_at, mm_nt(query, k_ref[start : start + block, :]), masked))
        top = functools.reduce(jnp.maximum, [jnp.max(p, axis=1, keepdims=True) for p in parts])
        parts = [jnp.exp(p - top).astype(BF16) for p in parts]
        out, logs = jnp.zeros((block, LANES), F32), jnp.zeros((block, LANES), F32)
        for head, mask in enumerate(masks):
            span = slice(head * block, (head + 1) * block)
            mixed, low = jnp.zeros((block, LANES), F32), 0
            for part in parts:
                high = low + part.shape[1]
                mixed += mm(part[span], counted[head, low:high, :])
                low = high
            other = LANES // 2 if head == 0 else 0
            total = mixed[:, other : other + 1]
            out = jnp.where(mask, mixed * (1.0 / total), out)
            logs = jnp.where(lane == head, top[span] + jnp.log(total), logs)
        o_ref[start : start + block, :] = out.astype(BF16)
        lse_ref[0, :, start : start + block] = logs.T[:2]


def attention_backward_kernel(
    rows,
    window,
    q_ref,
    k_ref,
    v_ref,
    bias_ref,
    lse_ref,
    o_ref,
    do_ref,
    dq_ref,
    dk_ref,
    dv_ref,
    dk_acc,
    dv_acc,
    biased,
    reduced,
):
    block = query_block(rows)
    masks = head_masks(block)
    score_scale = (LANES // 2) ** (-0.5)
    extend_keys(biased, k_ref, bias_ref)
    reduced[:, :LANES] = v_ref[...]
    reduced[:, LANES:] = first_lanes([jnp.full((rows, 1), -1.0, F32)] * 2)
    one = first_lanes([jnp.ones((2 * block, 1), F32)])
    for index in reversed(range(rows // block)):
        start = index * block
        query = stacked((q_ref[start : start + block, :] * score_scale).astype(BF16), masks)
        extended = jnp.concatenate([query, one], axis=1)
        grad = stacked(do_ref[start : start + block, :], masks)
        mixed = o_ref[start : start + block, :].astype(F32)
        delta = jnp.sum(grad.astype(F32) * jnp.concatenate([mixed, mixed], axis=0), axis=1, keepdims=True)
        near = delta.astype(BF16).astype(F32)
        grad_extended = jnp.concatenate([grad, first_lanes([near, delta - near])], axis=1)
        lse = jnp.concatenate([lse_ref[0, head : head + 1, start : start + block] for head in range(2)], axis=1)
        parts = masked_scores(k_ref, biased, query, extended, bias_ref, start, block, window)
        turned = jnp.zeros((2 * block, LANES), F32)
        for low, high, part in ranges(parts):
            weights = jnp.exp(part - lse)
            change = (weights * mm_nt(reduced[low:high, :], grad_extended)).astype(BF16)
            dv = mm(weights.astype(BF16), grad)
            dk = mm(change, query)
            if index == rows // block - 1:
                dv_acc[low:high, :] = dv
                dk_acc[low:high, :] = dk
            else:
                dv_acc[low:high, :] += dv
                dk_acc[low:high, :] += dk
            turned += mm_tn(change, k_ref[low:high, :])
        dq = jnp.where(masks[0], turned[:block], turned[block:]) * score_scale
        dq_ref[start : start + block, :] = dq.astype(BF16)
    dk_ref[...] = dk_acc[...].astype(BF16)
    dv_ref[...] = dv_acc[...].astype(BF16)


def attention_specs(rows, width):
    pairs = width // LANES
    wide = lambda part: pl.BlockSpec((rows, LANES), lambda i, part=part: (0, part * pairs + i))
    bias = pl.BlockSpec((rows, 1), lambda i: (0, 0))
    return pairs, wide, bias


def attention_forward(projected, bias):
    rows, width = projected.shape[0], projected.shape[1] // 3
    pairs, wide, bias_spec = attention_specs(rows, width)
    window = WINDOW if rows > WINDOW else None
    return pl.pallas_call(
        functools.partial(attention_forward_kernel, rows, window),
        grid=(pairs,),
        in_specs=[wide(0), wide(1), wide(2), bias_spec],
        out_specs=[wide(0), pl.BlockSpec((1, 2, rows), lambda i: (i, 0, 0))],
        out_shape=[
            jax.ShapeDtypeStruct((rows, width), BF16),
            jax.ShapeDtypeStruct((pairs, 2, rows), F32),
        ],
        scratch_shapes=[pltpu.VMEM((rows, 2 * LANES), BF16), pltpu.VMEM((2, rows, LANES), BF16)],
        compiler_params=pltpu.CompilerParams(vmem_limit_bytes=VMEM_LIMIT),
        cost_estimate=FREE,
    )(projected, projected, projected, bias)


def attention_backward(projected, bias, lse, mixture, grad_mixture):
    rows, width = grad_mixture.shape
    pairs, wide, bias_spec = attention_specs(rows, width)
    window = WINDOW if rows > WINDOW else None
    shape = jax.ShapeDtypeStruct((rows, width), BF16)
    return pl.pallas_call(
        functools.partial(attention_backward_kernel, rows, window),
        grid=(pairs,),
        in_specs=[
            wide(0),
            wide(1),
            wide(2),
            bias_spec,
            pl.BlockSpec((1, 2, rows), lambda i: (i, 0, 0)),
            wide(0),
            wide(0),
        ],
        out_specs=[wide(0), wide(0), wide(0)],
        out_shape=[shape, shape, shape],
        scratch_shapes=[
            pltpu.VMEM((rows, LANES), F32),
            pltpu.VMEM((rows, LANES), F32),
            pltpu.VMEM((rows, 2 * LANES), BF16),
            pltpu.VMEM((rows, 2 * LANES), BF16),
        ],
        compiler_params=pltpu.CompilerParams(vmem_limit_bytes=VMEM_LIMIT),
        cost_estimate=LONG,
    )(projected, projected, projected, bias, lse, mixture, grad_mixture)


def swap(array):
    return lax.ppermute(array, "section", [(0, 1), (1, 0)])


def exchange(array, bits, size, sends=None):
    if sends == "flips":
        return tuple(
            lax.ppermute(part, "dp", [(i, i ^ flip) for i in range(size)]) for part, flip in zip(array, bits)
        )
    pairs = [
        (core * size + i, core * size + (i ^ (1 << bit)))
        for core, bit in enumerate(bits)
        for i in range(size)
        if sends is None or sends(core, i)
    ]
    return jax.tree.map(lambda part: lax.ppermute(part, ("section", "dp"), pairs), array)


def bit_count(size):
    return size.bit_length() - 1


def orders(size, middle):
    bits = bit_count(size)
    others = tuple(reversed(range(2, bits - 1)))
    result = []
    for core in range(2):
        lowest = (0, 1) if core == 0 else (1, 0)
        order = ()
        for entry in middle:
            order += others if entry is None else (lowest[0] if entry == -1 else lowest[1],)
        result.append(order)
    return result


def mask_of(index, order, places):
    return sum(((index >> t) & 1) << places.index(bit) for t, bit in enumerate(order))


def placement(order_pair, places):
    position = lax.axis_index("dp")
    own = sum(((position >> bit) & 1) << p for p, bit in enumerate(places))
    count = 1 << len(places)
    masks = [jnp.asarray([mask_of(j, order, places) for j in range(count)], jnp.int32) for order in order_pair]
    return (own ^ jnp.where(lax.axis_index("section") == 0, masks[0], masks[1])).astype(jnp.int32)


def aligned(rows, cuts=()):
    return rows % 16 == 0 and all(c % LANES == 0 and r % 16 == 0 for r0, r1, c0, c1 in cuts for r, c in ((r0, c0), (r1, c1)))


def assembly_kernel(bounds, cuts, table, *refs):
    step = pl.program_id(0)
    parts, outs = refs[: len(bounds)], refs[len(bounds) :]

    def store(ref):
        for (r0, r1, c0, c1), out in zip(cuts, outs):
            out[...] = ref[0, r0:r1, c0:c1]

    for (low, high), ref in zip(bounds, parts):
        pl.when((step >= low) & (step < high))(functools.partial(store, ref))


def assembled(parts, table, cuts, offset=0, width=None):
    rows = parts[0].shape[1]
    width = width or parts[0].shape[2]
    ends = np.cumsum([part.shape[0] for part in parts])
    count = int(ends[-1])
    bounds = [(int(end) - part.shape[0], int(end)) for end, part in zip(ends, parts)]
    shapes = [(count * (r1 - r0), c1 - c0) for r0, r1, c0, c1 in cuts]
    if not aligned(rows, cuts):
        stack = jnp.concatenate(parts, axis=0)[jnp.argsort(table)][..., offset : offset + width]
        return [stack[:, r0:r1, c0:c1].reshape(s) for (r0, r1, c0, c1), s in zip(cuts, shapes)]
    return pl.pallas_call(
        functools.partial(assembly_kernel, bounds, cuts),
        grid_spec=pltpu.PrefetchScalarGridSpec(
            num_scalar_prefetch=1,
            grid=(count,),
            in_specs=[
                pl.BlockSpec(
                    (1, rows, width),
                    lambda j, t, low=low, high=high: (jnp.clip(j, low, high - 1) - low, 0, offset // width),
                )
                for low, high in bounds
            ],
            out_specs=[pl.BlockSpec((r1 - r0, c1 - c0), lambda j, t: (t[j], 0)) for r0, r1, c0, c1 in cuts],
        ),
        out_shape=[jax.ShapeDtypeStruct(s, parts[0].dtype) for s in shapes],
        compiler_params=pltpu.CompilerParams(vmem_limit_bytes=VMEM_LIMIT),
        cost_estimate=FREE,
    )(table, *parts)


def quarters(parts):
    if len(parts) == 4:
        return [(part, 0) for part in parts]
    return [(part, k) for part in parts for k in range(2)]


def whole_kernel(cuts, table, *refs):
    quarter = refs[0].shape[0]
    for index in range(4 * quarter):
        part, place = refs[index // quarter], table[index]
        for (r0, r1, c0, c1), out in zip(cuts, refs[4:]):
            rows = r1 - r0
            out[pl.ds(pl.multiple_of(place * rows, 16), rows), :] = part[index % quarter, r0:r1, c0:c1]


def assembled_fours(parts, table, cuts, width=None, cost=FREE):
    rows = parts[0].shape[1]
    width = width or parts[0].shape[2]
    count = sum(part.shape[0] for part in parts)
    shapes = [(count * (r1 - r0), c1 - c0) for r0, r1, c0, c1 in cuts]
    if not aligned(rows, cuts):
        stack = jnp.concatenate(parts, axis=0)[jnp.argsort(table)]
        return [stack[:, r0:r1, c0:c1].reshape(s) for (r0, r1, c0, c1), s in zip(cuts, shapes)]
    return pl.pallas_call(
        functools.partial(whole_kernel, cuts),
        grid_spec=pltpu.PrefetchScalarGridSpec(
            num_scalar_prefetch=1,
            grid=(1,),
            in_specs=[pl.BlockSpec((count // 4, rows, width), lambda j, t, k=k: (k, 0, 0)) for _, k in quarters(parts)],
            out_specs=[pl.BlockSpec(shape, lambda j, t: (0, 0)) for shape in shapes],
        ),
        out_shape=[jax.ShapeDtypeStruct(s, parts[0].dtype) for s in shapes],
        compiler_params=pltpu.CompilerParams(vmem_limit_bytes=VMEM_LIMIT),
        cost_estimate=cost,
    )(table, *[part for part, _ in quarters(parts)])


def split_kernel(half, count, table, *refs):
    send, keep = refs[-2:]
    rows = refs[0].shape[0] // (2 * half)
    for index in range(2 * half):
        place, base = table[index], 0
        for ref in refs[:count]:
            block = ref[pl.ds(pl.multiple_of(place * rows, 16), rows), :]
            (keep if index < half else send)[index % half, :, base : base + ref.shape[1]] = block
            base += ref.shape[1]


def split_stack(grads, table, count, into=None):
    half, rows = count // 2, grads[0].shape[0] // count
    width = sum(grad.shape[1] for grad in grads)
    if not (aligned(rows) and all(grad.shape[1] % LANES == 0 for grad in grads)):
        stack = jnp.concatenate([grad.reshape(count, rows, grad.shape[1]) for grad in grads], axis=2)[table]
        halves = [stack[half:], stack[:half]]
        if into is not None:
            halves = [jnp.concatenate([part, old[..., width:]], axis=2) for part, old in zip(halves, into)]
        return halves
    full = width if into is None else into[0].shape[2]
    shape = jax.ShapeDtypeStruct((half, rows, full), BF16)
    into = [] if into is None else list(into)
    half_spec = pl.BlockSpec((half, rows, width), lambda j, t: (0, 0, 0))
    return pl.pallas_call(
        functools.partial(split_kernel, half, len(grads)),
        grid_spec=pltpu.PrefetchScalarGridSpec(
            num_scalar_prefetch=1,
            grid=(1,),
            in_specs=[pl.BlockSpec(grad.shape, lambda j, t: (0, 0)) for grad in grads]
            + [pl.BlockSpec(memory_space=pl.ANY) for _ in into],
            out_specs=[half_spec, half_spec],
        ),
        out_shape=[shape, shape],
        input_output_aliases={1 + len(grads) + k: k for k in range(len(into))},
        compiler_params=pltpu.CompilerParams(vmem_limit_bytes=VMEM_LIMIT),
        cost_estimate=FREE,
    )(table, *grads, *into)


def write_rows(target, parts, table, rows):
    index = 0
    for part in parts:
        for k in range(part.shape[0]):
            target[pl.ds(pl.multiple_of(table[index] * rows, 16), rows), :] = part[k]
            index += 1


def product_kernel(rows, count, gelu, table, x_ref, *refs):
    parts, outs, weight = refs[:count], refs[count:-1], refs[-1]
    write_rows(weight, parts, table, rows)
    result = jnp.dot(x_ref[...], weight[...], preferred_element_type=F32)
    if not gelu:
        outs[0][...] = result.astype(outs[0].dtype)
        return
    square = result * result
    bend = jnp.tanh(GELU_SCALE * (result + GELU_CUBE * (result * square)))
    outs[0][...] = (0.5 * result * (1.0 + bend)).astype(outs[0].dtype)
    slope = 0.5 * (1.0 + bend)
    slope += (0.5 * GELU_SCALE) * result * (1.0 - bend * bend) * (1.0 + (3.0 * GELU_CUBE) * square)
    outs[1][...] = slope.astype(outs[1].dtype)


def outer_kernel(rows, bounds, places, x_ref, *refs):
    grads, (send, keep, weight, turned) = refs[: len(bounds)], refs[len(bounds) :]
    step = pl.program_id(0)

    @pl.when(step == 0)
    def _():
        turned[...] = x_ref[...].T

    grad = grads[-1][...]
    for (low, high), ref in list(zip(bounds, grads))[:-1]:
        grad = jnp.where((step >= low) & (step < high), ref[...], grad)
    weight[...] = mm(turned[...], grad).astype(BF16)
    half = keep.shape[0]
    for index in range(2 * half):
        block = weight[pl.ds(pl.multiple_of(places[index] * rows, 16), rows), :]
        (keep if index < half else send)[index % half] = block


def inner_kernel(rows, bounds, table, *refs):
    parts, grads, (dx_ref, weight, total) = refs[:4], refs[4 : 4 + len(bounds)], refs[4 + len(bounds) :]
    step = pl.program_id(0)

    @pl.when(step == 0)
    def _():
        total[...] = jnp.zeros_like(total)

    write_rows(weight, parts, table, rows)
    grad = grads[-1][...]
    for (low, high), ref in list(zip(bounds, grads))[:-1]:
        grad = jnp.where((step >= low) & (step < high), ref[...], grad)
    total[...] += mm_nt(grad, weight[...])

    @pl.when(step == pl.num_programs(0) - 1)
    def _():
        dx_ref[...] = total[...].astype(BF16)


def pullback_kernel(rows, count, bounds, table, places, x_ref, *refs):
    parts, grads = refs[:count], refs[count : count + len(bounds)]
    dx_ref, send, keep, weight, turned, total = refs[count + len(bounds) :]
    step = pl.program_id(0)

    @pl.when(step == 0)
    def _():
        turned[...] = x_ref[...].T
        total[...] = jnp.zeros_like(total)

    write_rows(weight, parts, table, rows)
    grad = grads[-1][...]
    for (low, high), ref in list(zip(bounds, grads))[:-1]:
        grad = jnp.where((step >= low) & (step < high), ref[...], grad)
    total[...] += lax.dot_general(grad, weight[...], (((1,), (1,)), ((), ())), preferred_element_type=F32)
    weight[...] = jnp.dot(turned[...], grad, preferred_element_type=F32).astype(BF16)
    half = keep.shape[0]
    for index in range(2 * half):
        block = weight[pl.ds(pl.multiple_of(places[index] * rows, 16), rows), :]
        (keep if index < half else send)[index % half] = block

    @pl.when(step == pl.num_programs(0) - 1)
    def _():
        dx_ref[...] = total[...].astype(BF16)


def feed_forward_kernel(rows, table, places, x_ref, grad_ref, down_ref, slope_ref, act_ref, *refs):
    parts, (dx_ref, down_out, send, keep, weight, turned, total) = refs[:4], refs[4:]
    step = pl.program_id(0)

    @pl.when(step == 0)
    def _():
        turned[...] = x_ref[...].T
        total[...] = jnp.zeros_like(total)

    grad = grad_ref[...]
    change = (mm_nt(grad, down_ref[...]) * slope_ref[...].astype(F32)).astype(BF16)
    down_out[...] = mm_tn(act_ref[...], grad).astype(BF16)
    write_rows(weight, parts, table, rows)
    total[...] += mm_nt(change, weight[...])
    weight[...] = mm(turned[...], change).astype(BF16)
    half = keep.shape[0]
    for index in range(2 * half):
        block = weight[pl.ds(pl.multiple_of(places[index] * rows, 16), rows), :]
        (keep if index < half else send)[index % half] = block

    @pl.when(step == pl.num_programs(0) - 1)
    def _():
        dx_ref[...] = total[...].astype(BF16)


TILE = 384


class Weight:
    def __init__(self, parts, table, offset, width):
        self.parts, self.table, self.offset, self.width = parts, table, offset, width
        self.rows = parts[0].shape[1]
        self.count = sum(part.shape[0] for part in parts)
        self.aligned = aligned(self.rows) and offset % TILE == 0 and width % TILE == 0

    def whole(self):
        cut = (0, self.rows, 0, self.width)
        stack = jnp.concatenate(self.parts, axis=0)[jnp.argsort(self.table)]
        return stack[..., self.offset : self.offset + self.width].reshape(-1, self.width)

    def part_specs(self):
        first = self.offset // TILE
        return [
            pl.BlockSpec((self.count // 4, self.rows, TILE), lambda i, *tables, k=k: (k, 0, first + i))
            for _, k in quarters(self.parts)
        ]

    def product(self, x, gelu=False):
        if not self.aligned:
            result = mm(x, self.whole())
            if not gelu:
                return result.astype(BF16)
            slope = jax.vjp(jax.nn.gelu, result)[1](jnp.ones_like(result))[0]
            return jax.nn.gelu(result).astype(BF16), slope.astype(BF16)
        tokens, depth = x.shape
        outs = 2 if gelu else 1
        shape = jax.ShapeDtypeStruct((tokens, self.width), BF16)
        results = pl.pallas_call(
            functools.partial(product_kernel, self.rows, 4, gelu),
            grid_spec=pltpu.PrefetchScalarGridSpec(
                num_scalar_prefetch=1,
                grid=(self.width // TILE,),
                in_specs=[pl.BlockSpec((tokens, depth), lambda i, t: (0, 0))] + self.part_specs(),
                out_specs=[pl.BlockSpec((tokens, TILE), lambda i, t: (0, i))] * outs,
                scratch_shapes=[pltpu.VMEM((depth, TILE), BF16)],
            ),
            out_shape=[shape] * outs,
            compiler_params=pltpu.CompilerParams(vmem_limit_bytes=VMEM_LIMIT),
            cost_estimate=LONG if gelu else FREE,
        )(self.table, x, *[part for part, _ in quarters(self.parts)])
        return results if gelu else results[0]

    def feed_forward_pullback(self, x, grad, down, slope, activated, places, lead):
        if not self.aligned or down.shape[0] != self.width:
            change = (slope.astype(F32) * mm_nt(grad, down)).astype(BF16)
            dx, halves = self.pullback(x, [change], places, lead)
            return dx, mm_tn(activated, grad).astype(BF16), halves
        tokens, depth = x.shape
        half = jax.ShapeDtypeStruct((self.count // 2, self.rows, lead + self.width), BF16)
        half_spec = pl.BlockSpec((self.count // 2, self.rows, TILE), lambda i, t, p: (0, 0, lead // TILE + i))
        full = pl.BlockSpec((tokens, depth), lambda i, t, p: (0, 0))
        units = pl.BlockSpec((tokens, TILE), lambda i, t, p: (0, i))
        unit_rows = pl.BlockSpec((TILE, depth), lambda i, t, p: (i, 0))
        result = pl.pallas_call(
            functools.partial(feed_forward_kernel, self.rows),
            grid_spec=pltpu.PrefetchScalarGridSpec(
                num_scalar_prefetch=2,
                grid=(self.width // TILE,),
                in_specs=[full, full, unit_rows, units, units] + self.part_specs(),
                out_specs=[full, unit_rows, half_spec, half_spec],
                scratch_shapes=[
                    pltpu.VMEM((depth, TILE), BF16),
                    pltpu.VMEM((depth, tokens), BF16),
                    pltpu.VMEM((tokens, depth), F32),
                ],
            ),
            out_shape=[jax.ShapeDtypeStruct((tokens, depth), BF16), jax.ShapeDtypeStruct(down.shape, BF16), half, half],
            compiler_params=pltpu.CompilerParams(vmem_limit_bytes=VMEM_LIMIT),
            cost_estimate=FREE,
        )(self.table, places, x, grad, down, slope, activated, *[part for part, _ in quarters(self.parts)])
        return result[0], result[1], result[2:]

    def grad_specs(self, tokens, grads):
        ends = np.cumsum([grad.shape[1] // TILE for grad in grads])
        bounds = [(int(end) - grad.shape[1] // TILE, int(end)) for end, grad in zip(ends, grads)]
        specs = [
            pl.BlockSpec((tokens, TILE), lambda i, t, low=low, high=high: (0, jnp.clip(i, low, high - 1) - low))
            for low, high in bounds
        ]
        return bounds, specs

    def outer(self, x, grads, places):
        if not self.aligned:
            return split_stack([mm_tn(x, jnp.concatenate(grads, axis=1)).astype(BF16)], places, self.count)
        tokens, depth = x.shape
        bounds, specs = self.grad_specs(tokens, grads)
        half = jax.ShapeDtypeStruct((self.count // 2, self.rows, self.width), BF16)
        half_spec = pl.BlockSpec((self.count // 2, self.rows, TILE), lambda i, t: (0, 0, i))
        return pl.pallas_call(
            functools.partial(outer_kernel, self.rows, bounds),
            grid_spec=pltpu.PrefetchScalarGridSpec(
                num_scalar_prefetch=1,
                grid=(self.width // TILE,),
                in_specs=[pl.BlockSpec((tokens, depth), lambda i, t: (0, 0))] + specs,
                out_specs=[half_spec, half_spec],
                scratch_shapes=[pltpu.VMEM((depth, TILE), BF16), pltpu.VMEM((depth, tokens), BF16)],
            ),
            out_shape=[half, half],
            compiler_params=pltpu.CompilerParams(vmem_limit_bytes=VMEM_LIMIT),
            cost_estimate=FREE,
        )(places, x, *grads)

    def inner(self, grads):
        if not self.aligned:
            return mm_nt(jnp.concatenate(grads, axis=1), self.whole()).astype(BF16)
        tokens, depth = grads[0].shape[0], self.rows * self.count
        bounds, specs = self.grad_specs(tokens, grads)
        return pl.pallas_call(
            functools.partial(inner_kernel, self.rows, bounds),
            grid_spec=pltpu.PrefetchScalarGridSpec(
                num_scalar_prefetch=1,
                grid=(self.width // TILE,),
                in_specs=self.part_specs() + specs,
                out_specs=pl.BlockSpec((tokens, depth), lambda i, t: (0, 0)),
                scratch_shapes=[pltpu.VMEM((depth, TILE), BF16), pltpu.VMEM((tokens, depth), F32)],
            ),
            out_shape=jax.ShapeDtypeStruct((tokens, depth), BF16),
            compiler_params=pltpu.CompilerParams(vmem_limit_bytes=VMEM_LIMIT),
            cost_estimate=FREE,
        )(self.table, *[part for part, _ in quarters(self.parts)], *grads)

    def pullback(self, x, grads, places, lead=0):
        if not self.aligned:
            grad = jnp.concatenate(grads, axis=1)
            halves = split_stack([mm_tn(x, grad).astype(BF16)], places, self.count)
            return mm_nt(grad, self.whole()).astype(BF16), [jnp.pad(h, ((0, 0), (0, 0), (lead, 0))) for h in halves]
        tokens, depth = x.shape
        ends = np.cumsum([grad.shape[1] // TILE for grad in grads])
        bounds = [(int(end) - grad.shape[1] // TILE, int(end)) for end, grad in zip(ends, grads)]
        half = jax.ShapeDtypeStruct((self.count // 2, self.rows, lead + self.width), BF16)
        half_spec = pl.BlockSpec((self.count // 2, self.rows, TILE), lambda i, t, p: (0, 0, lead // TILE + i))
        result = pl.pallas_call(
            functools.partial(pullback_kernel, self.rows, 4, bounds),
            grid_spec=pltpu.PrefetchScalarGridSpec(
                num_scalar_prefetch=2,
                grid=(self.width // TILE,),
                in_specs=[pl.BlockSpec((tokens, depth), lambda i, t, p: (0, 0))]
                + self.part_specs()
                + [
                    pl.BlockSpec((tokens, TILE), lambda i, t, p, low=low, high=high: (0, jnp.clip(i, low, high - 1) - low))
                    for low, high in bounds
                ],
                out_specs=[pl.BlockSpec((tokens, depth), lambda i, t, p: (0, 0)), half_spec, half_spec],
                scratch_shapes=[
                    pltpu.VMEM((depth, TILE), BF16),
                    pltpu.VMEM((depth, tokens), BF16),
                    pltpu.VMEM((tokens, depth), F32),
                ],
            ),
            out_shape=[jax.ShapeDtypeStruct((tokens, depth), BF16), half, half],
            compiler_params=pltpu.CompilerParams(vmem_limit_bytes=VMEM_LIMIT),
            cost_estimate=FREE,
        )(self.table, places, x, *[part for part, _ in quarters(self.parts)], *grads)
        return result[0], result[1:]


class Stream:
    def __init__(self, size, steps):
        self.size, self.steps = size, steps
        self.arriving = None
        self.value = None
        self.done = False
        self.pending = None

    def begin(self, arrived=None):
        try:
            self.pending = self.steps.send(arrived)
        except StopIteration as stop:
            self.pending, self.value, self.done = None, stop.value, True

    def launch(self):
        outgoing, bits, sends = self.pending
        self.arriving, self.pending = exchange(outgoing, bits, self.size, sends), None

    def result(self):
        if self.arriving is None and self.pending is None and not self.done:
            self.begin()
        while not self.done:
            if self.arriving is None:
                self.launch()
            arrived, self.arriving = self.arriving, None
            self.begin(arrived)
        return self.value


def advance(streams, tied, hold=()):
    for stream in streams:
        if stream.arriving is None and stream.pending is None and not stream.done:
            stream.begin()
    moving = [stream for stream in streams if not stream.done]
    ending = [stream for stream in moving if stream.arriving is not None]
    fresh = [stream for stream in moving if stream.arriving is None]
    arrived, outgoing, tied = lax.optimization_barrier(
        ([s.arriving for s in ending], [s.pending[0] for s in fresh], tied)
    )
    for stream, array in zip(fresh, outgoing):
        stream.pending = (array,) + stream.pending[1:]
    for stream, array in zip(ending, arrived):
        stream.arriving = None
        stream.begin(array)
    for stream in moving:
        if not stream.done and stream not in hold:
            stream.launch()
    return tied


def top_sends(size):
    top = bit_count(size) - 1
    return lambda core, i: (i >> top) == core


def doubling(held, order_pair, first=0, twice=False):
    parts = (held,)
    steps = list(zip(*order_pair))[first:]
    for index, bits in enumerate(steps):
        if len(parts) > 1 and not (twice and index == len(steps) - 1):
            parts = (jnp.concatenate(parts, axis=0),)
        arrived = yield lax.optimization_barrier(parts), bits, None
        parts = parts + arrived
    return parts


def gather_all(packed, order_pair, twice):
    return (yield from doubling(packed[None], order_pair, 0, twice))


def gather_core(piece, order_pair, places):
    size = lax.axis_size("dp")
    top = bit_count(size) - 1
    arrived = yield piece, (top, top), top_sends(size)
    mine = (lax.axis_index("dp") >> top) == lax.axis_index("section")
    parts = yield from doubling(jnp.where(mine, piece, arrived)[None], order_pair)
    table, cuts = placement(order_pair, places), [(0, piece.shape[0], 0, piece.shape[1])]
    return assembled_fours(parts, table, cuts) if len(places) > 1 else assembled(parts, table, cuts)


def own_bit(pair):
    position = lax.axis_index("dp")
    return (position >> jnp.where(lax.axis_index("section") == 0, pair[0], pair[1])) & 1


def gather_square(blocks, order_pair, places, cuts):
    first, second = list(zip(*order_pair))[:2]
    a, b = own_bit(first), own_bit(second)
    kept = lax.dynamic_index_in_dim(blocks, a, 0, keepdims=False)
    arrived = yield lax.dynamic_index_in_dim(blocks, 1 - a, 0, keepdims=False), first, None
    held = jnp.stack([kept, arrived])
    kept = lax.dynamic_index_in_dim(held, b, 1, keepdims=False)
    arrived = yield lax.dynamic_index_in_dim(held, 1 - b, 1, keepdims=False), second, None
    parts = yield from doubling(jnp.concatenate([kept, arrived], axis=0), order_pair, 2)
    return assembled(parts, placement(order_pair, places), cuts)


def total_of(terms):
    return sum(term.astype(F32) for term in terms)


def halving(send, kept, order_pair, last=0):
    terms, outgoing = [kept], send
    for bits in reversed(list(zip(*order_pair))[last:]):
        if outgoing is None:
            half = terms[0].shape[0] // 2
            outgoing = total_of([term[half:] for term in terms]).astype(BF16)
            terms = [term[:half] for term in terms]
        arrived = yield outgoing, bits, None
        terms, outgoing = terms + [arrived], None
    return terms


def scatter_all(halves, order_pair):
    terms = yield from halving(*halves, order_pair)
    return total_of(terms)[0].astype(BF16)


def scatter_core(grad, order_pair, places, size):
    halves = split_stack([grad], placement(order_pair, places), 1 << len(places))
    terms = yield from halving(*halves, order_pair)
    top = bit_count(size) - 1
    sends = top_sends(size)
    arrived = yield total_of(terms)[0].astype(BF16), (top, top), lambda core, i: not sends(core, i)
    return (total_of(terms)[0] + arrived.astype(F32)).astype(BF16)


def scatter_square(grad, order_pair, places):
    halves = split_stack([grad], placement(order_pair, places), 1 << len(places))
    terms = yield from halving(*halves, order_pair, 2)
    held = total_of(terms).astype(BF16)
    first, second = list(zip(*order_pair))[:2]
    arrived = yield held[2:], second, None
    held = jnp.stack([held[:2], arrived])
    arrived = yield held[:, 1], first, None
    return jnp.stack([held[:, 0], arrived])


def scatter_small(vector, size):
    position = lax.axis_index("dp")
    held = vector.reshape(size // 4, 4, vector.shape[2])
    for count, low in ((4, 0), (size // 4, 2)):
        own = (position >> low) & (count - 1)

        def part(index):
            return lax.dynamic_index_in_dim(held, index, 1 if low == 0 else 0, keepdims=False)

        outgoing = tuple(part(own ^ other) for other in range(1, count))
        arrived = yield outgoing, tuple(other << low for other in range(1, count)), "flips"
        held = part(own) + sum(arrived)
    return held


def in_square(blocks):
    is_first = lax.axis_index("section") == 0
    middle = jnp.where(is_first, blocks[1:3], jnp.stack([blocks[2], blocks[1]]))
    return jnp.concatenate([blocks[:1], middle, blocks[3:]], axis=0)


SQUARE = ((0, 1), (1, 0))


def gather_in_square(rows):
    held = rows[None]
    for bits in SQUARE:
        arrived = yield held, bits, None
        held = jnp.concatenate([held, arrived], axis=0)
    return in_square(held)


def scatter_in_square(blocks):
    held = in_square(blocks)
    for bits in reversed(SQUARE):
        half = held.shape[0] // 2
        arrived = yield held[half:].astype(BF16), bits, None
        held = held[:half] + arrived.astype(F32)
    return held[0]


def local(
    size,
    bytes_in,
    lengths,
    patch_index,
    patch_count,
    gain_l1,
    qkv_l,
    out_l,
    gain_l2,
    up_l,
    down_l,
    patch_proj,
    gain_g1,
    qkv_g,
    out_g,
    gain_g2,
    up_g,
    down_g,
    out_grad,
):
    core = lax.axis_index("section")
    position = lax.axis_index("dp")
    is_first = core == 0
    seq_rows, half_l = bytes_in.shape[1:]
    width_l, width_g = 2 * half_l, out_g.shape[1]
    half_g = width_g // 2
    rows_l, rows_g = out_l.shape[0], out_g.shape[0]
    units_l, units_g = down_l.shape[0], down_g.shape[0]
    micro_total, slot_total = patch_index.shape[1:]
    slots = micro_total * slot_total
    bits = bit_count(size)
    every = tuple(range(bits))

    def joined(mine, theirs, axis=1):
        low = jnp.where(is_first, mine, theirs)
        high = jnp.where(is_first, theirs, mine)
        return jnp.concatenate([low, high], axis=axis)

    def shared(mine, axis=1):
        return joined(mine, swap(mine), axis)

    def half_of(array, which, axis=1):
        length = array.shape[axis] // 2
        return lax.dynamic_slice_in_dim(array, which * length, length, axis)

    def slope_of(upward):
        return jax.vjp(jax.nn.gelu, upward)[1](jnp.ones_like(upward))[0]

    def summed_cores(part):
        part = part.astype(BF16)
        return part.astype(F32) + swap(part).astype(F32)

    def own_heads(weight):
        return jnp.concatenate([half_of(third, core) for third in jnp.split(weight, 3, axis=1)], axis=1)

    def square_columns(weight):
        pieces = jnp.split(weight, size // 2, axis=1)
        return [jnp.concatenate(pieces[k::4], axis=1) for k in range(4)]

    def gain_block():
        columns = [gain.reshape(rows_l, -1) for gain in (gain_l1, gain_l2, gain_g1, gain_g2)]
        block = jnp.concatenate(columns, axis=1)
        return jnp.pad(block, ((0, 0), (0, TILE - block.shape[1])))

    lows_first = orders(size, (-1, -2, None))
    lows_last = orders(size, (None, -1, -2))
    plane = [o[:2] + (bits - 1,) + o[2:] for o in orders(size, (-1, -2, None))]
    line = orders(size, (None,))
    below, beyond = tuple(range(bits - 1)), tuple(range(2, bits - 1))

    fresh = functools.partial(Stream, size)
    up_width, qkv_width = up_l.shape[1] // 2, 3 * half_g
    square_units = units_g * (size // 8)
    rises, falls = (None, -1, -2), (-1, None, -2)
    order_l = [(bits - 1,) + orders(size, middle)[which] for which, middle in enumerate((falls, rises))]
    order_g = [(bits - 1,) + orders(size, middle)[which] for which, middle in enumerate((rises, falls))]
    gather_g = [(bits - 1,) + order for order in orders(size, rises)]
    table, table_g, places_g = (placement(order, every) for order in (order_l, gather_g, order_g))
    side_l = half_l + half_g
    stream_l = fresh(
        gather_all(
            jnp.concatenate(
                [half_of(out_l, core), half_of(patch_proj, core), gain_block(), own_heads(qkv_l), half_of(up_l, core)],
                axis=1,
            ),
            order_l,
            True,
        )
    )
    stream_down_l = fresh(gather_core(down_l, lows_last, below))
    stream_g = fresh(gather_all(own_heads(qkv_g), gather_g, False))
    stream_out_g = fresh(gather_all(half_of(out_g, core), gather_g, False))
    square = square_columns(half_of(up_g, core))
    one_two = jnp.where(is_first, square[2], square[1])
    two_one = jnp.where(is_first, square[1], square[2])
    blocks = jnp.stack([square[0], one_two, two_one, square[3]]).reshape(2, 2, rows_g, square_units)
    stream_up_g = fresh(gather_square(blocks, plane, every, [(0, rows_g, 0, square_units)]))
    stream_down_g = fresh(
        gather_core(down_g[:, :width_l], line, beyond)
    )

    bias_l = jnp.where(jnp.arange(seq_rows) < lengths[0], 0.0, NEG).astype(F32)[:, None]
    live = (jnp.arange(slot_total)[None, :] < patch_count[0][:, None]).reshape(slots)
    bias_g = jnp.where(live, 0.0, NEG).astype(F32)[:, None]
    positions = patch_index[0].reshape(slots)
    picks = positions[:, None] == jnp.arange(seq_rows)[None, :]
    picks_live = (picks & live[:, None]).astype(BF16)
    picks = picks.astype(BF16)

    advance([stream_l], ())
    seq_inputs = shared(bytes_in[0])
    inputs = seq_inputs.astype(F32)
    scale_l1 = row_scale(inputs)
    seq_grads = shared(out_grad[0])
    grad_top_b = mm(picks_live, seq_grads).astype(BF16)
    scale_l1 = advance([stream_l, stream_up_g, stream_down_l, stream_g], scale_l1)
    stream_top = fresh(gather_in_square(half_of(grad_top_b, core)))
    grad_top_b = advance([stream_l, stream_up_g, stream_down_l, stream_top], grad_top_b)
    advance([stream_l, stream_g, stream_top, stream_up_g], (), [stream_up_g])

    advance([stream_l, stream_g, stream_down_l, stream_up_g, stream_down_g, stream_top, stream_out_g], ())
    parts = stream_l.result()
    front = side_l + TILE
    out_wl, proj_w, gains = assembled_fours(
        parts,
        table,
        [(0, rows_l, 0, half_l), (0, rows_l, half_l, side_l), (0, rows_l, side_l, side_l + LANES)],
        front,
        LONG,
    )
    qkv_wl = Weight(parts, table, front, 3 * half_l)
    up_wl = Weight(parts, table, front + 3 * half_l, up_width)
    gain_one_l, gain_two_l = gains[:, 0].astype(F32), gains[:, 1].astype(F32)
    per = width_g // width_l
    gain_one_g, gain_two_g = (
        gains[:, low : low + per].reshape(width_g).astype(F32) for low in (2, 2 + per)
    )
    normed_l = (inputs * scale_l1 * gain_one_l).astype(BF16)
    projected_l = qkv_wl.product(normed_l)
    own_mixture_l, lse_l = attention_forward(projected_l, bias_l)
    mixture_l = own_mixture_l
    mixture_l, out_wl, proj_w = advance(
        [stream_down_l, stream_up_g, stream_down_g, stream_out_g], (mixture_l, out_wl, proj_w), [stream_up_g]
    )
    mixture_l = advance([stream_g], mixture_l)
    mixture_l, out_wl = shared(mixture_l), shared(out_wl)
    out_own_l = half_of(out_wl, core, 0)
    hidden_l = inputs + mm(mixture_l, out_wl)
    scale_l2 = row_scale(hidden_l)
    normed_l2 = (hidden_l * scale_l2 * gain_two_l).astype(BF16)
    activated_l, slope_l = up_wl.product(normed_l2, gelu=True)
    activated_l, proj_w = advance(
        [stream_down_l, stream_down_g, stream_out_g, stream_up_g], (activated_l, proj_w)
    )
    proj_w = shared(proj_w)
    (down_wl,) = stream_down_l.result()
    partial_l = mm(activated_l, down_wl)
    local_out = half_of(hidden_l, core) + half_of(partial_l, core) + swap(half_of(partial_l, 1 - core))

    boundary = shared(mm(picks, local_out.astype(BF16)).astype(BF16))
    start_rows = mm(boundary, proj_w)
    scale_g1 = row_scale(start_rows)
    square_top = shared(stream_top.result().reshape(4 * slots, half_l))
    scale_g1, square_top = advance([stream_g, stream_out_g, stream_up_g], (scale_g1, square_top))
    qkv_wg = Weight(stream_g.result(), table_g, 0, qkv_width)
    normed_g = (start_rows * scale_g1 * gain_one_g).astype(BF16)
    projected_g = qkv_wg.product(normed_g)
    own_mixture_g, lse_g = attention_forward(projected_g, bias_g)
    mixture_g = own_mixture_g
    mixture_g = advance([stream_out_g], mixture_g)
    (out_wg,) = assembled_fours(stream_out_g.result(), table_g, [(0, rows_g, 0, half_g)])
    out_theirs_g = swap(out_wg)
    mixture_g = shared(mixture_g)
    hidden_g = start_rows + joined(mm(mixture_g, out_wg), mm(mixture_g, out_theirs_g))
    scale_g2 = row_scale(hidden_g)
    normed_g2 = (hidden_g * scale_g2 * gain_two_g).astype(BF16)
    square_normed = fresh(gather_in_square(half_of(normed_g2, core))).result()
    square_normed = shared(square_normed.reshape(4 * slots, half_g))
    (up_wg,) = stream_up_g.result()
    (down_wg,) = stream_down_g.result()
    upward_g = mm(square_normed, up_wg)
    activated_g = jax.nn.gelu(upward_g).astype(BF16)

    grad_down_g = mm_tn(activated_g, square_top).astype(BF16)
    stream_down_g = fresh(scatter_core(grad_down_g, line, beyond, size))
    grad_act_g = mm_nt(square_top, down_wg)
    grad_up_g_rows = jax.vjp(jax.nn.gelu, upward_g)[1](grad_act_g)[0].astype(BF16)
    grad_up_g = mm_tn(square_normed, grad_up_g_rows).astype(BF16)
    stream_up_g = fresh(scatter_square(grad_up_g, plane, every))
    part = mm_nt(grad_up_g_rows, up_wg)
    part = half_of(part, core) + swap(half_of(part, 1 - core).astype(BF16)).astype(F32)
    part = advance([stream_down_g, stream_up_g], part)
    part = shared(fresh(scatter_in_square(part.reshape(4, slots, half_g))).result())
    pulled, grad_gain_g2 = norm_backward(part, hidden_g, scale_g2, gain_two_g)
    grad_hidden_g = jnp.pad(grad_top_b.astype(F32), ((0, 0), (0, width_g - width_l))) + pulled
    grad_hidden_gb = grad_hidden_g.astype(BF16)
    mine_gb, theirs_gb = half_of(grad_hidden_gb, core), half_of(grad_hidden_gb, 1 - core)
    grad_out_g = mm_tn(mixture_g, mine_gb).astype(BF16)
    stream_out_g = fresh(scatter_all(split_stack([grad_out_g], places_g, size), order_g))
    grad_mixture_g = (
        mm_nt(mine_gb, half_of(out_wg, core, 0)) + mm_nt(theirs_gb, half_of(out_theirs_g, core, 0))
    ).astype(BF16)
    partial_g = mm(activated_g, down_wg)
    partial_g = half_of(partial_g, core) + swap(half_of(partial_g, 1 - core).astype(BF16)).astype(F32)
    stream_out = fresh(scatter_in_square(partial_g.reshape(4, slots, half_l)))
    grad_mixture_g = advance([stream_out_g, stream_out], grad_mixture_g)
    grad_projected_g = attention_backward(projected_g, bias_g, lse_g, own_mixture_g, grad_mixture_g)
    part, halves = qkv_wg.pullback(normed_g, grad_projected_g, places_g)
    stream_g = fresh(scatter_all(halves, order_g))
    part = advance([stream_g, stream_out, stream_out_g, stream_down_g], part)
    part = summed_cores(part)
    part = advance([stream_up_g], part)
    pulled, grad_gain_g1 = norm_backward(part, start_rows, scale_g1, gain_one_g)
    grad_start = (grad_hidden_g + pulled).astype(BF16)
    grad_proj = mm_tn(boundary, half_of(grad_start, core)).astype(BF16)

    grad_rows = mm_nt(grad_start, proj_w).astype(BF16)
    grad_local = seq_grads.astype(F32) + mm_tn(picks, grad_rows)
    grad_local_b = grad_local.astype(BF16)
    part, grad_down_l, up_halves = up_wl.feed_forward_pullback(
        normed_l2, grad_local_b, down_wl, slope_l, activated_l, table, side_l
    )
    stream_down_l = fresh(scatter_core(grad_down_l, lows_first, below, size))
    part, up_halves = advance([stream_g, stream_down_g, stream_up_g, stream_out_g], (part, up_halves))
    part = summed_cores(part)
    pulled, grad_gain_l2 = norm_backward(part, hidden_l, scale_l2, gain_two_l)
    grad_hidden_l = grad_local + pulled
    grad_hidden_lb = grad_hidden_l.astype(BF16)
    grad_out_l = mm_tn(mixture_l, half_of(grad_hidden_lb, core)).astype(BF16)
    stream_up_l = fresh(scatter_all(split_stack([grad_out_l, grad_proj], table, size, up_halves), order_l))
    grad_mixture_l = mm_nt(grad_hidden_lb, out_own_l).astype(BF16)
    grad_mixture_l = advance([stream_g, stream_down_l, stream_up_l], grad_mixture_l)
    grad_projected_l = attention_backward(projected_l, bias_l, lse_l, own_mixture_l, grad_mixture_l)
    grad_projected_l = advance([stream_out_g, stream_up_g], grad_projected_l)
    stream_qkv_l = fresh(scatter_all(qkv_wl.outer(normed_l, grad_projected_l, table), order_l))
    grad_projected_l = advance([stream_qkv_l], grad_projected_l)
    part = advance([stream_up_l, stream_up_g, stream_g, stream_down_l], qkv_wl.inner(grad_projected_l))
    part = summed_cores(part)
    pulled, grad_gain_l1 = norm_backward(part, inputs, scale_l1, gain_one_l)
    input_grad = half_of(grad_hidden_l + pulled, core).astype(BF16)[None]
    gains = jnp.concatenate(
        [
            grad.reshape(size, 1, grad.shape[0] // size)
            for grad in (grad_gain_l1, grad_gain_l2, grad_gain_g1, grad_gain_g2)
        ],
        axis=2,
    )
    returned = half_of(hidden_g[:, :width_l], core) + stream_out.result()
    hidden_out = (local_out + mm_tn(picks_live, returned.astype(BF16))).astype(BF16)[None]
    stream_gains = fresh(scatter_small(gains, size))
    input_grad = advance([stream_qkv_l, stream_up_l, stream_down_l, stream_gains], input_grad)
    advance([stream_qkv_l, stream_gains, stream_down_l, stream_out_g, stream_g], ())
    advance([stream_up_l, stream_gains], ())
    advance([stream_qkv_l], ())
    advance([stream_up_l, stream_qkv_l, stream_down_l], ())

    def joined_columns(mine, theirs):
        return joined(mine, theirs).astype(F32)

    def joined_heads(mine, theirs):
        low, high = jnp.where(is_first, mine, theirs), jnp.where(is_first, theirs, mine)
        thirds = [jnp.split(part, 3, axis=1) for part in (low, high)]
        return jnp.concatenate([part for pair in zip(*thirds) for part in pair], axis=1).astype(F32)

    def from_owner(mine, theirs):
        return jnp.where((position >> (bits - 1)) == core, mine, theirs).astype(F32)

    def in_order(blocks):
        low = own_bit((0, 0)), own_bit((1, 1))
        rows, width = blocks.shape[2:]
        placed = []
        for y in range(2):
            for x in range(2):
                dx, dy = x ^ low[0], y ^ low[1]
                index = jnp.where(is_first, 2 * dx + dy, 2 * dy + dx)
                placed.append(lax.dynamic_index_in_dim(blocks.reshape(4, rows, width), index, 0, keepdims=False))
        pieces = [jnp.split(part, size // 8, axis=1) for part in placed]
        return jnp.concatenate([piece for group in zip(*pieces) for piece in group], axis=1)

    down_g_mine = stream_down_g.result()
    total_down_g = from_owner(down_g_mine, swap(down_g_mine))
    total_down_g = jnp.pad(total_down_g, ((0, 0), (0, width_g - width_l)))
    up_g_mine = in_order(stream_up_g.result())
    total_up_g = joined_columns(up_g_mine, swap(up_g_mine))
    g_mine = stream_g.result()
    total_qkv_g = joined_heads(g_mine, swap(g_mine))
    out_g_mine = stream_out_g.result()
    total_out_g = joined_columns(out_g_mine, swap(out_g_mine))
    down_l_mine = stream_down_l.result()
    total_down_l = from_owner(down_l_mine, swap(down_l_mine))
    l_mine = stream_up_l.result()
    l_theirs = swap(l_mine)
    cuts = [0, half_l, side_l, side_l + up_width]
    total_out_l, total_proj, total_up_l = (
        joined_columns(l_mine[:, low:high], l_theirs[:, low:high]) for low, high in zip(cuts, cuts[1:])
    )
    q_mine = stream_qkv_l.result()
    total_qkv_l = joined_heads(q_mine, swap(q_mine))
    gains = stream_gains.result()
    gains = jnp.where(is_first, gains, lax.ppermute(gains, "section", [(0, 1)]))
    total_gain_l1 = gains[:rows_l]
    total_gain_l2 = gains[rows_l : 2 * rows_l]
    total_gain_g1 = gains[2 * rows_l : 2 * rows_l + rows_g]
    total_gain_g2 = gains[2 * rows_l + rows_g :]
    return (
        hidden_out,
        input_grad,
        total_gain_l1,
        total_qkv_l,
        total_out_l,
        total_gain_l2,
        total_up_l,
        total_down_l,
        total_proj,
        total_gain_g1,
        total_qkv_g,
        total_out_g,
        total_gain_g2,
        total_up_g,
        total_down_g,
    )


def solution(mesh):
    rows, vector = P("dp", None), P("dp")
    features = P("dp", None, "section")
    in_specs = (
        features,
        vector,
        P("dp", None, None),
        rows,
        vector,
        rows,
        rows,
        vector,
        rows,
        rows,
        rows,
        vector,
        rows,
        rows,
        vector,
        rows,
        rows,
        features,
    )
    out_specs = (
        features,
        features,
        vector,
        rows,
        rows,
        vector,
        rows,
        rows,
        rows,
        vector,
        rows,
        rows,
        vector,
        rows,
        rows,
    )
    return jax.shard_map(
        functools.partial(local, mesh.shape["dp"]),
        mesh=mesh,
        in_specs=in_specs,
        out_specs=out_specs,
        check_vma=False,
    )
```

```python
import functools

import jax
import jax.numpy as jnp
import numpy as np
from jax import lax
from jax.experimental import pallas as pl
from jax.experimental.pallas import tpu as pltpu
from jax.sharding import PartitionSpec as P

WINDOW = 1536
EPSILON = 1e-06
LANES = 128
GELU_SCALE = (2.0 / np.pi) ** 0.5
GELU_CUBE = 0.044715
NEG = -1e30
VMEM_LIMIT = 48 * 1024 * 1024
FREE = pl.CostEstimate(flops=0, bytes_accessed=0, transcendentals=0)
LONG = pl.CostEstimate(flops=10**11, bytes_accessed=0, transcendentals=0)
F32 = jnp.float32
BF16 = jnp.bfloat16


def mm(left, right):
    return jnp.dot(left, right, preferred_element_type=F32)


def mm_nt(left, right):
    return lax.dot_general(left, right, (((1,), (1,)), ((), ())), preferred_element_type=F32)


def mm_tn(left, right):
    return lax.dot_general(left, right, (((0,), (0,)), ((), ())), preferred_element_type=F32)


def row_scale(values):
    return lax.rsqrt(jnp.mean(values * values, axis=-1, keepdims=True) + EPSILON)


def norm_backward(grad_normed, values, scale, gain):
    grad_gain = jnp.sum(grad_normed * values * scale, axis=0)
    pulled = grad_normed * gain
    inner = jnp.mean(pulled * values, axis=-1, keepdims=True)
    return scale * pulled - values * (scale * scale * scale * inner), grad_gain


def query_block(rows):
    return 256 if rows % 256 == 0 else rows


def head_masks(block):
    lane = lax.broadcasted_iota(jnp.int32, (block, LANES), 1)
    return [lane < LANES // 2, lane >= LANES // 2]


def stacked(values, masks):
    return jnp.concatenate([jnp.where(mask, values, jnp.zeros_like(values)) for mask in masks], axis=0)


def first_lanes(values):
    lane = lax.broadcasted_iota(jnp.int32, (values[0].shape[0], LANES), 1)
    result = jnp.zeros(lane.shape, F32)
    for index, value in enumerate(values):
        result = jnp.where(lane == index, value, result)
    return result.astype(BF16)


def masked_scores(keys, biased, query, extended, bias, start, block, window):
    key_at = lax.broadcasted_iota(jnp.int32, (block, 2 * block), 0)
    query_at = lax.broadcasted_iota(jnp.int32, (block, 2 * block), 1)
    query_at = jnp.where(query_at < block, query_at, query_at - block)
    parts = []
    if start:
        before = mm_nt(biased[:start], extended)
        if window is not None:
            far = lax.broadcasted_iota(jnp.int32, (start, 2 * block), 0)
            own = lax.broadcasted_iota(jnp.int32, (start, 2 * block), 1)
            own = jnp.where(own < block, own, own - block) + start
            before = jnp.where(own - far < window, before, NEG)
        parts.append(before)
    diagonal = mm_nt(keys[start : start + block], query)
    masked = jnp.where(key_at < query_at, diagonal + bias[start : start + block], NEG)
    parts.append(jnp.where(key_at == query_at, diagonal, masked))
    return parts


def ranges(parts):
    low = 0
    for part in parts:
        yield low, low + part.shape[0], part
        low += part.shape[0]


def extend_keys(biased, k_ref, bias_ref):
    biased[:, :LANES] = k_ref[...]
    biased[:, LANES:] = first_lanes([bias_ref[...]])


def attention_forward_kernel(rows, window, q_ref, k_ref, v_ref, bias_ref, o_ref, lse_ref, biased, counted):
    block = query_block(rows)
    masks = head_masks(block)
    score_scale = (LANES // 2) ** (-0.5)
    lane = lax.broadcasted_iota(jnp.int32, (block, LANES), 1)
    extend_keys(biased, k_ref, bias_ref)
    for head, mask in enumerate(head_masks(rows)):
        counted[head] = jnp.where(mask, v_ref[...], jnp.ones_like(v_ref))
    one = first_lanes([jnp.ones((2 * block, 1), F32)])
    query_at = lax.broadcasted_iota(jnp.int32, (2 * block, block), 0)
    query_at = jnp.where(query_at < block, query_at, query_at - block)
    key_at = lax.broadcasted_iota(jnp.int32, (2 * block, block), 1)
    for index in range(rows // block):
        start = index * block
        query = stacked((q_ref[start : start + block, :] * score_scale).astype(BF16), masks)
        extended = jnp.concatenate([query, one], axis=1)
        parts = []
        if start:
            before = mm_nt(extended, biased[:start, :])
            if window is not None:
                far = lax.broadcasted_iota(jnp.int32, (2 * block, start), 1)
                own = lax.broadcasted_iota(jnp.int32, (2 * block, start), 0)
                own = jnp.where(own < block, own, own - block) + start
                before = jnp.where(own - far < window, before, NEG)
            parts.append(before)
        masked = jnp.where(key_at < query_at, mm_nt(extended, biased[start : start + block, :]), NEG)
        parts.append(jnp.where(key_at == query_at, mm_nt(query, k_ref[start : start + block, :]), masked))
        top = functools.reduce(jnp.maximum, [jnp.max(p, axis=1, keepdims=True) for p in parts])
        parts = [jnp.exp(p - top).astype(BF16) for p in parts]
        out, logs = jnp.zeros((block, LANES), F32), jnp.zeros((block, LANES), F32)
        for head, mask in enumerate(masks):
            span = slice(head * block, (head + 1) * block)
            mixed, low = jnp.zeros((block, LANES), F32), 0
            for part in parts:
                high = low + part.shape[1]
                mixed += mm(part[span], counted[head, low:high, :])
                low = high
            other = LANES // 2 if head == 0 else 0
            total = mixed[:, other : other + 1]
            out = jnp.where(mask, mixed * (1.0 / total), out)
            logs = jnp.where(lane == head, top[span] + jnp.log(total), logs)
        o_ref[start : start + block, :] = out.astype(BF16)
        lse_ref[0, :, start : start + block] = logs.T[:2]


def attention_backward_kernel(
    rows,
    window,
    q_ref,
    k_ref,
    v_ref,
    bias_ref,
    lse_ref,
    o_ref,
    do_ref,
    dq_ref,
    dk_ref,
    dv_ref,
    dk_acc,
    dv_acc,
    biased,
    reduced,
):
    block = query_block(rows)
    masks = head_masks(block)
    score_scale = (LANES // 2) ** (-0.5)
    extend_keys(biased, k_ref, bias_ref)
    reduced[:, :LANES] = v_ref[...]
    reduced[:, LANES:] = first_lanes([jnp.full((rows, 1), -1.0, F32)] * 2)
    one = first_lanes([jnp.ones((2 * block, 1), F32)])
    for index in reversed(range(rows // block)):
        start = index * block
        query = stacked((q_ref[start : start + block, :] * score_scale).astype(BF16), masks)
        extended = jnp.concatenate([query, one], axis=1)
        grad = stacked(do_ref[start : start + block, :], masks)
        mixed = o_ref[start : start + block, :].astype(F32)
        delta = jnp.sum(grad.astype(F32) * jnp.concatenate([mixed, mixed], axis=0), axis=1, keepdims=True)
        near = delta.astype(BF16).astype(F32)
        grad_extended = jnp.concatenate([grad, first_lanes([near, delta - near])], axis=1)
        lse = jnp.concatenate([lse_ref[0, head : head + 1, start : start + block] for head in range(2)], axis=1)
        parts = masked_scores(k_ref, biased, query, extended, bias_ref, start, block, window)
        turned = jnp.zeros((2 * block, LANES), F32)
        for low, high, part in ranges(parts):
            weights = jnp.exp(part - lse)
            change = (weights * mm_nt(reduced[low:high, :], grad_extended)).astype(BF16)
            dv = mm(weights.astype(BF16), grad)
            dk = mm(change, query)
            if index == rows // block - 1:
                dv_acc[low:high, :] = dv
                dk_acc[low:high, :] = dk
            else:
                dv_acc[low:high, :] += dv
                dk_acc[low:high, :] += dk
            turned += mm_tn(change, k_ref[low:high, :])
        dq = jnp.where(masks[0], turned[:block], turned[block:]) * score_scale
        dq_ref[start : start + block, :] = dq.astype(BF16)
    dk_ref[...] = dk_acc[...].astype(BF16)
    dv_ref[...] = dv_acc[...].astype(BF16)


def attention_specs(rows, width):
    pairs = width // LANES
    wide = lambda part: pl.BlockSpec((rows, LANES), lambda i, part=part: (0, part * pairs + i))
    bias = pl.BlockSpec((rows, 1), lambda i: (0, 0))
    return pairs, wide, bias


def attention_forward(projected, bias):
    rows, width = projected.shape[0], projected.shape[1] // 3
    pairs, wide, bias_spec = attention_specs(rows, width)
    window = WINDOW if rows > WINDOW else None
    return pl.pallas_call(
        functools.partial(attention_forward_kernel, rows, window),
        grid=(pairs,),
        in_specs=[wide(0), wide(1), wide(2), bias_spec],
        out_specs=[wide(0), pl.BlockSpec((1, 2, rows), lambda i: (i, 0, 0))],
        out_shape=[
            jax.ShapeDtypeStruct((rows, width), BF16),
            jax.ShapeDtypeStruct((pairs, 2, rows), F32),
        ],
        scratch_shapes=[pltpu.VMEM((rows, 2 * LANES), BF16), pltpu.VMEM((2, rows, LANES), BF16)],
        compiler_params=pltpu.CompilerParams(vmem_limit_bytes=VMEM_LIMIT),
        cost_estimate=FREE,
    )(projected, projected, projected, bias)


def attention_backward(projected, bias, lse, mixture, grad_mixture):
    rows, width = grad_mixture.shape
    pairs, wide, bias_spec = attention_specs(rows, width)
    window = WINDOW if rows > WINDOW else None
    shape = jax.ShapeDtypeStruct((rows, width), BF16)
    return pl.pallas_call(
        functools.partial(attention_backward_kernel, rows, window),
        grid=(pairs,),
        in_specs=[
            wide(0),
            wide(1),
            wide(2),
            bias_spec,
            pl.BlockSpec((1, 2, rows), lambda i: (i, 0, 0)),
            wide(0),
            wide(0),
        ],
        out_specs=[wide(0), wide(0), wide(0)],
        out_shape=[shape, shape, shape],
        scratch_shapes=[
            pltpu.VMEM((rows, LANES), F32),
            pltpu.VMEM((rows, LANES), F32),
            pltpu.VMEM((rows, 2 * LANES), BF16),
            pltpu.VMEM((rows, 2 * LANES), BF16),
        ],
        compiler_params=pltpu.CompilerParams(vmem_limit_bytes=VMEM_LIMIT),
        cost_estimate=LONG,
    )(projected, projected, projected, bias, lse, mixture, grad_mixture)


def swap(array):
    return lax.ppermute(array, "section", [(0, 1), (1, 0)])


def exchange(array, bits, size, sends=None):
    if sends == "flips":
        return tuple(
            lax.ppermute(part, "dp", [(i, i ^ flip) for i in range(size)]) for part, flip in zip(array, bits)
        )
    pairs = [
        (core * size + i, core * size + (i ^ (1 << bit)))
        for core, bit in enumerate(bits)
        for i in range(size)
        if sends is None or sends(core, i)
    ]
    return jax.tree.map(lambda part: lax.ppermute(part, ("section", "dp"), pairs), array)


def bit_count(size):
    return size.bit_length() - 1


def orders(size, middle):
    bits = bit_count(size)
    others = tuple(reversed(range(2, bits - 1)))
    result = []
    for core in range(2):
        lowest = (0, 1) if core == 0 else (1, 0)
        order = ()
        for entry in middle:
            order += others if entry is None else (lowest[0] if entry == -1 else lowest[1],)
        result.append(order)
    return result


def mask_of(index, order, places):
    return sum(((index >> t) & 1) << places.index(bit) for t, bit in enumerate(order))


def placement(order_pair, places):
    position = lax.axis_index("dp")
    own = sum(((position >> bit) & 1) << p for p, bit in enumerate(places))
    count = 1 << len(places)
    masks = [jnp.asarray([mask_of(j, order, places) for j in range(count)], jnp.int32) for order in order_pair]
    return (own ^ jnp.where(lax.axis_index("section") == 0, masks[0], masks[1])).astype(jnp.int32)


def aligned(rows, cuts=()):
    return rows % 16 == 0 and all(c % LANES == 0 and r % 16 == 0 for r0, r1, c0, c1 in cuts for r, c in ((r0, c0), (r1, c1)))


def assembly_kernel(bounds, cuts, table, *refs):
    step = pl.program_id(0)
    parts, outs = refs[: len(bounds)], refs[len(bounds) :]

    def store(ref):
        for (r0, r1, c0, c1), out in zip(cuts, outs):
            out[...] = ref[0, r0:r1, c0:c1]

    for (low, high), ref in zip(bounds, parts):
        pl.when((step >= low) & (step < high))(functools.partial(store, ref))


def assembled(parts, table, cuts, offset=0, width=None):
    rows = parts[0].shape[1]
    width = width or parts[0].shape[2]
    ends = np.cumsum([part.shape[0] for part in parts])
    count = int(ends[-1])
    bounds = [(int(end) - part.shape[0], int(end)) for end, part in zip(ends, parts)]
    shapes = [(count * (r1 - r0), c1 - c0) for r0, r1, c0, c1 in cuts]
    if not aligned(rows, cuts):
        stack = jnp.concatenate(parts, axis=0)[jnp.argsort(table)][..., offset : offset + width]
        return [stack[:, r0:r1, c0:c1].reshape(s) for (r0, r1, c0, c1), s in zip(cuts, shapes)]
    return pl.pallas_call(
        functools.partial(assembly_kernel, bounds, cuts),
        grid_spec=pltpu.PrefetchScalarGridSpec(
            num_scalar_prefetch=1,
            grid=(count,),
            in_specs=[
                pl.BlockSpec(
                    (1, rows, width),
                    lambda j, t, low=low, high=high: (jnp.clip(j, low, high - 1) - low, 0, offset // width),
                )
                for low, high in bounds
            ],
            out_specs=[pl.BlockSpec((r1 - r0, c1 - c0), lambda j, t: (t[j], 0)) for r0, r1, c0, c1 in cuts],
        ),
        out_shape=[jax.ShapeDtypeStruct(s, parts[0].dtype) for s in shapes],
        compiler_params=pltpu.CompilerParams(vmem_limit_bytes=VMEM_LIMIT),
        cost_estimate=FREE,
    )(table, *parts)


def quarters(parts):
    if len(parts) == 4:
        return [(part, 0) for part in parts]
    return [(part, k) for part in parts for k in range(2)]


def whole_kernel(cuts, table, *refs):
    quarter = refs[0].shape[0]
    for index in range(4 * quarter):
        part, place = refs[index // quarter], table[index]
        for (r0, r1, c0, c1), out in zip(cuts, refs[4:]):
            rows = r1 - r0
            out[pl.ds(pl.multiple_of(place * rows, 16), rows), :] = part[index % quarter, r0:r1, c0:c1]


def assembled_fours(parts, table, cuts, width=None, cost=FREE):
    rows = parts[0].shape[1]
    width = width or parts[0].shape[2]
    count = sum(part.shape[0] for part in parts)
    shapes = [(count * (r1 - r0), c1 - c0) for r0, r1, c0, c1 in cuts]
    if not aligned(rows, cuts):
        stack = jnp.concatenate(parts, axis=0)[jnp.argsort(table)]
        return [stack[:, r0:r1, c0:c1].reshape(s) for (r0, r1, c0, c1), s in zip(cuts, shapes)]
    return pl.pallas_call(
        functools.partial(whole_kernel, cuts),
        grid_spec=pltpu.PrefetchScalarGridSpec(
            num_scalar_prefetch=1,
            grid=(1,),
            in_specs=[pl.BlockSpec((count // 4, rows, width), lambda j, t, k=k: (k, 0, 0)) for _, k in quarters(parts)],
            out_specs=[pl.BlockSpec(shape, lambda j, t: (0, 0)) for shape in shapes],
        ),
        out_shape=[jax.ShapeDtypeStruct(s, parts[0].dtype) for s in shapes],
        compiler_params=pltpu.CompilerParams(vmem_limit_bytes=VMEM_LIMIT),
        cost_estimate=cost,
    )(table, *[part for part, _ in quarters(parts)])


def split_kernel(half, count, table, *refs):
    send, keep = refs[-2:]
    rows = refs[0].shape[0] // (2 * half)
    for index in range(2 * half):
        place, base = table[index], 0
        for ref in refs[:count]:
            block = ref[pl.ds(pl.multiple_of(place * rows, 16), rows), :]
            (keep if index < half else send)[index % half, :, base : base + ref.shape[1]] = block
            base += ref.shape[1]


def split_stack(grads, table, count, into=None):
    half, rows = count // 2, grads[0].shape[0] // count
    width = sum(grad.shape[1] for grad in grads)
    if not (aligned(rows) and all(grad.shape[1] % LANES == 0 for grad in grads)):
        stack = jnp.concatenate([grad.reshape(count, rows, grad.shape[1]) for grad in grads], axis=2)[table]
        halves = [stack[half:], stack[:half]]
        if into is not None:
            halves = [jnp.concatenate([part, old[..., width:]], axis=2) for part, old in zip(halves, into)]
        return halves
    full = width if into is None else into[0].shape[2]
    shape = jax.ShapeDtypeStruct((half, rows, full), BF16)
    into = [] if into is None else list(into)
    half_spec = pl.BlockSpec((half, rows, width), lambda j, t: (0, 0, 0))
    return pl.pallas_call(
        functools.partial(split_kernel, half, len(grads)),
        grid_spec=pltpu.PrefetchScalarGridSpec(
            num_scalar_prefetch=1,
            grid=(1,),
            in_specs=[pl.BlockSpec(grad.shape, lambda j, t: (0, 0)) for grad in grads]
            + [pl.BlockSpec(memory_space=pl.ANY) for _ in into],
            out_specs=[half_spec, half_spec],
        ),
        out_shape=[shape, shape],
        input_output_aliases={1 + len(grads) + k: k for k in range(len(into))},
        compiler_params=pltpu.CompilerParams(vmem_limit_bytes=VMEM_LIMIT),
        cost_estimate=FREE,
    )(table, *grads, *into)


def write_rows(target, parts, table, rows):
    index = 0
    for part in parts:
        for k in range(part.shape[0]):
            target[pl.ds(pl.multiple_of(table[index] * rows, 16), rows), :] = part[k]
            index += 1


def product_kernel(rows, count, gelu, table, x_ref, *refs):
    parts, outs, weight = refs[:count], refs[count:-1], refs[-1]
    write_rows(weight, parts, table, rows)
    result = jnp.dot(x_ref[...], weight[...], preferred_element_type=F32)
    if not gelu:
        outs[0][...] = result.astype(outs[0].dtype)
        return
    square = result * result
    bend = jnp.tanh(GELU_SCALE * (result + GELU_CUBE * (result * square)))
    outs[0][...] = (0.5 * result * (1.0 + bend)).astype(outs[0].dtype)
    slope = 0.5 * (1.0 + bend)
    slope += (0.5 * GELU_SCALE) * result * (1.0 - bend * bend) * (1.0 + (3.0 * GELU_CUBE) * square)
    outs[1][...] = slope.astype(outs[1].dtype)


def outer_kernel(rows, bounds, places, x_ref, *refs):
    grads, (send, keep, weight, turned) = refs[: len(bounds)], refs[len(bounds) :]
    step = pl.program_id(0)

    @pl.when(step == 0)
    def _():
        turned[...] = x_ref[...].T

    grad = grads[-1][...]
    for (low, high), ref in list(zip(bounds, grads))[:-1]:
        grad = jnp.where((step >= low) & (step < high), ref[...], grad)
    weight[...] = mm(turned[...], grad).astype(BF16)
    half = keep.shape[0]
    for index in range(2 * half):
        block = weight[pl.ds(pl.multiple_of(places[index] * rows, 16), rows), :]
        (keep if index < half else send)[index % half] = block


def inner_kernel(rows, bounds, table, *refs):
    parts, grads, (dx_ref, weight, total) = refs[:4], refs[4 : 4 + len(bounds)], refs[4 + len(bounds) :]
    step = pl.program_id(0)

    @pl.when(step == 0)
    def _():
        total[...] = jnp.zeros_like(total)

    write_rows(weight, parts, table, rows)
    grad = grads[-1][...]
    for (low, high), ref in list(zip(bounds, grads))[:-1]:
        grad = jnp.where((step >= low) & (step < high), ref[...], grad)
    total[...] += mm_nt(grad, weight[...])

    @pl.when(step == pl.num_programs(0) - 1)
    def _():
        dx_ref[...] = total[...].astype(BF16)


def pullback_kernel(rows, count, bounds, table, places, x_ref, *refs):
    parts, grads = refs[:count], refs[count : count + len(bounds)]
    dx_ref, send, keep, weight, turned, total = refs[count + len(bounds) :]
    step = pl.program_id(0)

    @pl.when(step == 0)
    def _():
        turned[...] = x_ref[...].T
        total[...] = jnp.zeros_like(total)

    write_rows(weight, parts, table, rows)
    grad = grads[-1][...]
    for (low, high), ref in list(zip(bounds, grads))[:-1]:
        grad = jnp.where((step >= low) & (step < high), ref[...], grad)
    total[...] += lax.dot_general(grad, weight[...], (((1,), (1,)), ((), ())), preferred_element_type=F32)
    weight[...] = jnp.dot(turned[...], grad, preferred_element_type=F32).astype(BF16)
    half = keep.shape[0]
    for index in range(2 * half):
        block = weight[pl.ds(pl.multiple_of(places[index] * rows, 16), rows), :]
        (keep if index < half else send)[index % half] = block

    @pl.when(step == pl.num_programs(0) - 1)
    def _():
        dx_ref[...] = total[...].astype(BF16)


def feed_forward_kernel(rows, table, places, x_ref, grad_ref, down_ref, slope_ref, act_ref, *refs):
    parts, (dx_ref, down_out, send, keep, weight, turned, total) = refs[:4], refs[4:]
    step = pl.program_id(0)

    @pl.when(step == 0)
    def _():
        turned[...] = x_ref[...].T
        total[...] = jnp.zeros_like(total)

    grad = grad_ref[...]
    change = (mm_nt(grad, down_ref[...]) * slope_ref[...].astype(F32)).astype(BF16)
    down_out[...] = mm_tn(act_ref[...], grad).astype(BF16)
    write_rows(weight, parts, table, rows)
    total[...] += mm_nt(change, weight[...])
    weight[...] = mm(turned[...], change).astype(BF16)
    half = keep.shape[0]
    for index in range(2 * half):
        block = weight[pl.ds(pl.multiple_of(places[index] * rows, 16), rows), :]
        (keep if index < half else send)[index % half] = block

    @pl.when(step == pl.num_programs(0) - 1)
    def _():
        dx_ref[...] = total[...].astype(BF16)


TILE = 384


class Weight:
    def __init__(self, parts, table, offset, width, tile=TILE):
        self.parts, self.table, self.offset, self.width, self.tile = parts, table, offset, width, tile
        self.rows = parts[0].shape[1]
        self.count = sum(part.shape[0] for part in parts)
        self.aligned = aligned(self.rows) and offset % tile == 0 and width % tile == 0

    def whole(self):
        cut = (0, self.rows, 0, self.width)
        stack = jnp.concatenate(self.parts, axis=0)[jnp.argsort(self.table)]
        return stack[..., self.offset : self.offset + self.width].reshape(-1, self.width)

    def part_specs(self):
        first = self.offset // self.tile
        return [
            pl.BlockSpec((self.count // 4, self.rows, self.tile), lambda i, *tables, k=k: (k, 0, first + i))
            for _, k in quarters(self.parts)
        ]

    def product(self, x, gelu=False):
        if not self.aligned:
            result = mm(x, self.whole())
            if not gelu:
                return result.astype(BF16)
            slope = jax.vjp(jax.nn.gelu, result)[1](jnp.ones_like(result))[0]
            return jax.nn.gelu(result).astype(BF16), slope.astype(BF16)
        tokens, depth = x.shape
        outs = 2 if gelu else 1
        shape = jax.ShapeDtypeStruct((tokens, self.width), BF16)
        results = pl.pallas_call(
            functools.partial(product_kernel, self.rows, 4, gelu),
            grid_spec=pltpu.PrefetchScalarGridSpec(
                num_scalar_prefetch=1,
                grid=(self.width // self.tile,),
                in_specs=[pl.BlockSpec((tokens, depth), lambda i, t: (0, 0))] + self.part_specs(),
                out_specs=[pl.BlockSpec((tokens, self.tile), lambda i, t: (0, i))] * outs,
                scratch_shapes=[pltpu.VMEM((depth, self.tile), BF16)],
            ),
            out_shape=[shape] * outs,
            compiler_params=pltpu.CompilerParams(vmem_limit_bytes=VMEM_LIMIT),
            cost_estimate=LONG if gelu else FREE,
        )(self.table, x, *[part for part, _ in quarters(self.parts)])
        return results if gelu else results[0]

    def feed_forward_pullback(self, x, grad, down, slope, activated, places, lead):
        if not self.aligned or down.shape[0] != self.width:
            change = (slope.astype(F32) * mm_nt(grad, down)).astype(BF16)
            dx, halves = self.pullback(x, [change], places, lead)
            return dx, mm_tn(activated, grad).astype(BF16), halves
        tokens, depth = x.shape
        half = jax.ShapeDtypeStruct((self.count // 2, self.rows, lead + self.width), BF16)
        half_spec = pl.BlockSpec((self.count // 2, self.rows, self.tile), lambda i, t, p: (0, 0, lead // self.tile + i))
        full = pl.BlockSpec((tokens, depth), lambda i, t, p: (0, 0))
        units = pl.BlockSpec((tokens, self.tile), lambda i, t, p: (0, i))
        unit_rows = pl.BlockSpec((self.tile, depth), lambda i, t, p: (i, 0))
        result = pl.pallas_call(
            functools.partial(feed_forward_kernel, self.rows),
            grid_spec=pltpu.PrefetchScalarGridSpec(
                num_scalar_prefetch=2,
                grid=(self.width // self.tile,),
                in_specs=[full, full, unit_rows, units, units] + self.part_specs(),
                out_specs=[full, unit_rows, half_spec, half_spec],
                scratch_shapes=[
                    pltpu.VMEM((depth, self.tile), BF16),
                    pltpu.VMEM((depth, tokens), BF16),
                    pltpu.VMEM((tokens, depth), F32),
                ],
            ),
            out_shape=[jax.ShapeDtypeStruct((tokens, depth), BF16), jax.ShapeDtypeStruct(down.shape, BF16), half, half],
            compiler_params=pltpu.CompilerParams(vmem_limit_bytes=VMEM_LIMIT),
            cost_estimate=FREE,
        )(self.table, places, x, grad, down, slope, activated, *[part for part, _ in quarters(self.parts)])
        return result[0], result[1], result[2:]

    def grad_specs(self, tokens, grads):
        ends = np.cumsum([grad.shape[1] // self.tile for grad in grads])
        bounds = [(int(end) - grad.shape[1] // self.tile, int(end)) for end, grad in zip(ends, grads)]
        specs = [
            pl.BlockSpec((tokens, self.tile), lambda i, t, low=low, high=high: (0, jnp.clip(i, low, high - 1) - low))
            for low, high in bounds
        ]
        return bounds, specs

    def outer(self, x, grads, places):
        if not self.aligned:
            return split_stack([mm_tn(x, jnp.concatenate(grads, axis=1)).astype(BF16)], places, self.count)
        tokens, depth = x.shape
        bounds, specs = self.grad_specs(tokens, grads)
        half = jax.ShapeDtypeStruct((self.count // 2, self.rows, self.width), BF16)
        half_spec = pl.BlockSpec((self.count // 2, self.rows, self.tile), lambda i, t: (0, 0, i))
        return pl.pallas_call(
            functools.partial(outer_kernel, self.rows, bounds),
            grid_spec=pltpu.PrefetchScalarGridSpec(
                num_scalar_prefetch=1,
                grid=(self.width // self.tile,),
                in_specs=[pl.BlockSpec((tokens, depth), lambda i, t: (0, 0))] + specs,
                out_specs=[half_spec, half_spec],
                scratch_shapes=[pltpu.VMEM((depth, self.tile), BF16), pltpu.VMEM((depth, tokens), BF16)],
            ),
            out_shape=[half, half],
            compiler_params=pltpu.CompilerParams(vmem_limit_bytes=VMEM_LIMIT),
            cost_estimate=FREE,
        )(places, x, *grads)

    def inner(self, grads):
        if not self.aligned:
            return mm_nt(jnp.concatenate(grads, axis=1), self.whole()).astype(BF16)
        tokens, depth = grads[0].shape[0], self.rows * self.count
        bounds, specs = self.grad_specs(tokens, grads)
        return pl.pallas_call(
            functools.partial(inner_kernel, self.rows, bounds),
            grid_spec=pltpu.PrefetchScalarGridSpec(
                num_scalar_prefetch=1,
                grid=(self.width // self.tile,),
                in_specs=self.part_specs() + specs,
                out_specs=pl.BlockSpec((tokens, depth), lambda i, t: (0, 0)),
                scratch_shapes=[pltpu.VMEM((depth, self.tile), BF16), pltpu.VMEM((tokens, depth), F32)],
            ),
            out_shape=jax.ShapeDtypeStruct((tokens, depth), BF16),
            compiler_params=pltpu.CompilerParams(vmem_limit_bytes=VMEM_LIMIT),
            cost_estimate=FREE,
        )(self.table, *[part for part, _ in quarters(self.parts)], *grads)

    def pullback(self, x, grads, places, lead=0):
        if not self.aligned:
            grad = jnp.concatenate(grads, axis=1)
            halves = split_stack([mm_tn(x, grad).astype(BF16)], places, self.count)
            return mm_nt(grad, self.whole()).astype(BF16), [jnp.pad(h, ((0, 0), (0, 0), (lead, 0))) for h in halves]
        tokens, depth = x.shape
        ends = np.cumsum([grad.shape[1] // self.tile for grad in grads])
        bounds = [(int(end) - grad.shape[1] // self.tile, int(end)) for end, grad in zip(ends, grads)]
        half = jax.ShapeDtypeStruct((self.count // 2, self.rows, lead + self.width), BF16)
        half_spec = pl.BlockSpec((self.count // 2, self.rows, self.tile), lambda i, t, p: (0, 0, lead // self.tile + i))
        result = pl.pallas_call(
            functools.partial(pullback_kernel, self.rows, 4, bounds),
            grid_spec=pltpu.PrefetchScalarGridSpec(
                num_scalar_prefetch=2,
                grid=(self.width // self.tile,),
                in_specs=[pl.BlockSpec((tokens, depth), lambda i, t, p: (0, 0))]
                + self.part_specs()
                + [
                    pl.BlockSpec((tokens, self.tile), lambda i, t, p, low=low, high=high: (0, jnp.clip(i, low, high - 1) - low))
                    for low, high in bounds
                ],
                out_specs=[pl.BlockSpec((tokens, depth), lambda i, t, p: (0, 0)), half_spec, half_spec],
                scratch_shapes=[
                    pltpu.VMEM((depth, self.tile), BF16),
                    pltpu.VMEM((depth, tokens), BF16),
                    pltpu.VMEM((tokens, depth), F32),
                ],
            ),
            out_shape=[jax.ShapeDtypeStruct((tokens, depth), BF16), half, half],
            compiler_params=pltpu.CompilerParams(vmem_limit_bytes=VMEM_LIMIT),
            cost_estimate=FREE,
        )(self.table, places, x, *[part for part, _ in quarters(self.parts)], *grads)
        return result[0], result[1:]


class Stream:
    def __init__(self, size, steps):
        self.size, self.steps = size, steps
        self.arriving = None
        self.value = None
        self.done = False
        self.pending = None

    def begin(self, arrived=None):
        try:
            self.pending = self.steps.send(arrived)
        except StopIteration as stop:
            self.pending, self.value, self.done = None, stop.value, True

    def launch(self):
        outgoing, bits, sends = self.pending
        self.arriving, self.pending = exchange(outgoing, bits, self.size, sends), None

    def result(self):
        if self.arriving is None and self.pending is None and not self.done:
            self.begin()
        while not self.done:
            if self.arriving is None:
                self.launch()
            arrived, self.arriving = self.arriving, None
            self.begin(arrived)
        return self.value


def advance(streams, tied, hold=()):
    for stream in streams:
        if stream.arriving is None and stream.pending is None and not stream.done:
            stream.begin()
    moving = [stream for stream in streams if not stream.done]
    ending = [stream for stream in moving if stream.arriving is not None]
    fresh = [stream for stream in moving if stream.arriving is None]
    arrived, outgoing, tied = lax.optimization_barrier(
        ([s.arriving for s in ending], [s.pending[0] for s in fresh], tied)
    )
    for stream, array in zip(fresh, outgoing):
        stream.pending = (array,) + stream.pending[1:]
    for stream, array in zip(ending, arrived):
        stream.arriving = None
        stream.begin(array)
    for stream in moving:
        if not stream.done and stream not in hold:
            stream.launch()
    return tied


def top_sends(size):
    top = bit_count(size) - 1
    return lambda core, i: (i >> top) == core


def doubling(held, order_pair, first=0, twice=False):
    parts = (held,)
    steps = list(zip(*order_pair))[first:]
    for index, bits in enumerate(steps):
        if len(parts) > 1 and not (twice and index == len(steps) - 1):
            parts = (jnp.concatenate(parts, axis=0),)
        arrived = yield lax.optimization_barrier(parts), bits, None
        parts = parts + arrived
    return parts


def gather_all(packed, order_pair, twice):
    return (yield from doubling(packed[None], order_pair, 0, twice))


def gather_core(piece, order_pair, places):
    size = lax.axis_size("dp")
    top = bit_count(size) - 1
    arrived = yield piece, (top, top), top_sends(size)
    mine = (lax.axis_index("dp") >> top) == lax.axis_index("section")
    parts = yield from doubling(jnp.where(mine, piece, arrived)[None], order_pair)
    table, cuts = placement(order_pair, places), [(0, piece.shape[0], 0, piece.shape[1])]
    return assembled_fours(parts, table, cuts) if len(places) > 1 else assembled(parts, table, cuts)


def own_bit(pair):
    position = lax.axis_index("dp")
    return (position >> jnp.where(lax.axis_index("section") == 0, pair[0], pair[1])) & 1


def gather_square(blocks, order_pair, places, cuts):
    first, second = list(zip(*order_pair))[:2]
    a, b = own_bit(first), own_bit(second)
    kept = lax.dynamic_index_in_dim(blocks, a, 0, keepdims=False)
    arrived = yield lax.dynamic_index_in_dim(blocks, 1 - a, 0, keepdims=False), first, None
    held = jnp.stack([kept, arrived])
    kept = lax.dynamic_index_in_dim(held, b, 1, keepdims=False)
    arrived = yield lax.dynamic_index_in_dim(held, 1 - b, 1, keepdims=False), second, None
    parts = yield from doubling(jnp.concatenate([kept, arrived], axis=0), order_pair, 2)
    return assembled(parts, placement(order_pair, places), cuts)


def total_of(terms):
    return sum(term.astype(F32) for term in terms)


def halving(send, kept, order_pair, last=0):
    terms, outgoing = [kept], send
    for bits in reversed(list(zip(*order_pair))[last:]):
        if outgoing is None:
            half = terms[0].shape[0] // 2
            outgoing = total_of([term[half:] for term in terms]).astype(BF16)
            terms = [term[:half] for term in terms]
        arrived = yield outgoing, bits, None
        terms, outgoing = terms + [arrived], None
    return terms


def scatter_all(halves, order_pair):
    terms = yield from halving(*halves, order_pair)
    return total_of(terms)[0].astype(BF16)


def scatter_core(grad, order_pair, places, size):
    halves = split_stack([grad], placement(order_pair, places), 1 << len(places))
    terms = yield from halving(*halves, order_pair)
    top = bit_count(size) - 1
    sends = top_sends(size)
    arrived = yield total_of(terms)[0].astype(BF16), (top, top), lambda core, i: not sends(core, i)
    return (total_of(terms)[0] + arrived.astype(F32)).astype(BF16)


def scatter_square(grad, order_pair, places):
    halves = split_stack([grad], placement(order_pair, places), 1 << len(places))
    terms = yield from halving(*halves, order_pair, 2)
    held = total_of(terms).astype(BF16)
    first, second = list(zip(*order_pair))[:2]
    arrived = yield held[2:], second, None
    held = jnp.stack([held[:2], arrived])
    arrived = yield held[:, 1], first, None
    return jnp.stack([held[:, 0], arrived])


def scatter_small(vector, size):
    position = lax.axis_index("dp")
    held = vector.reshape(size // 4, 4, vector.shape[2])
    for count, low in ((4, 0), (size // 4, 2)):
        own = (position >> low) & (count - 1)

        def part(index):
            return lax.dynamic_index_in_dim(held, index, 1 if low == 0 else 0, keepdims=False)

        outgoing = tuple(part(own ^ other) for other in range(1, count))
        arrived = yield outgoing, tuple(other << low for other in range(1, count)), "flips"
        held = part(own) + sum(arrived)
    return held


def in_square(blocks, whose=0):
    is_first = lax.axis_index("section") == whose
    middle = jnp.where(is_first, blocks[1:3], jnp.stack([blocks[2], blocks[1]]))
    return jnp.concatenate([blocks[:1], middle, blocks[3:]], axis=0)


SQUARE = ((0, 1), (1, 0))


def gather_in_square(rows):
    held = rows[None]
    for bits in SQUARE:
        arrived = yield held, bits, None
        held = jnp.concatenate([held, arrived], axis=0)
    return in_square(held)


def scatter_in_square(blocks):
    held = in_square(blocks)
    for bits in reversed(SQUARE):
        half = held.shape[0] // 2
        arrived = yield held[half:].astype(BF16), bits, None
        held = held[:half] + arrived.astype(F32)
    return held[0]


def local(
    size,
    bytes_in,
    lengths,
    patch_index,
    patch_count,
    gain_l1,
    qkv_l,
    out_l,
    gain_l2,
    up_l,
    down_l,
    patch_proj,
    gain_g1,
    qkv_g,
    out_g,
    gain_g2,
    up_g,
    down_g,
    out_grad,
):
    core = lax.axis_index("section")
    position = lax.axis_index("dp")
    is_first = core == 0
    seq_rows, half_l = bytes_in.shape[1:]
    width_l, width_g = 2 * half_l, out_g.shape[1]
    half_g = width_g // 2
    rows_l, rows_g = out_l.shape[0], out_g.shape[0]
    units_l, units_g = down_l.shape[0], down_g.shape[0]
    micro_total, slot_total = patch_index.shape[1:]
    slots = micro_total * slot_total
    bits = bit_count(size)
    every = tuple(range(bits))

    def joined(mine, theirs, axis=1):
        low = jnp.where(is_first, mine, theirs)
        high = jnp.where(is_first, theirs, mine)
        return jnp.concatenate([low, high], axis=axis)

    def shared(mine, axis=1):
        return joined(mine, swap(mine), axis)

    def half_of(array, which, axis=1):
        length = array.shape[axis] // 2
        return lax.dynamic_slice_in_dim(array, which * length, length, axis)

    def slope_of(upward):
        return jax.vjp(jax.nn.gelu, upward)[1](jnp.ones_like(upward))[0]

    def summed_cores(part):
        part = part.astype(BF16)
        return part.astype(F32) + swap(part).astype(F32)

    def own_heads(weight):
        return jnp.concatenate([half_of(third, core) for third in jnp.split(weight, 3, axis=1)], axis=1)

    def square_columns(weight):
        pieces = jnp.split(weight, size // 2, axis=1)
        return [jnp.concatenate(pieces[k::4], axis=1) for k in range(4)]

    def gain_block():
        columns = [gain.reshape(rows_l, -1) for gain in (gain_l1, gain_l2, gain_g1, gain_g2)]
        block = jnp.concatenate(columns, axis=1)
        return jnp.pad(block, ((0, 0), (0, TILE - block.shape[1])))

    lows_first = orders(size, (-1, -2, None))
    lows_last = orders(size, (None, -1, -2))
    plane = [o[:2] + (bits - 1,) + o[2:] for o in orders(size, (-1, -2, None))]
    line = orders(size, (None,))
    below, beyond = tuple(range(bits - 1)), tuple(range(2, bits - 1))

    fresh = functools.partial(Stream, size)
    up_width, qkv_width = up_l.shape[1] // 2, 3 * half_g
    square_units = units_g * (size // 8)
    rises, falls = (None, -1, -2), (-1, None, -2)
    order_l = [(bits - 1,) + orders(size, middle)[which] for which, middle in enumerate((falls, rises))]
    order_g = [(bits - 1,) + orders(size, middle)[which] for which, middle in enumerate((rises, falls))]
    gather_g = [(bits - 1,) + order for order in orders(size, rises)]
    table, table_g, places_g = (placement(order, every) for order in (order_l, gather_g, order_g))
    side_l = half_l + half_g
    stream_l = fresh(
        gather_all(
            jnp.concatenate(
                [half_of(out_l, core), half_of(patch_proj, core), gain_block(), own_heads(qkv_l), half_of(up_l, core)],
                axis=1,
            ),
            order_l,
            True,
        )
    )
    stream_down_l = fresh(gather_core(down_l, lows_last, below))
    stream_g = fresh(gather_all(own_heads(qkv_g), gather_g, False))
    stream_out_g = fresh(gather_all(half_of(out_g, core), gather_g, False))
    square = square_columns(half_of(up_g, core))
    one_two = jnp.where(is_first, square[2], square[1])
    two_one = jnp.where(is_first, square[1], square[2])
    blocks = jnp.stack([square[0], one_two, two_one, square[3]]).reshape(2, 2, rows_g, square_units)
    stream_up_g = fresh(gather_square(blocks, plane, every, [(0, rows_g, 0, square_units)]))
    stream_down_g = fresh(
        gather_core(down_g[:, :width_l], line, beyond)
    )

    bias_l = jnp.where(jnp.arange(seq_rows) < lengths[0], 0.0, NEG).astype(F32)[:, None]
    live = (jnp.arange(slot_total)[None, :] < patch_count[0][:, None]).reshape(slots)
    bias_g = jnp.where(live, 0.0, NEG).astype(F32)[:, None]
    positions = patch_index[0].reshape(slots)
    picks = positions[:, None] == jnp.arange(seq_rows)[None, :]
    picks_live = (picks & live[:, None]).astype(BF16)
    picks = picks.astype(BF16)

    advance([stream_l], ())
    seq_inputs = shared(bytes_in[0])
    inputs = seq_inputs.astype(F32)
    scale_l1 = row_scale(inputs)
    seq_grads = shared(out_grad[0])
    grad_top_b = mm(picks_live, seq_grads).astype(BF16)
    scale_l1 = advance([stream_l, stream_up_g, stream_down_l, stream_g], scale_l1)
    stream_top = fresh(gather_in_square(half_of(grad_top_b, core)))
    grad_top_b = advance([stream_l, stream_up_g, stream_down_l, stream_top], grad_top_b)
    advance([stream_l, stream_g, stream_top, stream_up_g], (), [stream_up_g])

    advance([stream_l, stream_g, stream_down_l, stream_up_g, stream_down_g, stream_top, stream_out_g], ())
    parts = stream_l.result()
    front = side_l + TILE
    out_wl, proj_w, gains = assembled_fours(
        parts,
        table,
        [(0, rows_l, 0, half_l), (0, rows_l, half_l, side_l), (0, rows_l, side_l, side_l + LANES)],
        front,
        LONG,
    )
    qkv_wl = Weight(parts, table, front, 3 * half_l)
    up_wl = Weight(parts, table, front + 3 * half_l, up_width)
    gain_one_l, gain_two_l = gains[:, 0].astype(F32), gains[:, 1].astype(F32)
    per = width_g // width_l
    gain_one_g, gain_two_g = (
        gains[:, low : low + per].reshape(width_g).astype(F32) for low in (2, 2 + per)
    )
    normed_l = (inputs * scale_l1 * gain_one_l).astype(BF16)
    projected_l = qkv_wl.product(normed_l)
    own_mixture_l, lse_l = attention_forward(projected_l, bias_l)
    mixture_l = own_mixture_l
    mixture_l, out_wl, proj_w = advance(
        [stream_down_l, stream_up_g, stream_down_g, stream_out_g], (mixture_l, out_wl, proj_w), [stream_up_g]
    )
    mixture_l = advance([stream_g], mixture_l)
    mixture_l, out_wl = shared(mixture_l), shared(out_wl)
    out_own_l = half_of(out_wl, core, 0)
    hidden_l = inputs + mm(mixture_l, out_wl)
    scale_l2 = row_scale(hidden_l)
    normed_l2 = (hidden_l * scale_l2 * gain_two_l).astype(BF16)
    activated_l, slope_l = up_wl.product(normed_l2, gelu=True)
    activated_l, proj_w = advance(
        [stream_down_l, stream_down_g, stream_out_g, stream_up_g], (activated_l, proj_w)
    )
    proj_w = shared(proj_w)
    (down_wl,) = stream_down_l.result()
    partial_l = mm(activated_l, down_wl)
    local_out = half_of(hidden_l, core) + half_of(partial_l, core) + swap(half_of(partial_l, 1 - core))

    boundary = shared(mm(picks, local_out.astype(BF16)).astype(BF16))
    start_rows = mm(boundary, proj_w)
    scale_g1 = row_scale(start_rows)
    square_top = shared(stream_top.result().reshape(4 * slots, half_l))
    scale_g1, square_top = advance([stream_g, stream_out_g, stream_up_g], (scale_g1, square_top))
    qkv_wg = Weight(stream_g.result(), table_g, 0, qkv_width, half_g)
    normed_g = (start_rows * scale_g1 * gain_one_g).astype(BF16)
    projected_g = qkv_wg.product(normed_g)
    own_mixture_g, lse_g = attention_forward(projected_g, bias_g)
    mixture_g = own_mixture_g
    mixture_g = advance([stream_out_g], mixture_g)
    (out_wg,) = assembled_fours(stream_out_g.result(), table_g, [(0, rows_g, 0, half_g)])
    out_theirs_g = swap(out_wg)
    mixture_g = shared(mixture_g)
    hidden_g = start_rows + joined(mm(mixture_g, out_wg), mm(mixture_g, out_theirs_g))
    scale_g2 = row_scale(hidden_g)
    normed_g2 = (hidden_g * scale_g2 * gain_two_g).astype(BF16)
    near = half_of(normed_g2, core)[None]
    near = jnp.concatenate([near, exchange(near, SQUARE[0], size)], axis=0)
    far = exchange(near, SQUARE[1], size)
    mine = jnp.concatenate([near, far], axis=0)
    theirs = jnp.concatenate([swap(near), swap(far)], axis=0)
    mine, theirs = in_square(mine), in_square(theirs, 1)
    square_normed = joined(mine.reshape(4 * slots, half_g), theirs.reshape(4 * slots, half_g))
    (up_wg,) = stream_up_g.result()
    (down_wg,) = stream_down_g.result()
    upward_g = mm(square_normed, up_wg)
    activated_g = jax.nn.gelu(upward_g).astype(BF16)

    grad_down_g = mm_tn(activated_g, square_top).astype(BF16)
    stream_down_g = fresh(scatter_core(grad_down_g, line, beyond, size))
    grad_act_g = mm_nt(square_top, down_wg)
    grad_up_g_rows = jax.vjp(jax.nn.gelu, upward_g)[1](grad_act_g)[0].astype(BF16)
    grad_up_g = mm_tn(square_normed, grad_up_g_rows).astype(BF16)
    stream_up_g = fresh(scatter_square(grad_up_g, plane, every))
    part = mm_nt(grad_up_g_rows, up_wg)
    part = half_of(part, core) + swap(half_of(part, 1 - core).astype(BF16)).astype(F32)
    part = advance([stream_down_g, stream_up_g], part)
    part = shared(fresh(scatter_in_square(part.reshape(4, slots, half_g))).result())
    pulled, grad_gain_g2 = norm_backward(part, hidden_g, scale_g2, gain_two_g)
    grad_hidden_g = jnp.pad(grad_top_b.astype(F32), ((0, 0), (0, width_g - width_l))) + pulled
    grad_hidden_gb = grad_hidden_g.astype(BF16)
    mine_gb, theirs_gb = half_of(grad_hidden_gb, core), half_of(grad_hidden_gb, 1 - core)
    grad_out_g = mm_tn(mixture_g, mine_gb).astype(BF16)
    stream_out_g = fresh(scatter_all(split_stack([grad_out_g], places_g, size), order_g))
    grad_mixture_g = (
        mm_nt(mine_gb, half_of(out_wg, core, 0)) + mm_nt(theirs_gb, half_of(out_theirs_g, core, 0))
    ).astype(BF16)
    partial_g = mm(activated_g, down_wg)
    partial_g = half_of(partial_g, core) + swap(half_of(partial_g, 1 - core).astype(BF16)).astype(F32)
    stream_out = fresh(scatter_in_square(partial_g.reshape(4, slots, half_l)))
    grad_mixture_g = advance([stream_out_g, stream_out], grad_mixture_g)
    grad_projected_g = attention_backward(projected_g, bias_g, lse_g, own_mixture_g, grad_mixture_g)
    part, halves = qkv_wg.pullback(normed_g, grad_projected_g, places_g)
    stream_g = fresh(scatter_all(halves, order_g))
    part = advance([stream_g, stream_out, stream_out_g, stream_down_g], part)
    part = summed_cores(part)
    part = advance([stream_up_g], part)
    pulled, grad_gain_g1 = norm_backward(part, start_rows, scale_g1, gain_one_g)
    grad_start = (grad_hidden_g + pulled).astype(BF16)
    grad_proj = mm_tn(boundary, half_of(grad_start, core)).astype(BF16)

    grad_rows = mm_nt(grad_start, proj_w).astype(BF16)
    grad_local = seq_grads.astype(F32) + mm_tn(picks, grad_rows)
    grad_local_b = grad_local.astype(BF16)
    part, grad_down_l, up_halves = up_wl.feed_forward_pullback(
        normed_l2, grad_local_b, down_wl, slope_l, activated_l, table, side_l
    )
    stream_down_l = fresh(scatter_core(grad_down_l, lows_first, below, size))
    part, up_halves = advance(
        [stream_g, stream_down_g, stream_up_g, stream_out_g], (part, up_halves), [stream_up_g, stream_out_g]
    )
    part = summed_cores(part)
    pulled, grad_gain_l2 = norm_backward(part, hidden_l, scale_l2, gain_two_l)
    grad_hidden_l = grad_local + pulled
    grad_hidden_lb = grad_hidden_l.astype(BF16)
    grad_out_l = mm_tn(mixture_l, half_of(grad_hidden_lb, core)).astype(BF16)
    stream_up_l = fresh(scatter_all(split_stack([grad_out_l, grad_proj], table, size, up_halves), order_l))
    grad_mixture_l = mm_nt(grad_hidden_lb, out_own_l).astype(BF16)
    grad_mixture_l = advance([stream_g, stream_down_l, stream_up_l, stream_up_g, stream_out_g], grad_mixture_l)
    grad_projected_l = attention_backward(projected_l, bias_l, lse_l, own_mixture_l, grad_mixture_l)
    grad_projected_l = advance([stream_out_g, stream_up_g], grad_projected_l)
    stream_qkv_l = fresh(scatter_all(qkv_wl.outer(normed_l, grad_projected_l, table), order_l))
    grad_projected_l = advance([stream_qkv_l], grad_projected_l)
    part = advance([stream_up_l, stream_up_g, stream_g, stream_down_l], qkv_wl.inner(grad_projected_l))
    part = summed_cores(part)
    pulled, grad_gain_l1 = norm_backward(part, inputs, scale_l1, gain_one_l)
    input_grad = half_of(grad_hidden_l + pulled, core).astype(BF16)[None]
    gains = jnp.concatenate(
        [
            grad.reshape(size, 1, grad.shape[0] // size)
            for grad in (grad_gain_l1, grad_gain_l2, grad_gain_g1, grad_gain_g2)
        ],
        axis=2,
    )
    returned = half_of(hidden_g[:, :width_l], core) + stream_out.result()
    hidden_out = (local_out + mm_tn(picks_live, returned.astype(BF16))).astype(BF16)[None]
    stream_gains = fresh(scatter_small(gains, size))
    input_grad = advance([stream_qkv_l, stream_up_l, stream_down_l, stream_gains], input_grad)
    advance([stream_qkv_l, stream_gains, stream_down_l, stream_out_g, stream_g], (), [stream_gains])
    advance([stream_up_l, stream_gains, stream_down_l], ())
    advance([stream_qkv_l, stream_gains], ())
    advance([stream_up_l, stream_qkv_l], ())

    def joined_columns(mine, theirs):
        return joined(mine, theirs).astype(F32)

    def joined_heads(mine, theirs):
        low, high = jnp.where(is_first, mine, theirs), jnp.where(is_first, theirs, mine)
        thirds = [jnp.split(part, 3, axis=1) for part in (low, high)]
        return jnp.concatenate([part for pair in zip(*thirds) for part in pair], axis=1).astype(F32)

    def from_owner(mine, theirs):
        return jnp.where((position >> (bits - 1)) == core, mine, theirs).astype(F32)

    def in_order(blocks):
        low = own_bit((0, 0)), own_bit((1, 1))
        rows, width = blocks.shape[2:]
        placed = []
        for y in range(2):
            for x in range(2):
                dx, dy = x ^ low[0], y ^ low[1]
                index = jnp.where(is_first, 2 * dx + dy, 2 * dy + dx)
                placed.append(lax.dynamic_index_in_dim(blocks.reshape(4, rows, width), index, 0, keepdims=False))
        pieces = [jnp.split(part, size // 8, axis=1) for part in placed]
        return jnp.concatenate([piece for group in zip(*pieces) for piece in group], axis=1)

    down_g_mine = stream_down_g.result()
    total_down_g = from_owner(down_g_mine, swap(down_g_mine))
    total_down_g = jnp.pad(total_down_g, ((0, 0), (0, width_g - width_l)))
    up_g_mine = in_order(stream_up_g.result())
    total_up_g = joined_columns(up_g_mine, swap(up_g_mine))
    g_mine = stream_g.result()
    total_qkv_g = joined_heads(g_mine, swap(g_mine))
    out_g_mine = stream_out_g.result()
    total_out_g = joined_columns(out_g_mine, swap(out_g_mine))
    down_l_mine = stream_down_l.result()
    total_down_l = from_owner(down_l_mine, swap(down_l_mine))
    l_mine = stream_up_l.result()
    l_theirs = swap(l_mine)
    cuts = [0, half_l, side_l, side_l + up_width]
    total_out_l, total_proj, total_up_l = (
        joined_columns(l_mine[:, low:high], l_theirs[:, low:high]) for low, high in zip(cuts, cuts[1:])
    )
    q_mine = stream_qkv_l.result()
    total_qkv_l = joined_heads(q_mine, swap(q_mine))
    gains = stream_gains.result()
    gains = jnp.where(is_first, gains, lax.ppermute(gains, "section", [(0, 1)]))
    total_gain_l1 = gains[:rows_l]
    total_gain_l2 = gains[rows_l : 2 * rows_l]
    total_gain_g1 = gains[2 * rows_l : 2 * rows_l + rows_g]
    total_gain_g2 = gains[2 * rows_l + rows_g :]
    return (
        hidden_out,
        input_grad,
        total_gain_l1,
        total_qkv_l,
        total_out_l,
        total_gain_l2,
        total_up_l,
        total_down_l,
        total_proj,
        total_gain_g1,
        total_qkv_g,
        total_out_g,
        total_gain_g2,
        total_up_g,
        total_down_g,
    )


def solution(mesh):
    rows, vector = P("dp", None), P("dp")
    features = P("dp", None, "section")
    in_specs = (
        features,
        vector,
        P("dp", None, None),
        rows,
        vector,
        rows,
        rows,
        vector,
        rows,
        rows,
        rows,
        vector,
        rows,
        rows,
        vector,
        rows,
        rows,
        features,
    )
    out_specs = (
        features,
        features,
        vector,
        rows,
        rows,
        vector,
        rows,
        rows,
        rows,
        vector,
        rows,
        rows,
        vector,
        rows,
        rows,
    )
    return jax.shard_map(
        functools.partial(local, mesh.shape["dp"]),
        mesh=mesh,
        in_specs=in_specs,
        out_specs=out_specs,
        check_vma=False,
    )
```

```python
import functools

import jax
import jax.numpy as jnp
import numpy as np
from jax import lax
from jax.experimental import pallas as pl
from jax.experimental.pallas import tpu as pltpu
from jax.sharding import PartitionSpec as P

WINDOW = 1536
EPSILON = 1e-06
LANES = 128
GELU_SCALE = (2.0 / np.pi) ** 0.5
GELU_CUBE = 0.044715
NEG = -1e30
VMEM_LIMIT = 48 * 1024 * 1024
FREE = pl.CostEstimate(flops=0, bytes_accessed=0, transcendentals=0)
LONG = pl.CostEstimate(flops=10**11, bytes_accessed=0, transcendentals=0)
F32 = jnp.float32
BF16 = jnp.bfloat16


def mm(left, right):
    return jnp.dot(left, right, preferred_element_type=F32)


def mm_nt(left, right):
    return lax.dot_general(left, right, (((1,), (1,)), ((), ())), preferred_element_type=F32)


def mm_tn(left, right):
    return lax.dot_general(left, right, (((0,), (0,)), ((), ())), preferred_element_type=F32)


def row_scale(values):
    return lax.rsqrt(jnp.mean(values * values, axis=-1, keepdims=True) + EPSILON)


def norm_backward(grad_normed, values, scale, gain):
    grad_gain = jnp.sum(grad_normed * values * scale, axis=0)
    pulled = grad_normed * gain
    inner = jnp.mean(pulled * values, axis=-1, keepdims=True)
    return scale * pulled - values * (scale * scale * scale * inner), grad_gain


def query_block(rows):
    return 256 if rows % 256 == 0 else rows


def head_masks(block):
    lane = lax.broadcasted_iota(jnp.int32, (block, LANES), 1)
    return [lane < LANES // 2, lane >= LANES // 2]


def stacked(values, masks):
    return jnp.concatenate([jnp.where(mask, values, jnp.zeros_like(values)) for mask in masks], axis=0)


def first_lanes(values):
    lane = lax.broadcasted_iota(jnp.int32, (values[0].shape[0], LANES), 1)
    result = jnp.zeros(lane.shape, F32)
    for index, value in enumerate(values):
        result = jnp.where(lane == index, value, result)
    return result.astype(BF16)


def masked_scores(keys, biased, query, extended, bias, start, block, window):
    key_at = lax.broadcasted_iota(jnp.int32, (block, 2 * block), 0)
    query_at = lax.broadcasted_iota(jnp.int32, (block, 2 * block), 1)
    query_at = jnp.where(query_at < block, query_at, query_at - block)
    parts = []
    if start:
        before = mm_nt(biased[:start], extended)
        if window is not None:
            far = lax.broadcasted_iota(jnp.int32, (start, 2 * block), 0)
            own = lax.broadcasted_iota(jnp.int32, (start, 2 * block), 1)
            own = jnp.where(own < block, own, own - block) + start
            before = jnp.where(own - far < window, before, NEG)
        parts.append(before)
    diagonal = mm_nt(keys[start : start + block], query)
    masked = jnp.where(key_at < query_at, diagonal + bias[start : start + block], NEG)
    parts.append(jnp.where(key_at == query_at, diagonal, masked))
    return parts


def ranges(parts):
    low = 0
    for part in parts:
        yield low, low + part.shape[0], part
        low += part.shape[0]


def extend_keys(biased, k_ref, bias_ref):
    biased[:, :LANES] = k_ref[...]
    biased[:, LANES:] = first_lanes([bias_ref[...]])


def attention_forward_kernel(rows, window, q_ref, k_ref, v_ref, bias_ref, o_ref, lse_ref, biased, counted):
    block = query_block(rows)
    masks = head_masks(block)
    score_scale = (LANES // 2) ** (-0.5)
    lane = lax.broadcasted_iota(jnp.int32, (block, LANES), 1)
    extend_keys(biased, k_ref, bias_ref)
    for head, mask in enumerate(head_masks(rows)):
        counted[head] = jnp.where(mask, v_ref[...], jnp.ones_like(v_ref))
    one = first_lanes([jnp.ones((2 * block, 1), F32)])
    query_at = lax.broadcasted_iota(jnp.int32, (2 * block, block), 0)
    query_at = jnp.where(query_at < block, query_at, query_at - block)
    key_at = lax.broadcasted_iota(jnp.int32, (2 * block, block), 1)
    for index in range(rows // block):
        start = index * block
        query = stacked((q_ref[start : start + block, :] * score_scale).astype(BF16), masks)
        extended = jnp.concatenate([query, one], axis=1)
        parts = []
        if start:
            before = mm_nt(extended, biased[:start, :])
            if window is not None:
                far = lax.broadcasted_iota(jnp.int32, (2 * block, start), 1)
                own = lax.broadcasted_iota(jnp.int32, (2 * block, start), 0)
                own = jnp.where(own < block, own, own - block) + start
                before = jnp.where(own - far < window, before, NEG)
            parts.append(before)
        masked = jnp.where(key_at < query_at, mm_nt(extended, biased[start : start + block, :]), NEG)
        parts.append(jnp.where(key_at == query_at, mm_nt(query, k_ref[start : start + block, :]), masked))
        top = functools.reduce(jnp.maximum, [jnp.max(p, axis=1, keepdims=True) for p in parts])
        parts = [jnp.exp(p - top).astype(BF16) for p in parts]
        out, logs = jnp.zeros((block, LANES), F32), jnp.zeros((block, LANES), F32)
        for head, mask in enumerate(masks):
            span = slice(head * block, (head + 1) * block)
            mixed, low = jnp.zeros((block, LANES), F32), 0
            for part in parts:
                high = low + part.shape[1]
                mixed += mm(part[span], counted[head, low:high, :])
                low = high
            other = LANES // 2 if head == 0 else 0
            total = mixed[:, other : other + 1]
            out = jnp.where(mask, mixed * (1.0 / total), out)
            logs = jnp.where(lane == head, top[span] + jnp.log(total), logs)
        o_ref[start : start + block, :] = out.astype(BF16)
        lse_ref[0, :, start : start + block] = logs.T[:2]


def attention_backward_kernel(
    rows,
    window,
    q_ref,
    k_ref,
    v_ref,
    bias_ref,
    lse_ref,
    o_ref,
    do_ref,
    dq_ref,
    dk_ref,
    dv_ref,
    dk_acc,
    dv_acc,
    biased,
    reduced,
):
    block = query_block(rows)
    masks = head_masks(block)
    score_scale = (LANES // 2) ** (-0.5)
    extend_keys(biased, k_ref, bias_ref)
    reduced[:, :LANES] = v_ref[...]
    reduced[:, LANES:] = first_lanes([jnp.full((rows, 1), -1.0, F32)] * 2)
    one = first_lanes([jnp.ones((2 * block, 1), F32)])
    for index in reversed(range(rows // block)):
        start = index * block
        query = stacked((q_ref[start : start + block, :] * score_scale).astype(BF16), masks)
        extended = jnp.concatenate([query, one], axis=1)
        grad = stacked(do_ref[start : start + block, :], masks)
        mixed = o_ref[start : start + block, :].astype(F32)
        delta = jnp.sum(grad.astype(F32) * jnp.concatenate([mixed, mixed], axis=0), axis=1, keepdims=True)
        near = delta.astype(BF16).astype(F32)
        grad_extended = jnp.concatenate([grad, first_lanes([near, delta - near])], axis=1)
        lse = jnp.concatenate([lse_ref[0, head : head + 1, start : start + block] for head in range(2)], axis=1)
        parts = masked_scores(k_ref, biased, query, extended, bias_ref, start, block, window)
        turned = jnp.zeros((2 * block, LANES), F32)
        for low, high, part in ranges(parts):
            weights = jnp.exp(part - lse)
            change = (weights * mm_nt(reduced[low:high, :], grad_extended)).astype(BF16)
            dv = mm(weights.astype(BF16), grad)
            dk = mm(change, query)
            if index == rows // block - 1:
                dv_acc[low:high, :] = dv
                dk_acc[low:high, :] = dk
            else:
                dv_acc[low:high, :] += dv
                dk_acc[low:high, :] += dk
            turned += mm_tn(change, k_ref[low:high, :])
        dq = jnp.where(masks[0], turned[:block], turned[block:]) * score_scale
        dq_ref[start : start + block, :] = dq.astype(BF16)
    dk_ref[...] = dk_acc[...].astype(BF16)
    dv_ref[...] = dv_acc[...].astype(BF16)


def attention_specs(rows, width):
    pairs = width // LANES
    wide = lambda part: pl.BlockSpec((rows, LANES), lambda i, part=part: (0, part * pairs + i))
    bias = pl.BlockSpec((rows, 1), lambda i: (0, 0))
    return pairs, wide, bias


def attention_forward(projected, bias):
    rows, width = projected.shape[0], projected.shape[1] // 3
    pairs, wide, bias_spec = attention_specs(rows, width)
    window = WINDOW if rows > WINDOW else None
    return pl.pallas_call(
        functools.partial(attention_forward_kernel, rows, window),
        grid=(pairs,),
        in_specs=[wide(0), wide(1), wide(2), bias_spec],
        out_specs=[wide(0), pl.BlockSpec((1, 2, rows), lambda i: (i, 0, 0))],
        out_shape=[
            jax.ShapeDtypeStruct((rows, width), BF16),
            jax.ShapeDtypeStruct((pairs, 2, rows), F32),
        ],
        scratch_shapes=[pltpu.VMEM((rows, 2 * LANES), BF16), pltpu.VMEM((2, rows, LANES), BF16)],
        compiler_params=pltpu.CompilerParams(vmem_limit_bytes=VMEM_LIMIT),
        cost_estimate=FREE,
    )(projected, projected, projected, bias)


def attention_backward(projected, bias, lse, mixture, grad_mixture):
    rows, width = grad_mixture.shape
    pairs, wide, bias_spec = attention_specs(rows, width)
    window = WINDOW if rows > WINDOW else None
    shape = jax.ShapeDtypeStruct((rows, width), BF16)
    return pl.pallas_call(
        functools.partial(attention_backward_kernel, rows, window),
        grid=(pairs,),
        in_specs=[
            wide(0),
            wide(1),
            wide(2),
            bias_spec,
            pl.BlockSpec((1, 2, rows), lambda i: (i, 0, 0)),
            wide(0),
            wide(0),
        ],
        out_specs=[wide(0), wide(0), wide(0)],
        out_shape=[shape, shape, shape],
        scratch_shapes=[
            pltpu.VMEM((rows, LANES), F32),
            pltpu.VMEM((rows, LANES), F32),
            pltpu.VMEM((rows, 2 * LANES), BF16),
            pltpu.VMEM((rows, 2 * LANES), BF16),
        ],
        compiler_params=pltpu.CompilerParams(vmem_limit_bytes=VMEM_LIMIT),
        cost_estimate=LONG,
    )(projected, projected, projected, bias, lse, mixture, grad_mixture)


def swap(array):
    return lax.ppermute(array, "section", [(0, 1), (1, 0)])


def exchange(array, bits, size, sends=None):
    if sends == "flips":
        return tuple(
            lax.ppermute(part, "dp", [(i, i ^ flip) for i in range(size)]) for part, flip in zip(array, bits)
        )
    pairs = [
        (core * size + i, core * size + (i ^ (1 << bit)))
        for core, bit in enumerate(bits)
        for i in range(size)
        if sends is None or sends(core, i)
    ]
    return jax.tree.map(lambda part: lax.ppermute(part, ("section", "dp"), pairs), array)


def bit_count(size):
    return size.bit_length() - 1


def orders(size, middle):
    bits = bit_count(size)
    others = tuple(reversed(range(2, bits - 1)))
    result = []
    for core in range(2):
        lowest = (0, 1) if core == 0 else (1, 0)
        order = ()
        for entry in middle:
            order += others if entry is None else (lowest[0] if entry == -1 else lowest[1],)
        result.append(order)
    return result


def mask_of(index, order, places):
    return sum(((index >> t) & 1) << places.index(bit) for t, bit in enumerate(order))


def placement(order_pair, places):
    position = lax.axis_index("dp")
    own = sum(((position >> bit) & 1) << p for p, bit in enumerate(places))
    count = 1 << len(places)
    masks = [jnp.asarray([mask_of(j, order, places) for j in range(count)], jnp.int32) for order in order_pair]
    return (own ^ jnp.where(lax.axis_index("section") == 0, masks[0], masks[1])).astype(jnp.int32)


def aligned(rows, cuts=()):
    return rows % 16 == 0 and all(c % LANES == 0 and r % 16 == 0 for r0, r1, c0, c1 in cuts for r, c in ((r0, c0), (r1, c1)))


def assembly_kernel(bounds, cuts, table, *refs):
    step = pl.program_id(0)
    parts, outs = refs[: len(bounds)], refs[len(bounds) :]

    def store(ref):
        for (r0, r1, c0, c1), out in zip(cuts, outs):
            out[...] = ref[0, r0:r1, c0:c1]

    for (low, high), ref in zip(bounds, parts):
        pl.when((step >= low) & (step < high))(functools.partial(store, ref))


def assembled(parts, table, cuts, offset=0, width=None):
    rows = parts[0].shape[1]
    width = width or parts[0].shape[2]
    ends = np.cumsum([part.shape[0] for part in parts])
    count = int(ends[-1])
    bounds = [(int(end) - part.shape[0], int(end)) for end, part in zip(ends, parts)]
    shapes = [(count * (r1 - r0), c1 - c0) for r0, r1, c0, c1 in cuts]
    if not aligned(rows, cuts):
        stack = jnp.concatenate(parts, axis=0)[jnp.argsort(table)][..., offset : offset + width]
        return [stack[:, r0:r1, c0:c1].reshape(s) for (r0, r1, c0, c1), s in zip(cuts, shapes)]
    return pl.pallas_call(
        functools.partial(assembly_kernel, bounds, cuts),
        grid_spec=pltpu.PrefetchScalarGridSpec(
            num_scalar_prefetch=1,
            grid=(count,),
            in_specs=[
                pl.BlockSpec(
                    (1, rows, width),
                    lambda j, t, low=low, high=high: (jnp.clip(j, low, high - 1) - low, 0, offset // width),
                )
                for low, high in bounds
            ],
            out_specs=[pl.BlockSpec((r1 - r0, c1 - c0), lambda j, t: (t[j], 0)) for r0, r1, c0, c1 in cuts],
        ),
        out_shape=[jax.ShapeDtypeStruct(s, parts[0].dtype) for s in shapes],
        compiler_params=pltpu.CompilerParams(vmem_limit_bytes=VMEM_LIMIT),
        cost_estimate=FREE,
    )(table, *parts)


def quarters(parts):
    if len(parts) == 4:
        return [(part, 0) for part in parts]
    return [(part, k) for part in parts for k in range(2)]


def whole_kernel(cuts, table, *refs):
    quarter = refs[0].shape[0]
    for index in range(4 * quarter):
        part, place = refs[index // quarter], table[index]
        for (r0, r1, c0, c1), out in zip(cuts, refs[4:]):
            rows = r1 - r0
            out[pl.ds(pl.multiple_of(place * rows, 16), rows), :] = part[index % quarter, r0:r1, c0:c1]


def assembled_fours(parts, table, cuts, width=None, cost=FREE):
    rows = parts[0].shape[1]
    width = width or parts[0].shape[2]
    count = sum(part.shape[0] for part in parts)
    shapes = [(count * (r1 - r0), c1 - c0) for r0, r1, c0, c1 in cuts]
    if not aligned(rows, cuts):
        stack = jnp.concatenate(parts, axis=0)[jnp.argsort(table)]
        return [stack[:, r0:r1, c0:c1].reshape(s) for (r0, r1, c0, c1), s in zip(cuts, shapes)]
    return pl.pallas_call(
        functools.partial(whole_kernel, cuts),
        grid_spec=pltpu.PrefetchScalarGridSpec(
            num_scalar_prefetch=1,
            grid=(1,),
            in_specs=[pl.BlockSpec((count // 4, rows, width), lambda j, t, k=k: (k, 0, 0)) for _, k in quarters(parts)],
            out_specs=[pl.BlockSpec(shape, lambda j, t: (0, 0)) for shape in shapes],
        ),
        out_shape=[jax.ShapeDtypeStruct(s, parts[0].dtype) for s in shapes],
        compiler_params=pltpu.CompilerParams(vmem_limit_bytes=VMEM_LIMIT),
        cost_estimate=cost,
    )(table, *[part for part, _ in quarters(parts)])


def split_kernel(half, count, table, *refs):
    send, keep = refs[-2:]
    rows = refs[0].shape[0] // (2 * half)
    for index in range(2 * half):
        place, base = table[index], 0
        for ref in refs[:count]:
            block = ref[pl.ds(pl.multiple_of(place * rows, 16), rows), :]
            (keep if index < half else send)[index % half, :, base : base + ref.shape[1]] = block
            base += ref.shape[1]


def split_stack(grads, table, count, into=None):
    half, rows = count // 2, grads[0].shape[0] // count
    width = sum(grad.shape[1] for grad in grads)
    if not (aligned(rows) and all(grad.shape[1] % LANES == 0 for grad in grads)):
        stack = jnp.concatenate([grad.reshape(count, rows, grad.shape[1]) for grad in grads], axis=2)[table]
        halves = [stack[half:], stack[:half]]
        if into is not None:
            halves = [jnp.concatenate([part, old[..., width:]], axis=2) for part, old in zip(halves, into)]
        return halves
    full = width if into is None else into[0].shape[2]
    shape = jax.ShapeDtypeStruct((half, rows, full), BF16)
    into = [] if into is None else list(into)
    half_spec = pl.BlockSpec((half, rows, width), lambda j, t: (0, 0, 0))
    return pl.pallas_call(
        functools.partial(split_kernel, half, len(grads)),
        grid_spec=pltpu.PrefetchScalarGridSpec(
            num_scalar_prefetch=1,
            grid=(1,),
            in_specs=[pl.BlockSpec(grad.shape, lambda j, t: (0, 0)) for grad in grads]
            + [pl.BlockSpec(memory_space=pl.ANY) for _ in into],
            out_specs=[half_spec, half_spec],
        ),
        out_shape=[shape, shape],
        input_output_aliases={1 + len(grads) + k: k for k in range(len(into))},
        compiler_params=pltpu.CompilerParams(vmem_limit_bytes=VMEM_LIMIT),
        cost_estimate=FREE,
    )(table, *grads, *into)


def write_rows(target, parts, table, rows):
    index = 0
    for part in parts:
        for k in range(part.shape[0]):
            target[pl.ds(pl.multiple_of(table[index] * rows, 16), rows), :] = part[k]
            index += 1


def product_kernel(rows, count, gelu, table, x_ref, *refs):
    parts, outs, weight = refs[:count], refs[count:-1], refs[-1]
    write_rows(weight, parts, table, rows)
    result = jnp.dot(x_ref[...], weight[...], preferred_element_type=F32)
    if not gelu:
        outs[0][...] = result.astype(outs[0].dtype)
        return
    square = result * result
    bend = jnp.tanh(GELU_SCALE * (result + GELU_CUBE * (result * square)))
    outs[0][...] = (0.5 * result * (1.0 + bend)).astype(outs[0].dtype)
    slope = 0.5 * (1.0 + bend)
    slope += (0.5 * GELU_SCALE) * result * (1.0 - bend * bend) * (1.0 + (3.0 * GELU_CUBE) * square)
    outs[1][...] = slope.astype(outs[1].dtype)


def outer_kernel(rows, bounds, places, x_ref, *refs):
    grads, (send, keep, weight, turned) = refs[: len(bounds)], refs[len(bounds) :]
    step = pl.program_id(0)

    @pl.when(step == 0)
    def _():
        turned[...] = x_ref[...].T

    grad = grads[-1][...]
    for (low, high), ref in list(zip(bounds, grads))[:-1]:
        grad = jnp.where((step >= low) & (step < high), ref[...], grad)
    weight[...] = mm(turned[...], grad).astype(BF16)
    half = keep.shape[0]
    for index in range(2 * half):
        block = weight[pl.ds(pl.multiple_of(places[index] * rows, 16), rows), :]
        (keep if index < half else send)[index % half] = block


def inner_kernel(rows, bounds, table, *refs):
    parts, grads, (dx_ref, weight, total) = refs[:4], refs[4 : 4 + len(bounds)], refs[4 + len(bounds) :]
    step = pl.program_id(0)

    @pl.when(step == 0)
    def _():
        total[...] = jnp.zeros_like(total)

    write_rows(weight, parts, table, rows)
    grad = grads[-1][...]
    for (low, high), ref in list(zip(bounds, grads))[:-1]:
        grad = jnp.where((step >= low) & (step < high), ref[...], grad)
    total[...] += mm_nt(grad, weight[...])

    @pl.when(step == pl.num_programs(0) - 1)
    def _():
        dx_ref[...] = total[...].astype(BF16)


def pullback_kernel(rows, count, bounds, table, places, x_ref, *refs):
    parts, grads = refs[:count], refs[count : count + len(bounds)]
    dx_ref, send, keep, weight, turned, total = refs[count + len(bounds) :]
    step = pl.program_id(0)

    @pl.when(step == 0)
    def _():
        turned[...] = x_ref[...].T
        total[...] = jnp.zeros_like(total)

    write_rows(weight, parts, table, rows)
    grad = grads[-1][...]
    for (low, high), ref in list(zip(bounds, grads))[:-1]:
        grad = jnp.where((step >= low) & (step < high), ref[...], grad)
    total[...] += lax.dot_general(grad, weight[...], (((1,), (1,)), ((), ())), preferred_element_type=F32)
    weight[...] = jnp.dot(turned[...], grad, preferred_element_type=F32).astype(BF16)
    half = keep.shape[0]
    for index in range(2 * half):
        block = weight[pl.ds(pl.multiple_of(places[index] * rows, 16), rows), :]
        (keep if index < half else send)[index % half] = block

    @pl.when(step == pl.num_programs(0) - 1)
    def _():
        dx_ref[...] = total[...].astype(BF16)


def feed_forward_kernel(rows, table, places, x_ref, grad_ref, down_ref, slope_ref, act_ref, *refs):
    parts, (dx_ref, down_out, send, keep, weight, turned, total) = refs[:4], refs[4:]
    step = pl.program_id(0)

    @pl.when(step == 0)
    def _():
        turned[...] = x_ref[...].T
        total[...] = jnp.zeros_like(total)

    grad = grad_ref[...]
    change = (mm_nt(grad, down_ref[...]) * slope_ref[...].astype(F32)).astype(BF16)
    down_out[...] = mm_tn(act_ref[...], grad).astype(BF16)
    write_rows(weight, parts, table, rows)
    total[...] += mm_nt(change, weight[...])
    weight[...] = mm(turned[...], change).astype(BF16)
    half = keep.shape[0]
    for index in range(2 * half):
        block = weight[pl.ds(pl.multiple_of(places[index] * rows, 16), rows), :]
        (keep if index < half else send)[index % half] = block

    @pl.when(step == pl.num_programs(0) - 1)
    def _():
        dx_ref[...] = total[...].astype(BF16)


TILE = 384


class Weight:
    def __init__(self, parts, table, offset, width, tile=TILE):
        self.parts, self.table, self.offset, self.width, self.tile = parts, table, offset, width, tile
        self.rows = parts[0].shape[1]
        self.count = sum(part.shape[0] for part in parts)
        self.aligned = aligned(self.rows) and offset % tile == 0 and width % tile == 0

    def whole(self):
        cut = (0, self.rows, 0, self.width)
        stack = jnp.concatenate(self.parts, axis=0)[jnp.argsort(self.table)]
        return stack[..., self.offset : self.offset + self.width].reshape(-1, self.width)

    def part_specs(self):
        first = self.offset // self.tile
        return [
            pl.BlockSpec((self.count // 4, self.rows, self.tile), lambda i, *tables, k=k: (k, 0, first + i))
            for _, k in quarters(self.parts)
        ]

    def product(self, x, gelu=False):
        if not self.aligned:
            result = mm(x, self.whole())
            if not gelu:
                return result.astype(BF16)
            slope = jax.vjp(jax.nn.gelu, result)[1](jnp.ones_like(result))[0]
            return jax.nn.gelu(result).astype(BF16), slope.astype(BF16)
        tokens, depth = x.shape
        outs = 2 if gelu else 1
        shape = jax.ShapeDtypeStruct((tokens, self.width), BF16)
        results = pl.pallas_call(
            functools.partial(product_kernel, self.rows, 4, gelu),
            grid_spec=pltpu.PrefetchScalarGridSpec(
                num_scalar_prefetch=1,
                grid=(self.width // self.tile,),
                in_specs=[pl.BlockSpec((tokens, depth), lambda i, t: (0, 0))] + self.part_specs(),
                out_specs=[pl.BlockSpec((tokens, self.tile), lambda i, t: (0, i))] * outs,
                scratch_shapes=[pltpu.VMEM((depth, self.tile), BF16)],
            ),
            out_shape=[shape] * outs,
            compiler_params=pltpu.CompilerParams(vmem_limit_bytes=VMEM_LIMIT),
            cost_estimate=LONG if gelu else FREE,
        )(self.table, x, *[part for part, _ in quarters(self.parts)])
        return results if gelu else results[0]

    def feed_forward_pullback(self, x, grad, down, slope, activated, places, lead):
        if not self.aligned or down.shape[0] != self.width:
            change = (slope.astype(F32) * mm_nt(grad, down)).astype(BF16)
            dx, halves = self.pullback(x, [change], places, lead)
            return dx, mm_tn(activated, grad).astype(BF16), halves
        tokens, depth = x.shape
        half = jax.ShapeDtypeStruct((self.count // 2, self.rows, lead + self.width), BF16)
        half_spec = pl.BlockSpec((self.count // 2, self.rows, self.tile), lambda i, t, p: (0, 0, lead // self.tile + i))
        full = pl.BlockSpec((tokens, depth), lambda i, t, p: (0, 0))
        units = pl.BlockSpec((tokens, self.tile), lambda i, t, p: (0, i))
        unit_rows = pl.BlockSpec((self.tile, depth), lambda i, t, p: (i, 0))
        result = pl.pallas_call(
            functools.partial(feed_forward_kernel, self.rows),
            grid_spec=pltpu.PrefetchScalarGridSpec(
                num_scalar_prefetch=2,
                grid=(self.width // self.tile,),
                in_specs=[full, full, unit_rows, units, units] + self.part_specs(),
                out_specs=[full, unit_rows, half_spec, half_spec],
                scratch_shapes=[
                    pltpu.VMEM((depth, self.tile), BF16),
                    pltpu.VMEM((depth, tokens), BF16),
                    pltpu.VMEM((tokens, depth), F32),
                ],
            ),
            out_shape=[jax.ShapeDtypeStruct((tokens, depth), BF16), jax.ShapeDtypeStruct(down.shape, BF16), half, half],
            compiler_params=pltpu.CompilerParams(vmem_limit_bytes=VMEM_LIMIT),
            cost_estimate=FREE,
        )(self.table, places, x, grad, down, slope, activated, *[part for part, _ in quarters(self.parts)])
        return result[0], result[1], result[2:]

    def grad_specs(self, tokens, grads):
        ends = np.cumsum([grad.shape[1] // self.tile for grad in grads])
        bounds = [(int(end) - grad.shape[1] // self.tile, int(end)) for end, grad in zip(ends, grads)]
        specs = [
            pl.BlockSpec((tokens, self.tile), lambda i, t, low=low, high=high: (0, jnp.clip(i, low, high - 1) - low))
            for low, high in bounds
        ]
        return bounds, specs

    def outer(self, x, grads, places):
        if not self.aligned:
            return split_stack([mm_tn(x, jnp.concatenate(grads, axis=1)).astype(BF16)], places, self.count)
        tokens, depth = x.shape
        bounds, specs = self.grad_specs(tokens, grads)
        half = jax.ShapeDtypeStruct((self.count // 2, self.rows, self.width), BF16)
        half_spec = pl.BlockSpec((self.count // 2, self.rows, self.tile), lambda i, t: (0, 0, i))
        return pl.pallas_call(
            functools.partial(outer_kernel, self.rows, bounds),
            grid_spec=pltpu.PrefetchScalarGridSpec(
                num_scalar_prefetch=1,
                grid=(self.width // self.tile,),
                in_specs=[pl.BlockSpec((tokens, depth), lambda i, t: (0, 0))] + specs,
                out_specs=[half_spec, half_spec],
                scratch_shapes=[pltpu.VMEM((depth, self.tile), BF16), pltpu.VMEM((depth, tokens), BF16)],
            ),
            out_shape=[half, half],
            compiler_params=pltpu.CompilerParams(vmem_limit_bytes=VMEM_LIMIT),
            cost_estimate=FREE,
        )(places, x, *grads)

    def inner(self, grads):
        if not self.aligned:
            return mm_nt(jnp.concatenate(grads, axis=1), self.whole()).astype(BF16)
        tokens, depth = grads[0].shape[0], self.rows * self.count
        bounds, specs = self.grad_specs(tokens, grads)
        return pl.pallas_call(
            functools.partial(inner_kernel, self.rows, bounds),
            grid_spec=pltpu.PrefetchScalarGridSpec(
                num_scalar_prefetch=1,
                grid=(self.width // self.tile,),
                in_specs=self.part_specs() + specs,
                out_specs=pl.BlockSpec((tokens, depth), lambda i, t: (0, 0)),
                scratch_shapes=[pltpu.VMEM((depth, self.tile), BF16), pltpu.VMEM((tokens, depth), F32)],
            ),
            out_shape=jax.ShapeDtypeStruct((tokens, depth), BF16),
            compiler_params=pltpu.CompilerParams(vmem_limit_bytes=VMEM_LIMIT),
            cost_estimate=FREE,
        )(self.table, *[part for part, _ in quarters(self.parts)], *grads)

    def pullback(self, x, grads, places, lead=0):
        if not self.aligned:
            grad = jnp.concatenate(grads, axis=1)
            halves = split_stack([mm_tn(x, grad).astype(BF16)], places, self.count)
            return mm_nt(grad, self.whole()).astype(BF16), [jnp.pad(h, ((0, 0), (0, 0), (lead, 0))) for h in halves]
        tokens, depth = x.shape
        ends = np.cumsum([grad.shape[1] // self.tile for grad in grads])
        bounds = [(int(end) - grad.shape[1] // self.tile, int(end)) for end, grad in zip(ends, grads)]
        half = jax.ShapeDtypeStruct((self.count // 2, self.rows, lead + self.width), BF16)
        half_spec = pl.BlockSpec((self.count // 2, self.rows, self.tile), lambda i, t, p: (0, 0, lead // self.tile + i))
        result = pl.pallas_call(
            functools.partial(pullback_kernel, self.rows, 4, bounds),
            grid_spec=pltpu.PrefetchScalarGridSpec(
                num_scalar_prefetch=2,
                grid=(self.width // self.tile,),
                in_specs=[pl.BlockSpec((tokens, depth), lambda i, t, p: (0, 0))]
                + self.part_specs()
                + [
                    pl.BlockSpec((tokens, self.tile), lambda i, t, p, low=low, high=high: (0, jnp.clip(i, low, high - 1) - low))
                    for low, high in bounds
                ],
                out_specs=[pl.BlockSpec((tokens, depth), lambda i, t, p: (0, 0)), half_spec, half_spec],
                scratch_shapes=[
                    pltpu.VMEM((depth, self.tile), BF16),
                    pltpu.VMEM((depth, tokens), BF16),
                    pltpu.VMEM((tokens, depth), F32),
                ],
            ),
            out_shape=[jax.ShapeDtypeStruct((tokens, depth), BF16), half, half],
            compiler_params=pltpu.CompilerParams(vmem_limit_bytes=VMEM_LIMIT),
            cost_estimate=FREE,
        )(self.table, places, x, *[part for part, _ in quarters(self.parts)], *grads)
        return result[0], result[1:]


class Stream:
    def __init__(self, size, steps):
        self.size, self.steps = size, steps
        self.arriving = None
        self.value = None
        self.done = False
        self.pending = None

    def begin(self, arrived=None):
        try:
            self.pending = self.steps.send(arrived)
        except StopIteration as stop:
            self.pending, self.value, self.done = None, stop.value, True

    def launch(self):
        outgoing, bits, sends = self.pending
        self.arriving, self.pending = exchange(outgoing, bits, self.size, sends), None

    def result(self):
        if self.arriving is None and self.pending is None and not self.done:
            self.begin()
        while not self.done:
            if self.arriving is None:
                self.launch()
            arrived, self.arriving = self.arriving, None
            self.begin(arrived)
        return self.value


def advance(streams, tied, hold=()):
    for stream in streams:
        if stream.arriving is None and stream.pending is None and not stream.done:
            stream.begin()
    moving = [stream for stream in streams if not stream.done]
    ending = [stream for stream in moving if stream.arriving is not None]
    fresh = [stream for stream in moving if stream.arriving is None]
    arrived, outgoing, tied = lax.optimization_barrier(
        ([s.arriving for s in ending], [s.pending[0] for s in fresh], tied)
    )
    for stream, array in zip(fresh, outgoing):
        stream.pending = (array,) + stream.pending[1:]
    for stream, array in zip(ending, arrived):
        stream.arriving = None
        stream.begin(array)
    for stream in moving:
        if not stream.done and stream not in hold:
            stream.launch()
    return tied


def top_sends(size):
    top = bit_count(size) - 1
    return lambda core, i: (i >> top) == core


def doubling(held, order_pair, first=0, twice=False):
    parts = (held,)
    steps = list(zip(*order_pair))[first:]
    for index, bits in enumerate(steps):
        if len(parts) > 1 and not (twice and index == len(steps) - 1):
            parts = (jnp.concatenate(parts, axis=0),)
        arrived = yield lax.optimization_barrier(parts), bits, None
        parts = parts + arrived
    return parts


def gather_all(packed, order_pair, twice):
    return (yield from doubling(packed[None], order_pair, 0, twice))


def gather_core(piece, order_pair, places):
    size = lax.axis_size("dp")
    top = bit_count(size) - 1
    arrived = yield piece, (top, top), top_sends(size)
    mine = (lax.axis_index("dp") >> top) == lax.axis_index("section")
    parts = yield from doubling(jnp.where(mine, piece, arrived)[None], order_pair)
    table, cuts = placement(order_pair, places), [(0, piece.shape[0], 0, piece.shape[1])]
    return assembled_fours(parts, table, cuts) if len(places) > 1 else assembled(parts, table, cuts)


def own_bit(pair):
    position = lax.axis_index("dp")
    return (position >> jnp.where(lax.axis_index("section") == 0, pair[0], pair[1])) & 1


def gather_square(blocks, order_pair, places, cuts):
    first, second = list(zip(*order_pair))[:2]
    a, b = own_bit(first), own_bit(second)
    kept = lax.dynamic_index_in_dim(blocks, a, 0, keepdims=False)
    arrived = yield lax.dynamic_index_in_dim(blocks, 1 - a, 0, keepdims=False), first, None
    held = jnp.stack([kept, arrived])
    kept = lax.dynamic_index_in_dim(held, b, 1, keepdims=False)
    arrived = yield lax.dynamic_index_in_dim(held, 1 - b, 1, keepdims=False), second, None
    parts = yield from doubling(jnp.concatenate([kept, arrived], axis=0), order_pair, 2)
    return assembled(parts, placement(order_pair, places), cuts)


def total_of(terms):
    return sum(term.astype(F32) for term in terms)


def halving(send, kept, order_pair, last=0):
    terms, outgoing = [kept], send
    for bits in reversed(list(zip(*order_pair))[last:]):
        if outgoing is None:
            half = terms[0].shape[0] // 2
            outgoing = total_of([term[half:] for term in terms]).astype(BF16)
            terms = [term[:half] for term in terms]
        arrived = yield outgoing, bits, None
        terms, outgoing = terms + [arrived], None
    return terms


def scatter_all(halves, order_pair):
    terms = yield from halving(*halves, order_pair)
    return total_of(terms)[0].astype(BF16)


def scatter_core(grad, order_pair, places, size):
    halves = split_stack([grad], placement(order_pair, places), 1 << len(places))
    terms = yield from halving(*halves, order_pair)
    top = bit_count(size) - 1
    sends = top_sends(size)
    arrived = yield total_of(terms)[0].astype(BF16), (top, top), lambda core, i: not sends(core, i)
    return (total_of(terms)[0] + arrived.astype(F32)).astype(BF16)


def scatter_square(grad, order_pair, places):
    halves = split_stack([grad], placement(order_pair, places), 1 << len(places))
    terms = yield from halving(*halves, order_pair, 2)
    held = total_of(terms).astype(BF16)
    first, second = list(zip(*order_pair))[:2]
    arrived = yield held[2:], second, None
    held = jnp.stack([held[:2], arrived])
    arrived = yield held[:, 1], first, None
    return jnp.stack([held[:, 0], arrived])


def scatter_small(vector, size):
    position = lax.axis_index("dp")
    held = vector.reshape(size // 4, 4, vector.shape[2])
    for count, low in ((4, 0), (size // 4, 2)):
        own = (position >> low) & (count - 1)

        def part(index):
            return lax.dynamic_index_in_dim(held, index, 1 if low == 0 else 0, keepdims=False)

        outgoing = tuple(part(own ^ other) for other in range(1, count))
        arrived = yield outgoing, tuple(other << low for other in range(1, count)), "flips"
        held = part(own) + sum(arrived)
    return held


def in_square(blocks, whose=0):
    is_first = lax.axis_index("section") == whose
    middle = jnp.where(is_first, blocks[1:3], jnp.stack([blocks[2], blocks[1]]))
    return jnp.concatenate([blocks[:1], middle, blocks[3:]], axis=0)


SQUARE = ((0, 1), (1, 0))


def gather_in_square(rows):
    held = rows[None]
    for bits in SQUARE:
        arrived = yield held, bits, None
        held = jnp.concatenate([held, arrived], axis=0)
    return in_square(held)


def scatter_in_square(blocks):
    held = in_square(blocks)
    for bits in reversed(SQUARE):
        half = held.shape[0] // 2
        arrived = yield held[half:].astype(BF16), bits, None
        held = held[:half] + arrived.astype(F32)
    return held[0]


def local(
    size,
    bytes_in,
    lengths,
    patch_index,
    patch_count,
    gain_l1,
    qkv_l,
    out_l,
    gain_l2,
    up_l,
    down_l,
    patch_proj,
    gain_g1,
    qkv_g,
    out_g,
    gain_g2,
    up_g,
    down_g,
    out_grad,
):
    core = lax.axis_index("section")
    position = lax.axis_index("dp")
    is_first = core == 0
    seq_rows, half_l = bytes_in.shape[1:]
    width_l, width_g = 2 * half_l, out_g.shape[1]
    half_g = width_g // 2
    rows_l, rows_g = out_l.shape[0], out_g.shape[0]
    units_l, units_g = down_l.shape[0], down_g.shape[0]
    micro_total, slot_total = patch_index.shape[1:]
    slots = micro_total * slot_total
    bits = bit_count(size)
    every = tuple(range(bits))

    def joined(mine, theirs, axis=1):
        low = jnp.where(is_first, mine, theirs)
        high = jnp.where(is_first, theirs, mine)
        return jnp.concatenate([low, high], axis=axis)

    def shared(mine, axis=1):
        return joined(mine, swap(mine), axis)

    def half_of(array, which, axis=1):
        length = array.shape[axis] // 2
        return lax.dynamic_slice_in_dim(array, which * length, length, axis)

    def slope_of(upward):
        return jax.vjp(jax.nn.gelu, upward)[1](jnp.ones_like(upward))[0]

    def summed_cores(part):
        part = part.astype(BF16)
        return part.astype(F32) + swap(part).astype(F32)

    def own_heads(weight):
        return jnp.concatenate([half_of(third, core) for third in jnp.split(weight, 3, axis=1)], axis=1)

    def square_columns(weight):
        pieces = jnp.split(weight, size // 2, axis=1)
        return [jnp.concatenate(pieces[k::4], axis=1) for k in range(4)]

    def gain_block():
        columns = [gain.reshape(rows_l, -1) for gain in (gain_l1, gain_l2, gain_g1, gain_g2)]
        block = jnp.concatenate(columns, axis=1)
        return jnp.pad(block, ((0, 0), (0, TILE - block.shape[1])))

    lows_first = orders(size, (-1, -2, None))
    lows_last = orders(size, (None, -1, -2))
    plane = [o[:2] + (bits - 1,) + o[2:] for o in orders(size, (-1, -2, None))]
    line = orders(size, (None,))
    below, beyond = tuple(range(bits - 1)), tuple(range(2, bits - 1))

    fresh = functools.partial(Stream, size)
    up_width, qkv_width = up_l.shape[1] // 2, 3 * half_g
    square_units = units_g * (size // 8)
    rises, falls = (None, -1, -2), (-1, None, -2)
    order_l = [(bits - 1,) + orders(size, middle)[which] for which, middle in enumerate((falls, rises))]
    order_g = [(bits - 1,) + orders(size, middle)[which] for which, middle in enumerate((rises, falls))]
    gather_g = [(bits - 1,) + order for order in orders(size, rises)]
    table, table_g, places_g = (placement(order, every) for order in (order_l, gather_g, order_g))
    side_l = half_l + half_g
    stream_l = fresh(
        gather_all(
            jnp.concatenate(
                [half_of(out_l, core), half_of(patch_proj, core), gain_block(), own_heads(qkv_l), half_of(up_l, core)],
                axis=1,
            ),
            order_l,
            True,
        )
    )
    stream_down_l = fresh(gather_core(down_l, lows_last, below))
    stream_g = fresh(gather_all(own_heads(qkv_g), gather_g, False))
    stream_out_g = fresh(gather_all(half_of(out_g, core), gather_g, False))
    square = square_columns(half_of(up_g, core))
    one_two = jnp.where(is_first, square[2], square[1])
    two_one = jnp.where(is_first, square[1], square[2])
    blocks = jnp.stack([square[0], one_two, two_one, square[3]]).reshape(2, 2, rows_g, square_units)
    stream_up_g = fresh(gather_square(blocks, plane, every, [(0, rows_g, 0, square_units)]))
    stream_down_g = fresh(
        gather_core(down_g[:, :width_l], line, beyond)
    )

    bias_l = jnp.where(jnp.arange(seq_rows) < lengths[0], 0.0, NEG).astype(F32)[:, None]
    live = (jnp.arange(slot_total)[None, :] < patch_count[0][:, None]).reshape(slots)
    bias_g = jnp.where(live, 0.0, NEG).astype(F32)[:, None]
    positions = patch_index[0].reshape(slots)
    picks = positions[:, None] == jnp.arange(seq_rows)[None, :]
    picks_live = (picks & live[:, None]).astype(BF16)
    picks = picks.astype(BF16)

    advance([stream_l], ())
    seq_inputs = shared(bytes_in[0])
    inputs = seq_inputs.astype(F32)
    scale_l1 = row_scale(inputs)
    seq_grads = shared(out_grad[0])
    grad_top_b = mm(picks_live, seq_grads).astype(BF16)
    scale_l1 = advance([stream_l, stream_up_g, stream_down_l, stream_g], scale_l1)
    stream_top = fresh(gather_in_square(half_of(grad_top_b, core)))
    grad_top_b = advance([stream_l, stream_up_g, stream_down_l, stream_top], grad_top_b)
    advance([stream_l, stream_g, stream_top, stream_up_g], (), [stream_up_g])

    advance([stream_l, stream_g, stream_down_l, stream_up_g, stream_down_g, stream_top, stream_out_g], ())
    parts = stream_l.result()
    front = side_l + TILE
    out_wl, proj_w, gains = assembled_fours(
        parts,
        table,
        [(0, rows_l, 0, half_l), (0, rows_l, half_l, side_l), (0, rows_l, side_l, side_l + LANES)],
        front,
        LONG,
    )
    qkv_wl = Weight(parts, table, front, 3 * half_l)
    up_wl = Weight(parts, table, front + 3 * half_l, up_width)
    gain_one_l, gain_two_l = gains[:, 0].astype(F32), gains[:, 1].astype(F32)
    per = width_g // width_l
    gain_one_g, gain_two_g = (
        gains[:, low : low + per].reshape(width_g).astype(F32) for low in (2, 2 + per)
    )
    normed_l = (inputs * scale_l1 * gain_one_l).astype(BF16)
    projected_l = qkv_wl.product(normed_l)
    own_mixture_l, lse_l = attention_forward(projected_l, bias_l)
    mixture_l = own_mixture_l
    mixture_l, out_wl, proj_w = advance(
        [stream_down_l, stream_up_g, stream_down_g, stream_out_g], (mixture_l, out_wl, proj_w), [stream_up_g]
    )
    mixture_l = advance([stream_g], mixture_l)
    mixture_l, out_wl = shared(mixture_l), shared(out_wl)
    out_own_l = half_of(out_wl, core, 0)
    hidden_l = inputs + mm(mixture_l, out_wl)
    scale_l2 = row_scale(hidden_l)
    normed_l2 = (hidden_l * scale_l2 * gain_two_l).astype(BF16)
    activated_l, slope_l = up_wl.product(normed_l2, gelu=True)
    activated_l, proj_w = advance(
        [stream_down_l, stream_down_g, stream_out_g, stream_up_g], (activated_l, proj_w)
    )
    proj_w = shared(proj_w)
    (down_wl,) = stream_down_l.result()
    partial_l = mm(activated_l, down_wl)
    local_out = half_of(hidden_l, core) + half_of(partial_l, core) + swap(half_of(partial_l, 1 - core))

    boundary = shared(mm(picks, local_out.astype(BF16)).astype(BF16))
    start_rows = mm(boundary, proj_w)
    scale_g1 = row_scale(start_rows)
    square_top = shared(stream_top.result().reshape(4 * slots, half_l))
    scale_g1, square_top = advance([stream_g, stream_out_g, stream_up_g], (scale_g1, square_top))
    qkv_wg = Weight(stream_g.result(), table_g, 0, qkv_width, half_g)
    normed_g = (start_rows * scale_g1 * gain_one_g).astype(BF16)
    projected_g = qkv_wg.product(normed_g)
    own_mixture_g, lse_g = attention_forward(projected_g, bias_g)
    mixture_g = own_mixture_g
    mixture_g = advance([stream_out_g], mixture_g)
    (out_wg,) = assembled_fours(stream_out_g.result(), table_g, [(0, rows_g, 0, half_g)])
    out_theirs_g = swap(out_wg)
    mixture_g = shared(mixture_g)
    hidden_g = start_rows + joined(mm(mixture_g, out_wg), mm(mixture_g, out_theirs_g))
    scale_g2 = row_scale(hidden_g)
    normed_g2 = (hidden_g * scale_g2 * gain_two_g).astype(BF16)
    near = half_of(normed_g2, core)[None]
    near = jnp.concatenate([near, exchange(near, SQUARE[0], size)], axis=0)
    far = exchange(near, SQUARE[1], size)
    mine = jnp.concatenate([near, far], axis=0)
    theirs = jnp.concatenate([swap(near), swap(far)], axis=0)
    mine, theirs = in_square(mine), in_square(theirs, 1)
    square_normed = joined(mine.reshape(4 * slots, half_g), theirs.reshape(4 * slots, half_g))
    (up_wg,) = stream_up_g.result()
    (down_wg,) = stream_down_g.result()
    upward_g = mm(square_normed, up_wg)
    activated_g = jax.nn.gelu(upward_g).astype(BF16)

    grad_down_g = mm_tn(activated_g, square_top).astype(BF16)
    stream_down_g = fresh(scatter_core(grad_down_g, line, beyond, size))
    grad_act_g = mm_nt(square_top, down_wg)
    grad_up_g_rows = jax.vjp(jax.nn.gelu, upward_g)[1](grad_act_g)[0].astype(BF16)
    grad_up_g = mm_tn(square_normed, grad_up_g_rows).astype(BF16)
    stream_up_g = fresh(scatter_square(grad_up_g, plane, every))
    part = mm_nt(grad_up_g_rows, up_wg)
    part = half_of(part, core) + swap(half_of(part, 1 - core).astype(BF16)).astype(F32)
    part = advance([stream_down_g, stream_up_g], part)
    part = fresh(scatter_in_square(part.reshape(4, slots, half_g))).result().astype(BF16)
    part = shared(part).astype(F32)
    pulled, grad_gain_g2 = norm_backward(part, hidden_g, scale_g2, gain_two_g)
    grad_hidden_g = jnp.pad(grad_top_b.astype(F32), ((0, 0), (0, width_g - width_l))) + pulled
    grad_hidden_gb = grad_hidden_g.astype(BF16)
    mine_gb, theirs_gb = half_of(grad_hidden_gb, core), half_of(grad_hidden_gb, 1 - core)
    grad_out_g = mm_tn(mixture_g, mine_gb).astype(BF16)
    stream_out_g = fresh(scatter_all(split_stack([grad_out_g], places_g, size), order_g))
    grad_mixture_g = (
        mm_nt(mine_gb, half_of(out_wg, core, 0)) + mm_nt(theirs_gb, half_of(out_theirs_g, core, 0))
    ).astype(BF16)
    partial_g = mm(activated_g, down_wg)
    partial_g = half_of(partial_g, core) + swap(half_of(partial_g, 1 - core).astype(BF16)).astype(F32)
    stream_out = fresh(scatter_in_square(partial_g.reshape(4, slots, half_l)))
    grad_mixture_g = advance([stream_out_g, stream_out], grad_mixture_g)
    grad_projected_g = attention_backward(projected_g, bias_g, lse_g, own_mixture_g, grad_mixture_g)
    part, halves = qkv_wg.pullback(normed_g, grad_projected_g, places_g)
    stream_g = fresh(scatter_all(halves, order_g))
    part = advance([stream_g, stream_out, stream_out_g, stream_down_g], part)
    part = summed_cores(part)
    part = advance([stream_up_g], part)
    pulled, grad_gain_g1 = norm_backward(part, start_rows, scale_g1, gain_one_g)
    grad_start = (grad_hidden_g + pulled).astype(BF16)
    grad_proj = mm_tn(boundary, half_of(grad_start, core)).astype(BF16)

    grad_rows = mm_nt(grad_start, proj_w).astype(BF16)
    grad_local = seq_grads.astype(F32) + mm_tn(picks, grad_rows)
    grad_local_b = grad_local.astype(BF16)
    part, grad_down_l, up_halves = up_wl.feed_forward_pullback(
        normed_l2, grad_local_b, down_wl, slope_l, activated_l, table, side_l
    )
    stream_down_l = fresh(scatter_core(grad_down_l, lows_first, below, size))
    part, up_halves = advance(
        [stream_g, stream_down_g, stream_up_g, stream_out_g], (part, up_halves), [stream_up_g, stream_out_g]
    )
    part = summed_cores(part)
    pulled, grad_gain_l2 = norm_backward(part, hidden_l, scale_l2, gain_two_l)
    grad_hidden_l = grad_local + pulled
    grad_hidden_lb = grad_hidden_l.astype(BF16)
    grad_out_l = mm_tn(mixture_l, half_of(grad_hidden_lb, core)).astype(BF16)
    stream_up_l = fresh(scatter_all(split_stack([grad_out_l, grad_proj], table, size, up_halves), order_l))
    grad_mixture_l = mm_nt(grad_hidden_lb, out_own_l).astype(BF16)
    grad_mixture_l = advance([stream_g, stream_down_l, stream_up_l, stream_up_g, stream_out_g], grad_mixture_l)
    grad_projected_l = attention_backward(projected_l, bias_l, lse_l, own_mixture_l, grad_mixture_l)
    grad_projected_l = advance([stream_out_g, stream_up_g], grad_projected_l)
    stream_qkv_l = fresh(scatter_all(qkv_wl.outer(normed_l, grad_projected_l, table), order_l))
    grad_projected_l = advance([stream_qkv_l], grad_projected_l)
    part = advance([stream_up_l, stream_up_g, stream_g, stream_down_l], qkv_wl.inner(grad_projected_l))
    part = summed_cores(part)
    pulled, grad_gain_l1 = norm_backward(part, inputs, scale_l1, gain_one_l)
    input_grad = half_of(grad_hidden_l + pulled, core).astype(BF16)[None]
    gains = jnp.concatenate(
        [
            grad.reshape(size, 1, grad.shape[0] // size)
            for grad in (grad_gain_l1, grad_gain_l2, grad_gain_g1, grad_gain_g2)
        ],
        axis=2,
    )
    returned = half_of(hidden_g[:, :width_l], core) + stream_out.result()
    hidden_out = (local_out + mm_tn(picks_live, returned.astype(BF16))).astype(BF16)[None]
    stream_gains = fresh(scatter_small(gains, size))
    input_grad = advance([stream_qkv_l, stream_up_l, stream_down_l, stream_gains], input_grad)
    advance([stream_qkv_l, stream_gains, stream_down_l, stream_out_g, stream_g], (), [stream_gains])
    advance([stream_up_l, stream_gains, stream_down_l], ())
    advance([stream_qkv_l, stream_gains], ())
    advance([stream_up_l, stream_qkv_l], ())

    def joined_columns(mine, theirs):
        return joined(mine, theirs).astype(F32)

    def joined_heads(mine, theirs):
        low, high = jnp.where(is_first, mine, theirs), jnp.where(is_first, theirs, mine)
        thirds = [jnp.split(part, 3, axis=1) for part in (low, high)]
        return jnp.concatenate([part for pair in zip(*thirds) for part in pair], axis=1).astype(F32)

    def from_owner(mine, theirs):
        return jnp.where((position >> (bits - 1)) == core, mine, theirs).astype(F32)

    def in_order(blocks):
        low = own_bit((0, 0)), own_bit((1, 1))
        rows, width = blocks.shape[2:]
        placed = []
        for y in range(2):
            for x in range(2):
                dx, dy = x ^ low[0], y ^ low[1]
                index = jnp.where(is_first, 2 * dx + dy, 2 * dy + dx)
                placed.append(lax.dynamic_index_in_dim(blocks.reshape(4, rows, width), index, 0, keepdims=False))
        pieces = [jnp.split(part, size // 8, axis=1) for part in placed]
        return jnp.concatenate([piece for group in zip(*pieces) for piece in group], axis=1)

    down_g_mine = stream_down_g.result()
    total_down_g = from_owner(down_g_mine, swap(down_g_mine))
    total_down_g = jnp.pad(total_down_g, ((0, 0), (0, width_g - width_l)))
    up_g_mine = in_order(stream_up_g.result())
    total_up_g = joined_columns(up_g_mine, swap(up_g_mine))
    g_mine = stream_g.result()
    total_qkv_g = joined_heads(g_mine, swap(g_mine))
    out_g_mine = stream_out_g.result()
    total_out_g = joined_columns(out_g_mine, swap(out_g_mine))
    down_l_mine = stream_down_l.result()
    total_down_l = from_owner(down_l_mine, swap(down_l_mine))
    l_mine = stream_up_l.result()
    l_theirs = swap(l_mine)
    cuts = [0, half_l, side_l, side_l + up_width]
    total_out_l, total_proj, total_up_l = (
        joined_columns(l_mine[:, low:high], l_theirs[:, low:high]) for low, high in zip(cuts, cuts[1:])
    )
    q_mine = stream_qkv_l.result()
    total_qkv_l = joined_heads(q_mine, swap(q_mine))
    gains = stream_gains.result()
    gains = jnp.where(is_first, gains, lax.ppermute(gains, "section", [(0, 1)]))
    total_gain_l1 = gains[:rows_l]
    total_gain_l2 = gains[rows_l : 2 * rows_l]
    total_gain_g1 = gains[2 * rows_l : 2 * rows_l + rows_g]
    total_gain_g2 = gains[2 * rows_l + rows_g :]
    return (
        hidden_out,
        input_grad,
        total_gain_l1,
        total_qkv_l,
        total_out_l,
        total_gain_l2,
        total_up_l,
        total_down_l,
        total_proj,
        total_gain_g1,
        total_qkv_g,
        total_out_g,
        total_gain_g2,
        total_up_g,
        total_down_g,
    )


def solution(mesh):
    rows, vector = P("dp", None), P("dp")
    features = P("dp", None, "section")
    in_specs = (
        features,
        vector,
        P("dp", None, None),
        rows,
        vector,
        rows,
        rows,
        vector,
        rows,
        rows,
        rows,
        vector,
        rows,
        rows,
        vector,
        rows,
        rows,
        features,
    )
    out_specs = (
        features,
        features,
        vector,
        rows,
        rows,
        vector,
        rows,
        rows,
        rows,
        vector,
        rows,
        rows,
        vector,
        rows,
        rows,
    )
    return jax.shard_map(
        functools.partial(local, mesh.shape["dp"]),
        mesh=mesh,
        in_specs=in_specs,
        out_specs=out_specs,
        check_vma=False,
    )
```

```python
import functools

import jax
import jax.numpy as jnp
import numpy as np
from jax import lax
from jax.experimental import pallas as pl
from jax.experimental.pallas import tpu as pltpu
from jax.sharding import PartitionSpec as P

WINDOW = 1536
EPSILON = 1e-06
LANES = 128
GELU_SCALE = (2.0 / np.pi) ** 0.5
GELU_CUBE = 0.044715
NEG = -1e30
VMEM_LIMIT = 48 * 1024 * 1024
FREE = pl.CostEstimate(flops=0, bytes_accessed=0, transcendentals=0)
LONG = pl.CostEstimate(flops=10**11, bytes_accessed=0, transcendentals=0)
F32 = jnp.float32
BF16 = jnp.bfloat16


def mm(left, right):
    return jnp.dot(left, right, preferred_element_type=F32)


def mm_nt(left, right):
    return lax.dot_general(left, right, (((1,), (1,)), ((), ())), preferred_element_type=F32)


def mm_tn(left, right):
    return lax.dot_general(left, right, (((0,), (0,)), ((), ())), preferred_element_type=F32)


def row_scale(values):
    return lax.rsqrt(jnp.mean(values * values, axis=-1, keepdims=True) + EPSILON)


def norm_backward(grad_normed, values, scale, gain):
    grad_gain = jnp.sum(grad_normed * values * scale, axis=0)
    pulled = grad_normed * gain
    inner = jnp.mean(pulled * values, axis=-1, keepdims=True)
    return scale * pulled - values * (scale * scale * scale * inner), grad_gain


def query_block(rows):
    return 256 if rows % 256 == 0 else rows


def head_masks(block):
    lane = lax.broadcasted_iota(jnp.int32, (block, LANES), 1)
    return [lane < LANES // 2, lane >= LANES // 2]


def stacked(values, masks):
    return jnp.concatenate([jnp.where(mask, values, jnp.zeros_like(values)) for mask in masks], axis=0)


def first_lanes(values):
    lane = lax.broadcasted_iota(jnp.int32, (values[0].shape[0], LANES), 1)
    result = jnp.zeros(lane.shape, F32)
    for index, value in enumerate(values):
        result = jnp.where(lane == index, value, result)
    return result.astype(BF16)


def masked_scores(keys, biased, query, extended, bias, start, block, window):
    key_at = lax.broadcasted_iota(jnp.int32, (block, 2 * block), 0)
    query_at = lax.broadcasted_iota(jnp.int32, (block, 2 * block), 1)
    query_at = jnp.where(query_at < block, query_at, query_at - block)
    parts = []
    if start:
        before = mm_nt(biased[:start], extended)
        if window is not None:
            far = lax.broadcasted_iota(jnp.int32, (start, 2 * block), 0)
            own = lax.broadcasted_iota(jnp.int32, (start, 2 * block), 1)
            own = jnp.where(own < block, own, own - block) + start
            before = jnp.where(own - far < window, before, NEG)
        parts.append(before)
    diagonal = mm_nt(keys[start : start + block], query)
    masked = jnp.where(key_at < query_at, diagonal + bias[start : start + block], NEG)
    parts.append(jnp.where(key_at == query_at, diagonal, masked))
    return parts


def ranges(parts):
    low = 0
    for part in parts:
        yield low, low + part.shape[0], part
        low += part.shape[0]


def extend_keys(biased, k_ref, bias_ref):
    biased[:, :LANES] = k_ref[...]
    biased[:, LANES:] = first_lanes([bias_ref[...]])


def attention_forward_kernel(rows, window, q_ref, k_ref, v_ref, bias_ref, o_ref, lse_ref, biased, counted):
    block = query_block(rows)
    masks = head_masks(block)
    score_scale = (LANES // 2) ** (-0.5)
    lane = lax.broadcasted_iota(jnp.int32, (block, LANES), 1)
    extend_keys(biased, k_ref, bias_ref)
    for head, mask in enumerate(head_masks(rows)):
        counted[head] = jnp.where(mask, v_ref[...], jnp.ones_like(v_ref))
    one = first_lanes([jnp.ones((2 * block, 1), F32)])
    query_at = lax.broadcasted_iota(jnp.int32, (2 * block, block), 0)
    query_at = jnp.where(query_at < block, query_at, query_at - block)
    key_at = lax.broadcasted_iota(jnp.int32, (2 * block, block), 1)
    for index in range(rows // block):
        start = index * block
        query = stacked((q_ref[start : start + block, :] * score_scale).astype(BF16), masks)
        extended = jnp.concatenate([query, one], axis=1)
        parts = []
        if start:
            before = mm_nt(extended, biased[:start, :])
            if window is not None:
                far = lax.broadcasted_iota(jnp.int32, (2 * block, start), 1)
                own = lax.broadcasted_iota(jnp.int32, (2 * block, start), 0)
                own = jnp.where(own < block, own, own - block) + start
                before = jnp.where(own - far < window, before, NEG)
            parts.append(before)
        masked = jnp.where(key_at < query_at, mm_nt(extended, biased[start : start + block, :]), NEG)
        parts.append(jnp.where(key_at == query_at, mm_nt(query, k_ref[start : start + block, :]), masked))
        top = functools.reduce(jnp.maximum, [jnp.max(p, axis=1, keepdims=True) for p in parts])
        parts = [jnp.exp(p - top).astype(BF16) for p in parts]
        out, logs = jnp.zeros((block, LANES), F32), jnp.zeros((block, LANES), F32)
        for head, mask in enumerate(masks):
            span = slice(head * block, (head + 1) * block)
            mixed, low = jnp.zeros((block, LANES), F32), 0
            for part in parts:
                high = low + part.shape[1]
                mixed += mm(part[span], counted[head, low:high, :])
                low = high
            other = LANES // 2 if head == 0 else 0
            total = mixed[:, other : other + 1]
            out = jnp.where(mask, mixed * (1.0 / total), out)
            logs = jnp.where(lane == head, top[span] + jnp.log(total), logs)
        o_ref[start : start + block, :] = out.astype(BF16)
        lse_ref[0, :, start : start + block] = logs.T[:2]


def attention_backward_kernel(
    rows,
    window,
    q_ref,
    k_ref,
    v_ref,
    bias_ref,
    lse_ref,
    o_ref,
    do_ref,
    dq_ref,
    dk_ref,
    dv_ref,
    dk_acc,
    dv_acc,
    biased,
    reduced,
):
    block = query_block(rows)
    masks = head_masks(block)
    score_scale = (LANES // 2) ** (-0.5)
    extend_keys(biased, k_ref, bias_ref)
    reduced[:, :LANES] = v_ref[...]
    reduced[:, LANES:] = first_lanes([jnp.full((rows, 1), -1.0, F32)] * 2)
    one = first_lanes([jnp.ones((2 * block, 1), F32)])
    for index in reversed(range(rows // block)):
        start = index * block
        query = stacked((q_ref[start : start + block, :] * score_scale).astype(BF16), masks)
        extended = jnp.concatenate([query, one], axis=1)
        grad = stacked(do_ref[start : start + block, :], masks)
        mixed = o_ref[start : start + block, :].astype(F32)
        delta = jnp.sum(grad.astype(F32) * jnp.concatenate([mixed, mixed], axis=0), axis=1, keepdims=True)
        near = delta.astype(BF16).astype(F32)
        grad_extended = jnp.concatenate([grad, first_lanes([near, delta - near])], axis=1)
        lse = jnp.concatenate([lse_ref[0, head : head + 1, start : start + block] for head in range(2)], axis=1)
        parts = masked_scores(k_ref, biased, query, extended, bias_ref, start, block, window)
        turned = jnp.zeros((2 * block, LANES), F32)
        for low, high, part in ranges(parts):
            weights = jnp.exp(part - lse)
            change = (weights * mm_nt(reduced[low:high, :], grad_extended)).astype(BF16)
            dv = mm(weights.astype(BF16), grad)
            dk = mm(change, query)
            if index == rows // block - 1:
                dv_acc[low:high, :] = dv
                dk_acc[low:high, :] = dk
            else:
                dv_acc[low:high, :] += dv
                dk_acc[low:high, :] += dk
            turned += mm_tn(change, k_ref[low:high, :])
        dq = jnp.where(masks[0], turned[:block], turned[block:]) * score_scale
        dq_ref[start : start + block, :] = dq.astype(BF16)
    dk_ref[...] = dk_acc[...].astype(BF16)
    dv_ref[...] = dv_acc[...].astype(BF16)


def attention_specs(rows, width):
    pairs = width // LANES
    wide = lambda part: pl.BlockSpec((rows, LANES), lambda i, part=part: (0, part * pairs + i))
    bias = pl.BlockSpec((rows, 1), lambda i: (0, 0))
    return pairs, wide, bias


def attention_forward(projected, bias):
    rows, width = projected.shape[0], projected.shape[1] // 3
    pairs, wide, bias_spec = attention_specs(rows, width)
    window = WINDOW if rows > WINDOW else None
    return pl.pallas_call(
        functools.partial(attention_forward_kernel, rows, window),
        grid=(pairs,),
        in_specs=[wide(0), wide(1), wide(2), bias_spec],
        out_specs=[wide(0), pl.BlockSpec((1, 2, rows), lambda i: (i, 0, 0))],
        out_shape=[
            jax.ShapeDtypeStruct((rows, width), BF16),
            jax.ShapeDtypeStruct((pairs, 2, rows), F32),
        ],
        scratch_shapes=[pltpu.VMEM((rows, 2 * LANES), BF16), pltpu.VMEM((2, rows, LANES), BF16)],
        compiler_params=pltpu.CompilerParams(vmem_limit_bytes=VMEM_LIMIT),
        cost_estimate=FREE,
    )(projected, projected, projected, bias)


def attention_backward(projected, bias, lse, mixture, grad_mixture):
    rows, width = grad_mixture.shape
    pairs, wide, bias_spec = attention_specs(rows, width)
    window = WINDOW if rows > WINDOW else None
    shape = jax.ShapeDtypeStruct((rows, width), BF16)
    return pl.pallas_call(
        functools.partial(attention_backward_kernel, rows, window),
        grid=(pairs,),
        in_specs=[
            wide(0),
            wide(1),
            wide(2),
            bias_spec,
            pl.BlockSpec((1, 2, rows), lambda i: (i, 0, 0)),
            wide(0),
            wide(0),
        ],
        out_specs=[wide(0), wide(0), wide(0)],
        out_shape=[shape, shape, shape],
        scratch_shapes=[
            pltpu.VMEM((rows, LANES), F32),
            pltpu.VMEM((rows, LANES), F32),
            pltpu.VMEM((rows, 2 * LANES), BF16),
            pltpu.VMEM((rows, 2 * LANES), BF16),
        ],
        compiler_params=pltpu.CompilerParams(vmem_limit_bytes=VMEM_LIMIT),
        cost_estimate=LONG,
    )(projected, projected, projected, bias, lse, mixture, grad_mixture)


def swap(array):
    return lax.ppermute(array, "section", [(0, 1), (1, 0)])


def exchange(array, bits, size, sends=None):
    if sends == "flips":
        return tuple(
            lax.ppermute(part, "dp", [(i, i ^ flip) for i in range(size)]) for part, flip in zip(array, bits)
        )
    pairs = [
        (core * size + i, core * size + (i ^ (1 << bit)))
        for core, bit in enumerate(bits)
        for i in range(size)
        if sends is None or sends(core, i)
    ]
    return jax.tree.map(lambda part: lax.ppermute(part, ("section", "dp"), pairs), array)


def bit_count(size):
    return size.bit_length() - 1


def orders(size, middle):
    bits = bit_count(size)
    others = tuple(reversed(range(2, bits - 1)))
    result = []
    for core in range(2):
        lowest = (0, 1) if core == 0 else (1, 0)
        order = ()
        for entry in middle:
            order += others if entry is None else (lowest[0] if entry == -1 else lowest[1],)
        result.append(order)
    return result


def mask_of(index, order, places):
    return sum(((index >> t) & 1) << places.index(bit) for t, bit in enumerate(order))


def placement(order_pair, places):
    position = lax.axis_index("dp")
    own = sum(((position >> bit) & 1) << p for p, bit in enumerate(places))
    count = 1 << len(places)
    masks = [jnp.asarray([mask_of(j, order, places) for j in range(count)], jnp.int32) for order in order_pair]
    return (own ^ jnp.where(lax.axis_index("section") == 0, masks[0], masks[1])).astype(jnp.int32)


def aligned(rows, cuts=()):
    return rows % 16 == 0 and all(c % LANES == 0 and r % 16 == 0 for r0, r1, c0, c1 in cuts for r, c in ((r0, c0), (r1, c1)))


def assembly_kernel(bounds, cuts, table, *refs):
    step = pl.program_id(0)
    parts, outs = refs[: len(bounds)], refs[len(bounds) :]

    def store(ref):
        for (r0, r1, c0, c1), out in zip(cuts, outs):
            out[...] = ref[0, r0:r1, c0:c1]

    for (low, high), ref in zip(bounds, parts):
        pl.when((step >= low) & (step < high))(functools.partial(store, ref))


def assembled(parts, table, cuts, offset=0, width=None):
    rows = parts[0].shape[1]
    width = width or parts[0].shape[2]
    ends = np.cumsum([part.shape[0] for part in parts])
    count = int(ends[-1])
    bounds = [(int(end) - part.shape[0], int(end)) for end, part in zip(ends, parts)]
    shapes = [(count * (r1 - r0), c1 - c0) for r0, r1, c0, c1 in cuts]
    if not aligned(rows, cuts):
        stack = jnp.concatenate(parts, axis=0)[jnp.argsort(table)][..., offset : offset + width]
        return [stack[:, r0:r1, c0:c1].reshape(s) for (r0, r1, c0, c1), s in zip(cuts, shapes)]
    return pl.pallas_call(
        functools.partial(assembly_kernel, bounds, cuts),
        grid_spec=pltpu.PrefetchScalarGridSpec(
            num_scalar_prefetch=1,
            grid=(count,),
            in_specs=[
                pl.BlockSpec(
                    (1, rows, width),
                    lambda j, t, low=low, high=high: (jnp.clip(j, low, high - 1) - low, 0, offset // width),
                )
                for low, high in bounds
            ],
            out_specs=[pl.BlockSpec((r1 - r0, c1 - c0), lambda j, t: (t[j], 0)) for r0, r1, c0, c1 in cuts],
        ),
        out_shape=[jax.ShapeDtypeStruct(s, parts[0].dtype) for s in shapes],
        compiler_params=pltpu.CompilerParams(vmem_limit_bytes=VMEM_LIMIT),
        cost_estimate=FREE,
    )(table, *parts)


def quarters(parts):
    if len(parts) == 4:
        return [(part, 0) for part in parts]
    return [(part, k) for part in parts for k in range(2)]


def whole_kernel(cuts, table, *refs):
    quarter = refs[0].shape[0]
    for index in range(4 * quarter):
        part, place = refs[index // quarter], table[index]
        for (r0, r1, c0, c1), out in zip(cuts, refs[4:]):
            rows = r1 - r0
            out[pl.ds(pl.multiple_of(place * rows, 16), rows), :] = part[index % quarter, r0:r1, c0:c1]


def assembled_fours(parts, table, cuts, width=None, cost=FREE):
    rows = parts[0].shape[1]
    width = width or parts[0].shape[2]
    count = sum(part.shape[0] for part in parts)
    shapes = [(count * (r1 - r0), c1 - c0) for r0, r1, c0, c1 in cuts]
    if not aligned(rows, cuts):
        stack = jnp.concatenate(parts, axis=0)[jnp.argsort(table)]
        return [stack[:, r0:r1, c0:c1].reshape(s) for (r0, r1, c0, c1), s in zip(cuts, shapes)]
    return pl.pallas_call(
        functools.partial(whole_kernel, cuts),
        grid_spec=pltpu.PrefetchScalarGridSpec(
            num_scalar_prefetch=1,
            grid=(1,),
            in_specs=[pl.BlockSpec((count // 4, rows, width), lambda j, t, k=k: (k, 0, 0)) for _, k in quarters(parts)],
            out_specs=[pl.BlockSpec(shape, lambda j, t: (0, 0)) for shape in shapes],
        ),
        out_shape=[jax.ShapeDtypeStruct(s, parts[0].dtype) for s in shapes],
        compiler_params=pltpu.CompilerParams(vmem_limit_bytes=VMEM_LIMIT),
        cost_estimate=cost,
    )(table, *[part for part, _ in quarters(parts)])


def split_kernel(half, count, table, *refs):
    send, keep = refs[-2:]
    rows = refs[0].shape[0] // (2 * half)
    for index in range(2 * half):
        place, base = table[index], 0
        for ref in refs[:count]:
            block = ref[pl.ds(pl.multiple_of(place * rows, 16), rows), :]
            (keep if index < half else send)[index % half, :, base : base + ref.shape[1]] = block
            base += ref.shape[1]


def split_stack(grads, table, count, into=None):
    half, rows = count // 2, grads[0].shape[0] // count
    width = sum(grad.shape[1] for grad in grads)
    if not (aligned(rows) and all(grad.shape[1] % LANES == 0 for grad in grads)):
        stack = jnp.concatenate([grad.reshape(count, rows, grad.shape[1]) for grad in grads], axis=2)[table]
        halves = [stack[half:], stack[:half]]
        if into is not None:
            halves = [jnp.concatenate([part, old[..., width:]], axis=2) for part, old in zip(halves, into)]
        return halves
    full = width if into is None else into[0].shape[2]
    shape = jax.ShapeDtypeStruct((half, rows, full), BF16)
    into = [] if into is None else list(into)
    half_spec = pl.BlockSpec((half, rows, width), lambda j, t: (0, 0, 0))
    return pl.pallas_call(
        functools.partial(split_kernel, half, len(grads)),
        grid_spec=pltpu.PrefetchScalarGridSpec(
            num_scalar_prefetch=1,
            grid=(1,),
            in_specs=[pl.BlockSpec(grad.shape, lambda j, t: (0, 0)) for grad in grads]
            + [pl.BlockSpec(memory_space=pl.ANY) for _ in into],
            out_specs=[half_spec, half_spec],
        ),
        out_shape=[shape, shape],
        input_output_aliases={1 + len(grads) + k: k for k in range(len(into))},
        compiler_params=pltpu.CompilerParams(vmem_limit_bytes=VMEM_LIMIT),
        cost_estimate=FREE,
    )(table, *grads, *into)


def write_rows(target, parts, table, rows):
    index = 0
    for part in parts:
        for k in range(part.shape[0]):
            target[pl.ds(pl.multiple_of(table[index] * rows, 16), rows), :] = part[k]
            index += 1


def product_kernel(rows, count, gelu, table, x_ref, *refs):
    parts, outs, weight = refs[:count], refs[count:-1], refs[-1]
    write_rows(weight, parts, table, rows)
    result = jnp.dot(x_ref[...], weight[...], preferred_element_type=F32)
    if not gelu:
        outs[0][...] = result.astype(outs[0].dtype)
        return
    square = result * result
    bend = jnp.tanh(GELU_SCALE * (result + GELU_CUBE * (result * square)))
    outs[0][...] = (0.5 * result * (1.0 + bend)).astype(outs[0].dtype)
    slope = 0.5 * (1.0 + bend)
    slope += (0.5 * GELU_SCALE) * result * (1.0 - bend * bend) * (1.0 + (3.0 * GELU_CUBE) * square)
    outs[1][...] = slope.astype(outs[1].dtype)


def outer_kernel(rows, bounds, places, x_ref, *refs):
    grads, (send, keep, weight, turned) = refs[: len(bounds)], refs[len(bounds) :]
    step = pl.program_id(0)

    @pl.when(step == 0)
    def _():
        turned[...] = x_ref[...].T

    grad = grads[-1][...]
    for (low, high), ref in list(zip(bounds, grads))[:-1]:
        grad = jnp.where((step >= low) & (step < high), ref[...], grad)
    weight[...] = mm(turned[...], grad).astype(BF16)
    half = keep.shape[0]
    for index in range(2 * half):
        block = weight[pl.ds(pl.multiple_of(places[index] * rows, 16), rows), :]
        (keep if index < half else send)[index % half] = block


def inner_kernel(rows, bounds, table, *refs):
    parts, grads, (dx_ref, weight, total) = refs[:4], refs[4 : 4 + len(bounds)], refs[4 + len(bounds) :]
    step = pl.program_id(0)

    @pl.when(step == 0)
    def _():
        total[...] = jnp.zeros_like(total)

    write_rows(weight, parts, table, rows)
    grad = grads[-1][...]
    for (low, high), ref in list(zip(bounds, grads))[:-1]:
        grad = jnp.where((step >= low) & (step < high), ref[...], grad)
    total[...] += mm_nt(grad, weight[...])

    @pl.when(step == pl.num_programs(0) - 1)
    def _():
        dx_ref[...] = total[...].astype(BF16)


def pullback_kernel(rows, count, bounds, table, places, x_ref, *refs):
    parts, grads = refs[:count], refs[count : count + len(bounds)]
    dx_ref, send, keep, weight, turned, total = refs[count + len(bounds) :]
    step = pl.program_id(0)

    @pl.when(step == 0)
    def _():
        turned[...] = x_ref[...].T
        total[...] = jnp.zeros_like(total)

    write_rows(weight, parts, table, rows)
    grad = grads[-1][...]
    for (low, high), ref in list(zip(bounds, grads))[:-1]:
        grad = jnp.where((step >= low) & (step < high), ref[...], grad)
    total[...] += lax.dot_general(grad, weight[...], (((1,), (1,)), ((), ())), preferred_element_type=F32)
    weight[...] = jnp.dot(turned[...], grad, preferred_element_type=F32).astype(BF16)
    half = keep.shape[0]
    for index in range(2 * half):
        block = weight[pl.ds(pl.multiple_of(places[index] * rows, 16), rows), :]
        (keep if index < half else send)[index % half] = block

    @pl.when(step == pl.num_programs(0) - 1)
    def _():
        dx_ref[...] = total[...].astype(BF16)


def feed_forward_kernel(rows, table, places, x_ref, grad_ref, down_ref, slope_ref, act_ref, *refs):
    parts, (dx_ref, down_out, send, keep, weight, turned, total) = refs[:4], refs[4:]
    step = pl.program_id(0)

    @pl.when(step == 0)
    def _():
        turned[...] = x_ref[...].T
        total[...] = jnp.zeros_like(total)

    grad = grad_ref[...]
    change = (mm_nt(grad, down_ref[...]) * slope_ref[...].astype(F32)).astype(BF16)
    down_out[...] = mm_tn(act_ref[...], grad).astype(BF16)
    write_rows(weight, parts, table, rows)
    total[...] += mm_nt(change, weight[...])
    weight[...] = mm(turned[...], change).astype(BF16)
    half = keep.shape[0]
    for index in range(2 * half):
        block = weight[pl.ds(pl.multiple_of(places[index] * rows, 16), rows), :]
        (keep if index < half else send)[index % half] = block

    @pl.when(step == pl.num_programs(0) - 1)
    def _():
        dx_ref[...] = total[...].astype(BF16)


TILE = 384


class Weight:
    def __init__(self, parts, table, offset, width, tile=TILE):
        self.parts, self.table, self.offset, self.width, self.tile = parts, table, offset, width, tile
        self.rows = parts[0].shape[1]
        self.count = sum(part.shape[0] for part in parts)
        self.aligned = aligned(self.rows) and offset % tile == 0 and width % tile == 0

    def whole(self):
        cut = (0, self.rows, 0, self.width)
        stack = jnp.concatenate(self.parts, axis=0)[jnp.argsort(self.table)]
        return stack[..., self.offset : self.offset + self.width].reshape(-1, self.width)

    def part_specs(self):
        first = self.offset // self.tile
        return [
            pl.BlockSpec((self.count // 4, self.rows, self.tile), lambda i, *tables, k=k: (k, 0, first + i))
            for _, k in quarters(self.parts)
        ]

    def product(self, x, gelu=False):
        if not self.aligned:
            result = mm(x, self.whole())
            if not gelu:
                return result.astype(BF16)
            slope = jax.vjp(jax.nn.gelu, result)[1](jnp.ones_like(result))[0]
            return jax.nn.gelu(result).astype(BF16), slope.astype(BF16)
        tokens, depth = x.shape
        outs = 2 if gelu else 1
        shape = jax.ShapeDtypeStruct((tokens, self.width), BF16)
        results = pl.pallas_call(
            functools.partial(product_kernel, self.rows, 4, gelu),
            grid_spec=pltpu.PrefetchScalarGridSpec(
                num_scalar_prefetch=1,
                grid=(self.width // self.tile,),
                in_specs=[pl.BlockSpec((tokens, depth), lambda i, t: (0, 0))] + self.part_specs(),
                out_specs=[pl.BlockSpec((tokens, self.tile), lambda i, t: (0, i))] * outs,
                scratch_shapes=[pltpu.VMEM((depth, self.tile), BF16)],
            ),
            out_shape=[shape] * outs,
            compiler_params=pltpu.CompilerParams(vmem_limit_bytes=VMEM_LIMIT),
            cost_estimate=LONG if gelu else FREE,
        )(self.table, x, *[part for part, _ in quarters(self.parts)])
        return results if gelu else results[0]

    def feed_forward_pullback(self, x, grad, down, slope, activated, places, lead):
        if not self.aligned or down.shape[0] != self.width:
            change = (slope.astype(F32) * mm_nt(grad, down)).astype(BF16)
            dx, halves = self.pullback(x, [change], places, lead)
            return dx, mm_tn(activated, grad).astype(BF16), halves
        tokens, depth = x.shape
        half = jax.ShapeDtypeStruct((self.count // 2, self.rows, lead + self.width), BF16)
        half_spec = pl.BlockSpec((self.count // 2, self.rows, self.tile), lambda i, t, p: (0, 0, lead // self.tile + i))
        full = pl.BlockSpec((tokens, depth), lambda i, t, p: (0, 0))
        units = pl.BlockSpec((tokens, self.tile), lambda i, t, p: (0, i))
        unit_rows = pl.BlockSpec((self.tile, depth), lambda i, t, p: (i, 0))
        result = pl.pallas_call(
            functools.partial(feed_forward_kernel, self.rows),
            grid_spec=pltpu.PrefetchScalarGridSpec(
                num_scalar_prefetch=2,
                grid=(self.width // self.tile,),
                in_specs=[full, full, unit_rows, units, units] + self.part_specs(),
                out_specs=[full, unit_rows, half_spec, half_spec],
                scratch_shapes=[
                    pltpu.VMEM((depth, self.tile), BF16),
                    pltpu.VMEM((depth, tokens), BF16),
                    pltpu.VMEM((tokens, depth), F32),
                ],
            ),
            out_shape=[jax.ShapeDtypeStruct((tokens, depth), BF16), jax.ShapeDtypeStruct(down.shape, BF16), half, half],
            compiler_params=pltpu.CompilerParams(vmem_limit_bytes=VMEM_LIMIT),
            cost_estimate=FREE,
        )(self.table, places, x, grad, down, slope, activated, *[part for part, _ in quarters(self.parts)])
        return result[0], result[1], result[2:]

    def grad_specs(self, tokens, grads):
        ends = np.cumsum([grad.shape[1] // self.tile for grad in grads])
        bounds = [(int(end) - grad.shape[1] // self.tile, int(end)) for end, grad in zip(ends, grads)]
        specs = [
            pl.BlockSpec((tokens, self.tile), lambda i, t, low=low, high=high: (0, jnp.clip(i, low, high - 1) - low))
            for low, high in bounds
        ]
        return bounds, specs

    def outer(self, x, grads, places):
        if not self.aligned:
            return split_stack([mm_tn(x, jnp.concatenate(grads, axis=1)).astype(BF16)], places, self.count)
        tokens, depth = x.shape
        bounds, specs = self.grad_specs(tokens, grads)
        half = jax.ShapeDtypeStruct((self.count // 2, self.rows, self.width), BF16)
        half_spec = pl.BlockSpec((self.count // 2, self.rows, self.tile), lambda i, t: (0, 0, i))
        return pl.pallas_call(
            functools.partial(outer_kernel, self.rows, bounds),
            grid_spec=pltpu.PrefetchScalarGridSpec(
                num_scalar_prefetch=1,
                grid=(self.width // self.tile,),
                in_specs=[pl.BlockSpec((tokens, depth), lambda i, t: (0, 0))] + specs,
                out_specs=[half_spec, half_spec],
                scratch_shapes=[pltpu.VMEM((depth, self.tile), BF16), pltpu.VMEM((depth, tokens), BF16)],
            ),
            out_shape=[half, half],
            compiler_params=pltpu.CompilerParams(vmem_limit_bytes=VMEM_LIMIT),
            cost_estimate=FREE,
        )(places, x, *grads)

    def inner(self, grads):
        if not self.aligned:
            return mm_nt(jnp.concatenate(grads, axis=1), self.whole()).astype(BF16)
        tokens, depth = grads[0].shape[0], self.rows * self.count
        bounds, specs = self.grad_specs(tokens, grads)
        return pl.pallas_call(
            functools.partial(inner_kernel, self.rows, bounds),
            grid_spec=pltpu.PrefetchScalarGridSpec(
                num_scalar_prefetch=1,
                grid=(self.width // self.tile,),
                in_specs=self.part_specs() + specs,
                out_specs=pl.BlockSpec((tokens, depth), lambda i, t: (0, 0)),
                scratch_shapes=[pltpu.VMEM((depth, self.tile), BF16), pltpu.VMEM((tokens, depth), F32)],
            ),
            out_shape=jax.ShapeDtypeStruct((tokens, depth), BF16),
            compiler_params=pltpu.CompilerParams(vmem_limit_bytes=VMEM_LIMIT),
            cost_estimate=FREE,
        )(self.table, *[part for part, _ in quarters(self.parts)], *grads)

    def pullback(self, x, grads, places, lead=0):
        if not self.aligned:
            grad = jnp.concatenate(grads, axis=1)
            halves = split_stack([mm_tn(x, grad).astype(BF16)], places, self.count)
            return mm_nt(grad, self.whole()).astype(BF16), [jnp.pad(h, ((0, 0), (0, 0), (lead, 0))) for h in halves]
        tokens, depth = x.shape
        ends = np.cumsum([grad.shape[1] // self.tile for grad in grads])
        bounds = [(int(end) - grad.shape[1] // self.tile, int(end)) for end, grad in zip(ends, grads)]
        half = jax.ShapeDtypeStruct((self.count // 2, self.rows, lead + self.width), BF16)
        half_spec = pl.BlockSpec((self.count // 2, self.rows, self.tile), lambda i, t, p: (0, 0, lead // self.tile + i))
        result = pl.pallas_call(
            functools.partial(pullback_kernel, self.rows, 4, bounds),
            grid_spec=pltpu.PrefetchScalarGridSpec(
                num_scalar_prefetch=2,
                grid=(self.width // self.tile,),
                in_specs=[pl.BlockSpec((tokens, depth), lambda i, t, p: (0, 0))]
                + self.part_specs()
                + [
                    pl.BlockSpec((tokens, self.tile), lambda i, t, p, low=low, high=high: (0, jnp.clip(i, low, high - 1) - low))
                    for low, high in bounds
                ],
                out_specs=[pl.BlockSpec((tokens, depth), lambda i, t, p: (0, 0)), half_spec, half_spec],
                scratch_shapes=[
                    pltpu.VMEM((depth, self.tile), BF16),
                    pltpu.VMEM((depth, tokens), BF16),
                    pltpu.VMEM((tokens, depth), F32),
                ],
            ),
            out_shape=[jax.ShapeDtypeStruct((tokens, depth), BF16), half, half],
            compiler_params=pltpu.CompilerParams(vmem_limit_bytes=VMEM_LIMIT),
            cost_estimate=FREE,
        )(self.table, places, x, *[part for part, _ in quarters(self.parts)], *grads)
        return result[0], result[1:]


class Stream:
    def __init__(self, size, steps):
        self.size, self.steps = size, steps
        self.arriving = None
        self.value = None
        self.done = False
        self.pending = None

    def begin(self, arrived=None):
        try:
            self.pending = self.steps.send(arrived)
        except StopIteration as stop:
            self.pending, self.value, self.done = None, stop.value, True

    def launch(self):
        outgoing, bits, sends = self.pending
        self.arriving, self.pending = exchange(outgoing, bits, self.size, sends), None

    def result(self):
        if self.arriving is None and self.pending is None and not self.done:
            self.begin()
        while not self.done:
            if self.arriving is None:
                self.launch()
            arrived, self.arriving = self.arriving, None
            self.begin(arrived)
        return self.value


def advance(streams, tied, hold=()):
    for stream in streams:
        if stream.arriving is None and stream.pending is None and not stream.done:
            stream.begin()
    moving = [stream for stream in streams if not stream.done]
    ending = [stream for stream in moving if stream.arriving is not None]
    fresh = [stream for stream in moving if stream.arriving is None]
    arrived, outgoing, tied = lax.optimization_barrier(
        ([s.arriving for s in ending], [s.pending[0] for s in fresh], tied)
    )
    for stream, array in zip(fresh, outgoing):
        stream.pending = (array,) + stream.pending[1:]
    for stream, array in zip(ending, arrived):
        stream.arriving = None
        stream.begin(array)
    for stream in moving:
        if not stream.done and stream not in hold:
            stream.launch()
    return tied


def top_sends(size):
    top = bit_count(size) - 1
    return lambda core, i: (i >> top) == core


def doubling(held, order_pair, first=0, twice=False):
    parts = (held,)
    steps = list(zip(*order_pair))[first:]
    for index, bits in enumerate(steps):
        if len(parts) > 1 and not (twice and index == len(steps) - 1):
            parts = (jnp.concatenate(parts, axis=0),)
        arrived = yield lax.optimization_barrier(parts), bits, None
        parts = parts + arrived
    return parts


def gather_all(packed, order_pair, twice):
    return (yield from doubling(packed[None], order_pair, 0, twice))


def gather_core(piece, order_pair, places):
    size = lax.axis_size("dp")
    top = bit_count(size) - 1
    arrived = yield piece, (top, top), top_sends(size)
    mine = (lax.axis_index("dp") >> top) == lax.axis_index("section")
    parts = yield from doubling(jnp.where(mine, piece, arrived)[None], order_pair)
    table, cuts = placement(order_pair, places), [(0, piece.shape[0], 0, piece.shape[1])]
    return assembled_fours(parts, table, cuts) if len(places) > 1 else assembled(parts, table, cuts)


def own_bit(pair):
    position = lax.axis_index("dp")
    return (position >> jnp.where(lax.axis_index("section") == 0, pair[0], pair[1])) & 1


def gather_square(blocks, order_pair, places, cuts):
    first, second = list(zip(*order_pair))[:2]
    a, b = own_bit(first), own_bit(second)
    kept = lax.dynamic_index_in_dim(blocks, a, 0, keepdims=False)
    arrived = yield lax.dynamic_index_in_dim(blocks, 1 - a, 0, keepdims=False), first, None
    held = jnp.stack([kept, arrived])
    kept = lax.dynamic_index_in_dim(held, b, 1, keepdims=False)
    arrived = yield lax.dynamic_index_in_dim(held, 1 - b, 1, keepdims=False), second, None
    parts = yield from doubling(jnp.concatenate([kept, arrived], axis=0), order_pair, 2)
    return assembled(parts, placement(order_pair, places), cuts)


def total_of(terms):
    return sum(term.astype(F32) for term in terms)


def halving(send, kept, order_pair, last=0):
    terms, outgoing = [kept], send
    for bits in reversed(list(zip(*order_pair))[last:]):
        if outgoing is None:
            half = terms[0].shape[0] // 2
            outgoing = total_of([term[half:] for term in terms]).astype(BF16)
            terms = [term[:half] for term in terms]
        arrived = yield outgoing, bits, None
        terms, outgoing = terms + [arrived], None
    return terms


def scatter_all(halves, order_pair):
    terms = yield from halving(*halves, order_pair)
    return total_of(terms)[0].astype(BF16)


def scatter_core(grad, order_pair, places, size):
    halves = split_stack([grad], placement(order_pair, places), 1 << len(places))
    terms = yield from halving(*halves, order_pair)
    top = bit_count(size) - 1
    sends = top_sends(size)
    arrived = yield total_of(terms)[0].astype(BF16), (top, top), lambda core, i: not sends(core, i)
    return (total_of(terms)[0] + arrived.astype(F32)).astype(BF16)


def scatter_square(grad, order_pair, places):
    halves = split_stack([grad], placement(order_pair, places), 1 << len(places))
    terms = yield from halving(*halves, order_pair, 2)
    held = total_of(terms).astype(BF16)
    first, second = list(zip(*order_pair))[:2]
    arrived = yield held[2:], second, None
    held = jnp.stack([held[:2], arrived])
    arrived = yield held[:, 1], first, None
    return jnp.stack([held[:, 0], arrived])


def scatter_small(vector, size):
    position = lax.axis_index("dp")
    held = vector.reshape(size // 4, 4, vector.shape[2])
    for count, low in ((4, 0), (size // 4, 2)):
        own = (position >> low) & (count - 1)

        def part(index):
            return lax.dynamic_index_in_dim(held, index, 1 if low == 0 else 0, keepdims=False)

        outgoing = tuple(part(own ^ other) for other in range(1, count))
        arrived = yield outgoing, tuple(other << low for other in range(1, count)), "flips"
        held = part(own) + sum(arrived)
    return held


def in_square(blocks, whose=0):
    is_first = lax.axis_index("section") == whose
    middle = jnp.where(is_first, blocks[1:3], jnp.stack([blocks[2], blocks[1]]))
    return jnp.concatenate([blocks[:1], middle, blocks[3:]], axis=0)


SQUARE = ((0, 1), (1, 0))


def gather_in_square(rows):
    held = rows[None]
    for bits in SQUARE:
        arrived = yield held, bits, None
        held = jnp.concatenate([held, arrived], axis=0)
    return in_square(held)


def scatter_in_square(blocks):
    held = in_square(blocks)
    for bits in reversed(SQUARE):
        half = held.shape[0] // 2
        arrived = yield held[half:].astype(BF16), bits, None
        held = held[:half] + arrived.astype(F32)
    return held[0]


def local(
    size,
    bytes_in,
    lengths,
    patch_index,
    patch_count,
    gain_l1,
    qkv_l,
    out_l,
    gain_l2,
    up_l,
    down_l,
    patch_proj,
    gain_g1,
    qkv_g,
    out_g,
    gain_g2,
    up_g,
    down_g,
    out_grad,
):
    core = lax.axis_index("section")
    position = lax.axis_index("dp")
    is_first = core == 0
    seq_rows, half_l = bytes_in.shape[1:]
    width_l, width_g = 2 * half_l, out_g.shape[1]
    half_g = width_g // 2
    rows_l, rows_g = out_l.shape[0], out_g.shape[0]
    units_l, units_g = down_l.shape[0], down_g.shape[0]
    micro_total, slot_total = patch_index.shape[1:]
    slots = micro_total * slot_total
    bits = bit_count(size)
    every = tuple(range(bits))

    def joined(mine, theirs, axis=1):
        low = jnp.where(is_first, mine, theirs)
        high = jnp.where(is_first, theirs, mine)
        return jnp.concatenate([low, high], axis=axis)

    def shared(mine, axis=1):
        return joined(mine, swap(mine), axis)

    def half_of(array, which, axis=1):
        length = array.shape[axis] // 2
        return lax.dynamic_slice_in_dim(array, which * length, length, axis)

    def slope_of(upward):
        return jax.vjp(jax.nn.gelu, upward)[1](jnp.ones_like(upward))[0]

    def summed_cores(part):
        part = part.astype(BF16)
        return part.astype(F32) + swap(part).astype(F32)

    def own_heads(weight):
        return jnp.concatenate([half_of(third, core) for third in jnp.split(weight, 3, axis=1)], axis=1)

    def square_columns(weight):
        pieces = jnp.split(weight, size // 2, axis=1)
        return [jnp.concatenate(pieces[k::4], axis=1) for k in range(4)]

    def gain_block():
        columns = [gain.reshape(rows_l, -1) for gain in (gain_l1, gain_l2, gain_g1, gain_g2)]
        block = jnp.concatenate(columns, axis=1)
        return jnp.pad(block, ((0, 0), (0, TILE - block.shape[1])))

    lows_first = orders(size, (-1, -2, None))
    lows_last = orders(size, (None, -1, -2))
    plane = [o[:2] + (bits - 1,) + o[2:] for o in orders(size, (-1, -2, None))]
    line = orders(size, (None,))
    below, beyond = tuple(range(bits - 1)), tuple(range(2, bits - 1))

    fresh = functools.partial(Stream, size)
    up_width, qkv_width = up_l.shape[1] // 2, 3 * half_g
    square_units = units_g * (size // 8)
    rises, falls = (None, -1, -2), (-1, None, -2)
    order_l = [(bits - 1,) + orders(size, middle)[which] for which, middle in enumerate((falls, rises))]
    order_g = [(bits - 1,) + orders(size, middle)[which] for which, middle in enumerate((rises, falls))]
    gather_g = [(bits - 1,) + order for order in orders(size, rises)]
    table, table_g, places_g = (placement(order, every) for order in (order_l, gather_g, order_g))
    side_l = half_l + half_g
    stream_l = fresh(
        gather_all(
            jnp.concatenate(
                [half_of(out_l, core), half_of(patch_proj, core), gain_block(), own_heads(qkv_l), half_of(up_l, core)],
                axis=1,
            ),
            order_l,
            True,
        )
    )
    stream_down_l = fresh(gather_core(down_l, lows_last, below))
    stream_g = fresh(gather_all(own_heads(qkv_g), gather_g, False))
    stream_out_g = fresh(gather_all(half_of(out_g, core), gather_g, False))
    square = square_columns(half_of(up_g, core))
    one_two = jnp.where(is_first, square[2], square[1])
    two_one = jnp.where(is_first, square[1], square[2])
    blocks = jnp.stack([square[0], one_two, two_one, square[3]]).reshape(2, 2, rows_g, square_units)
    stream_up_g = fresh(gather_square(blocks, plane, every, [(0, rows_g, 0, square_units)]))
    stream_down_g = fresh(
        gather_core(down_g[:, :width_l], line, beyond)
    )

    bias_l = jnp.where(jnp.arange(seq_rows) < lengths[0], 0.0, NEG).astype(F32)[:, None]
    live = (jnp.arange(slot_total)[None, :] < patch_count[0][:, None]).reshape(slots)
    bias_g = jnp.where(live, 0.0, NEG).astype(F32)[:, None]
    positions = patch_index[0].reshape(slots)
    picks = positions[:, None] == jnp.arange(seq_rows)[None, :]
    picks_live = (picks & live[:, None]).astype(BF16)
    picks = picks.astype(BF16)

    advance([stream_l], ())
    seq_inputs = shared(bytes_in[0])
    inputs = seq_inputs.astype(F32)
    scale_l1 = row_scale(inputs)
    seq_grads = shared(out_grad[0])
    grad_top_b = mm(picks_live, seq_grads).astype(BF16)
    scale_l1 = advance([stream_l, stream_up_g, stream_down_l, stream_g], scale_l1)
    stream_top = fresh(gather_in_square(half_of(grad_top_b, core)))
    grad_top_b = advance([stream_l, stream_up_g, stream_down_l, stream_top], grad_top_b)
    advance([stream_l, stream_g, stream_top, stream_up_g], (), [stream_up_g])

    advance([stream_l, stream_g, stream_down_l, stream_up_g, stream_down_g, stream_top, stream_out_g], ())
    parts = stream_l.result()
    front = side_l + TILE
    out_wl, proj_w, gains = assembled_fours(
        parts,
        table,
        [(0, rows_l, 0, half_l), (0, rows_l, half_l, side_l), (0, rows_l, side_l, side_l + LANES)],
        front,
        LONG,
    )
    qkv_wl = Weight(parts, table, front, 3 * half_l)
    up_wl = Weight(parts, table, front + 3 * half_l, up_width)
    gain_one_l, gain_two_l = gains[:, 0].astype(F32), gains[:, 1].astype(F32)
    per = width_g // width_l
    gain_one_g, gain_two_g = (
        gains[:, low : low + per].reshape(width_g).astype(F32) for low in (2, 2 + per)
    )
    normed_l = (inputs * scale_l1 * gain_one_l).astype(BF16)
    projected_l = qkv_wl.product(normed_l)
    own_mixture_l, lse_l = attention_forward(projected_l, bias_l)
    mixture_l = own_mixture_l
    mixture_l, out_wl, proj_w = advance(
        [stream_down_l, stream_up_g, stream_down_g, stream_out_g], (mixture_l, out_wl, proj_w), [stream_up_g]
    )
    mixture_l = advance([stream_g], mixture_l)
    mixture_l, out_wl = shared(mixture_l), shared(out_wl)
    out_own_l = half_of(out_wl, core, 0)
    hidden_l = inputs + mm(mixture_l, out_wl)
    scale_l2 = row_scale(hidden_l)
    normed_l2 = (hidden_l * scale_l2 * gain_two_l).astype(BF16)
    activated_l, slope_l = up_wl.product(normed_l2, gelu=True)
    activated_l, proj_w = advance(
        [stream_down_l, stream_down_g, stream_out_g, stream_up_g], (activated_l, proj_w)
    )
    proj_w = shared(proj_w)
    (down_wl,) = stream_down_l.result()
    partial_l = mm(activated_l, down_wl)
    local_out = half_of(hidden_l, core) + half_of(partial_l, core) + swap(half_of(partial_l, 1 - core))

    boundary = shared(mm(picks, local_out.astype(BF16)).astype(BF16))
    start_rows = mm(boundary, proj_w)
    scale_g1 = row_scale(start_rows)
    square_top = shared(stream_top.result().reshape(4 * slots, half_l))
    scale_g1, square_top = advance([stream_g, stream_out_g, stream_up_g], (scale_g1, square_top))
    qkv_wg = Weight(stream_g.result(), table_g, 0, qkv_width, half_g)
    normed_g = (start_rows * scale_g1 * gain_one_g).astype(BF16)
    projected_g = qkv_wg.product(normed_g)
    own_mixture_g, lse_g = attention_forward(projected_g, bias_g)
    mixture_g = own_mixture_g
    mixture_g = advance([stream_out_g], mixture_g)
    (out_wg,) = assembled_fours(stream_out_g.result(), table_g, [(0, rows_g, 0, half_g)])
    out_theirs_g = swap(out_wg)
    mixture_g = shared(mixture_g)
    hidden_g = start_rows + joined(mm(mixture_g, out_wg), mm(mixture_g, out_theirs_g))
    scale_g2 = row_scale(hidden_g)
    normed_g2 = (hidden_g * scale_g2 * gain_two_g).astype(BF16)
    near = half_of(normed_g2, core)[None]
    near = jnp.concatenate([near, exchange(near, SQUARE[0], size)], axis=0)
    far = exchange(near, SQUARE[1], size)
    mine = jnp.concatenate([near, far], axis=0)
    theirs = jnp.concatenate([swap(near), swap(far)], axis=0)
    mine, theirs = in_square(mine), in_square(theirs, 1)
    square_normed = joined(mine.reshape(4 * slots, half_g), theirs.reshape(4 * slots, half_g))
    (up_wg,) = stream_up_g.result()
    (down_wg,) = stream_down_g.result()
    upward_g = mm(square_normed, up_wg)
    activated_g = jax.nn.gelu(upward_g).astype(BF16)

    grad_down_g = mm_tn(activated_g, square_top).astype(BF16)
    stream_down_g = fresh(scatter_core(grad_down_g, line, beyond, size))
    grad_act_g = mm_nt(square_top, down_wg)
    grad_up_g_rows = jax.vjp(jax.nn.gelu, upward_g)[1](grad_act_g)[0].astype(BF16)
    grad_up_g = mm_tn(square_normed, grad_up_g_rows).astype(BF16)
    stream_up_g = fresh(scatter_square(grad_up_g, plane, every))
    part = mm_nt(grad_up_g_rows, up_wg)
    mine = in_square(half_of(part, core).reshape(4, slots, half_g))
    theirs = in_square(half_of(part, 1 - core).astype(BF16).reshape(4, slots, half_g), 1)
    mine, theirs = advance([stream_down_g, stream_up_g], (mine, theirs))
    outgoing = (mine[2:] + swap(theirs[2:]).astype(F32)).astype(BF16)
    kept = mine[:2] + swap(theirs[:2]).astype(F32)
    kept = kept + exchange(outgoing, SQUARE[1], size).astype(F32)
    part = (kept[0] + exchange(kept[1].astype(BF16), SQUARE[0], size).astype(F32)).astype(BF16)
    part = shared(part).astype(F32)
    pulled, grad_gain_g2 = norm_backward(part, hidden_g, scale_g2, gain_two_g)
    grad_hidden_g = jnp.pad(grad_top_b.astype(F32), ((0, 0), (0, width_g - width_l))) + pulled
    grad_hidden_gb = grad_hidden_g.astype(BF16)
    mine_gb, theirs_gb = half_of(grad_hidden_gb, core), half_of(grad_hidden_gb, 1 - core)
    grad_out_g = mm_tn(mixture_g, mine_gb).astype(BF16)
    stream_out_g = fresh(scatter_all(split_stack([grad_out_g], places_g, size), order_g))
    grad_mixture_g = (
        mm_nt(mine_gb, half_of(out_wg, core, 0)) + mm_nt(theirs_gb, half_of(out_theirs_g, core, 0))
    ).astype(BF16)
    partial_g = mm(activated_g, down_wg)
    partial_g = half_of(partial_g, core) + swap(half_of(partial_g, 1 - core).astype(BF16)).astype(F32)
    stream_out = fresh(scatter_in_square(partial_g.reshape(4, slots, half_l)))
    grad_mixture_g = advance([stream_out_g, stream_out], grad_mixture_g)
    grad_projected_g = attention_backward(projected_g, bias_g, lse_g, own_mixture_g, grad_mixture_g)
    part, halves = qkv_wg.pullback(normed_g, grad_projected_g, places_g)
    stream_g = fresh(scatter_all(halves, order_g))
    part = advance([stream_g, stream_out, stream_out_g, stream_down_g], part)
    part = summed_cores(part)
    part = advance([stream_up_g], part)
    pulled, grad_gain_g1 = norm_backward(part, start_rows, scale_g1, gain_one_g)
    grad_start = (grad_hidden_g + pulled).astype(BF16)
    grad_proj = mm_tn(boundary, half_of(grad_start, core)).astype(BF16)

    grad_rows = mm_nt(grad_start, proj_w).astype(BF16)
    grad_local = seq_grads.astype(F32) + mm_tn(picks, grad_rows)
    grad_local_b = grad_local.astype(BF16)
    part, grad_down_l, up_halves = up_wl.feed_forward_pullback(
        normed_l2, grad_local_b, down_wl, slope_l, activated_l, table, side_l
    )
    stream_down_l = fresh(scatter_core(grad_down_l, lows_first, below, size))
    part, up_halves = advance(
        [stream_g, stream_down_g, stream_up_g, stream_out_g], (part, up_halves), [stream_up_g, stream_out_g]
    )
    part = summed_cores(part)
    pulled, grad_gain_l2 = norm_backward(part, hidden_l, scale_l2, gain_two_l)
    grad_hidden_l = grad_local + pulled
    grad_hidden_lb = grad_hidden_l.astype(BF16)
    grad_out_l = mm_tn(mixture_l, half_of(grad_hidden_lb, core)).astype(BF16)
    stream_up_l = fresh(scatter_all(split_stack([grad_out_l, grad_proj], table, size, up_halves), order_l))
    grad_mixture_l = mm_nt(grad_hidden_lb, out_own_l).astype(BF16)
    grad_mixture_l = advance([stream_g, stream_down_l, stream_up_l, stream_up_g, stream_out_g], grad_mixture_l)
    grad_projected_l = attention_backward(projected_l, bias_l, lse_l, own_mixture_l, grad_mixture_l)
    grad_projected_l = advance([stream_out_g, stream_up_g], grad_projected_l)
    stream_qkv_l = fresh(scatter_all(qkv_wl.outer(normed_l, grad_projected_l, table), order_l))
    grad_projected_l = advance([stream_qkv_l], grad_projected_l)
    part = advance([stream_up_l, stream_up_g, stream_g, stream_down_l], qkv_wl.inner(grad_projected_l))
    part = summed_cores(part)
    pulled, grad_gain_l1 = norm_backward(part, inputs, scale_l1, gain_one_l)
    input_grad = half_of(grad_hidden_l + pulled, core).astype(BF16)[None]
    gains = jnp.concatenate(
        [
            grad.reshape(size, 1, grad.shape[0] // size)
            for grad in (grad_gain_l1, grad_gain_l2, grad_gain_g1, grad_gain_g2)
        ],
        axis=2,
    )
    returned = half_of(hidden_g[:, :width_l], core) + stream_out.result()
    hidden_out = (local_out + mm_tn(picks_live, returned.astype(BF16))).astype(BF16)[None]
    stream_gains = fresh(scatter_small(gains, size))
    input_grad = advance([stream_qkv_l, stream_up_l, stream_down_l, stream_gains], input_grad)
    advance([stream_qkv_l, stream_gains, stream_down_l, stream_out_g, stream_g], (), [stream_gains])
    advance([stream_up_l, stream_gains, stream_down_l], ())
    advance([stream_qkv_l, stream_gains], ())
    advance([stream_up_l, stream_qkv_l], ())

    def joined_columns(mine, theirs):
        return joined(mine, theirs).astype(F32)

    def joined_heads(mine, theirs):
        low, high = jnp.where(is_first, mine, theirs), jnp.where(is_first, theirs, mine)
        thirds = [jnp.split(part, 3, axis=1) for part in (low, high)]
        return jnp.concatenate([part for pair in zip(*thirds) for part in pair], axis=1).astype(F32)

    def from_owner(mine, theirs):
        return jnp.where((position >> (bits - 1)) == core, mine, theirs).astype(F32)

    def in_order(blocks):
        low = own_bit((0, 0)), own_bit((1, 1))
        rows, width = blocks.shape[2:]
        placed = []
        for y in range(2):
            for x in range(2):
                dx, dy = x ^ low[0], y ^ low[1]
                index = jnp.where(is_first, 2 * dx + dy, 2 * dy + dx)
                placed.append(lax.dynamic_index_in_dim(blocks.reshape(4, rows, width), index, 0, keepdims=False))
        pieces = [jnp.split(part, size // 8, axis=1) for part in placed]
        return jnp.concatenate([piece for group in zip(*pieces) for piece in group], axis=1)

    down_g_mine = stream_down_g.result()
    total_down_g = from_owner(down_g_mine, swap(down_g_mine))
    total_down_g = jnp.pad(total_down_g, ((0, 0), (0, width_g - width_l)))
    up_g_mine = in_order(stream_up_g.result())
    total_up_g = joined_columns(up_g_mine, swap(up_g_mine))
    g_mine = stream_g.result()
    total_qkv_g = joined_heads(g_mine, swap(g_mine))
    out_g_mine = stream_out_g.result()
    total_out_g = joined_columns(out_g_mine, swap(out_g_mine))
    down_l_mine = stream_down_l.result()
    total_down_l = from_owner(down_l_mine, swap(down_l_mine))
    l_mine = stream_up_l.result()
    l_theirs = swap(l_mine)
    cuts = [0, half_l, side_l, side_l + up_width]
    total_out_l, total_proj, total_up_l = (
        joined_columns(l_mine[:, low:high], l_theirs[:, low:high]) for low, high in zip(cuts, cuts[1:])
    )
    q_mine = stream_qkv_l.result()
    total_qkv_l = joined_heads(q_mine, swap(q_mine))
    gains = stream_gains.result()
    gains = jnp.where(is_first, gains, lax.ppermute(gains, "section", [(0, 1)]))
    total_gain_l1 = gains[:rows_l]
    total_gain_l2 = gains[rows_l : 2 * rows_l]
    total_gain_g1 = gains[2 * rows_l : 2 * rows_l + rows_g]
    total_gain_g2 = gains[2 * rows_l + rows_g :]
    return (
        hidden_out,
        input_grad,
        total_gain_l1,
        total_qkv_l,
        total_out_l,
        total_gain_l2,
        total_up_l,
        total_down_l,
        total_proj,
        total_gain_g1,
        total_qkv_g,
        total_out_g,
        total_gain_g2,
        total_up_g,
        total_down_g,
    )


def solution(mesh):
    rows, vector = P("dp", None), P("dp")
    features = P("dp", None, "section")
    in_specs = (
        features,
        vector,
        P("dp", None, None),
        rows,
        vector,
        rows,
        rows,
        vector,
        rows,
        rows,
        rows,
        vector,
        rows,
        rows,
        vector,
        rows,
        rows,
        features,
    )
    out_specs = (
        features,
        features,
        vector,
        rows,
        rows,
        vector,
        rows,
        rows,
        rows,
        vector,
        rows,
        rows,
        vector,
        rows,
        rows,
    )
    return jax.shard_map(
        functools.partial(local, mesh.shape["dp"]),
        mesh=mesh,
        in_specs=in_specs,
        out_specs=out_specs,
        check_vma=False,
    )
```
